512 devices in a mesh: lat: 16 (over z_lo, x, core), lon: 32 (over y, z_hi).
Axes of the slice: x: 4, y: 8, z: 8 (z_hi: 4, z_lo: 2; z = z_hi * 2 + z_lo), core: 2. Of those that a mesh axis runs over, the one named last changes fastest.
Arguments:
- field: bfloat16 [64, 2048, 512], P('lat', 'lon'), may hold values from -6 to 6
- w_qkv: bfloat16 [512, 1152], replicated, may hold values from -2 to 2
- w_out: bfloat16 [512, 512], replicated, may hold values from -0.25 to 0.25
- conv_w: float32 [7, 7, 512], replicated, may hold values from -0.875 to 0.875
- w_in: bfloat16 [512, 1024], replicated, may hold values from -0.25 to 0.25
- w_back: bfloat16 [1024, 512], replicated, may hold values from -0.1875 to 0.1875
Outputs:
- result: bfloat16 [64, 2048, 512], P('lat', 'lon')
The draws below stay inside these ranges and needn't reach their ends.
All inputs are finite; a program needn't handle non-finite values.
Results may differ from the reference program's by a relative error of at most 0.012.
The reference program's roundings to bfloat16 on the way (of `normed`, `projected`, `heads`, `mixed`, `normed2` and `expanded`) count: a program that leaves them out, or rounds other values in their place, can miss the bound.
Values may be sent and summed in bfloat16 or wider, within the bound.
No kernel may reach another device: no remote copies, remote signals or barrier semaphores. Data moves between devices by JAX's collectives and lax.ppermute only.
A program may use at most 64 MiB of HBM per device.

```python
import math
import jax
import jax.numpy as jnp
from jax import lax

C = 512
HD = 64
ZHEADS = 4
MHEADS = 4
HID = 1024
ROWS = 64
COLS = 2048
QKV = 1152
AW = 512


def draw_w_qkv(key, part):
    key = jax.random.fold_in(key, 11)
    key_base = jax.random.fold_in(key, 0)
    width = (ZHEADS + 3 * MHEADS + 2) * HD
    base = jax.random.normal(key_base, (C, width), jnp.float32) / math.sqrt(C)
    column = jnp.arange(width)
    mq_end = (ZHEADS + MHEADS) * HD
    kz_end = mq_end + HD
    vz_end = kz_end + HD
    km_end = vz_end + MHEADS * HD
    aligned = (column < kz_end) | (column >= vz_end) & (column < km_end)
    factor = jnp.where(aligned, 2.5, 1.0)
    return jnp.clip(base * factor, -2.0, 2.0).astype(jnp.bfloat16)


def block_levels(stream_key, dims, cuts, least, high):
    loudness = 1.0
    for position, blocks in cuts:
        draws = jax.random.uniform(jax.random.fold_in(jax.random.fold_in(stream_key, 6), position), (blocks,), jnp.float32, least / len(cuts), high / len(cuts))
        loudness = loudness * jnp.repeat(jnp.exp(draws), dims[position] // blocks).reshape((-1,) + (1,) * (len(dims) - 1 - position))
    return loudness


def gaussian(stream_key, dims, deviation, most, cuts=(), dtype=jnp.bfloat16):
    drawn = deviation * jax.random.normal(stream_key, dims, jnp.float32)
    if cuts:
        drawn = drawn * block_levels(stream_key, dims, cuts, -0.22, 0.18)
    return jnp.clip(drawn, -most, most).astype(dtype)


def setup_inputs(seed: int = 0) -> dict:
    splits = jax.random.split(jax.random.key(seed), 7)
    return {
        "field": gaussian(splits[0], (ROWS, COLS, C), 1.0, 6.0, ((0, 16), (1, 32))),
        "w_qkv": draw_w_qkv(jax.random.fold_in(splits[6], 71), 0),
        "w_out": gaussian(splits[2], (AW, C), AW ** -0.5, 0.25),
        "conv_w": gaussian(splits[3], (7, 7, C), 49 ** -0.5, 0.875, (), jnp.float32),
        "w_in": gaussian(splits[4], (C, HID), C ** -0.5, 0.25),
        "w_back": gaussian(splits[5], (HID, C), HID ** -0.5, 0.1875),
    }


def layer_norm(values):
    center = values - lax.optimization_barrier(jnp.mean(values, axis=-1, keepdims=True))
    spread = lax.optimization_barrier(jnp.mean(center * center, axis=-1, keepdims=True))
    return center * lax.rsqrt(spread + 1e-06)

def rounded(values):
    return lax.optimization_barrier(values.astype(jnp.bfloat16))

def split_heads(projected):
    zq_end = ZHEADS * HD
    mq_end = zq_end + MHEADS * HD
    kz_end = mq_end + HD
    vz_end = kz_end + HD
    km_end = vz_end + MHEADS * HD
    lead = projected.shape[:2]
    zonal_q = projected[..., :zq_end].reshape(lead + (ZHEADS, HD))
    merid_q = projected[..., zq_end:mq_end].reshape(lead + (MHEADS, HD))
    zonal_k = projected[..., mq_end:kz_end]
    zonal_v = projected[..., kz_end:vz_end]
    merid_k = projected[..., vz_end:km_end].reshape(lead + (MHEADS, HD))
    merid_v = projected[..., km_end:].reshape(lead + (MHEADS, HD))
    return (zonal_q, merid_q, zonal_k, zonal_v, merid_k, merid_v)

def zonal_row(packed):
    queries, keys, values = packed
    block = math.gcd(COLS, 512)
    grouped = queries.reshape(COLS // block, block, ZHEADS, HD)
    keys_wide = keys.astype(jnp.float32)
    values_wide = values.astype(jnp.float32)

    def attend_block(query_block):
        scores = jnp.einsum('qhd,kd->hqk', query_block.astype(jnp.float32), keys_wide) * (1.0 / math.sqrt(HD))
        peak = lax.optimization_barrier(jnp.max(scores, axis=-1, keepdims=True))
        weights = jnp.exp(scores - peak)
        mass = lax.optimization_barrier(jnp.sum(weights, axis=-1))
        short = lax.optimization_barrier(weights.astype(jnp.bfloat16)).astype(jnp.float32)
        blended = jnp.einsum('hqk,kd->hqd', short, values_wide) / mass[..., None]
        return blended.transpose(1, 0, 2)
    return lax.map(attend_block, grouped).reshape(COLS, ZHEADS * HD)

def merid_block(packed):
    queries, keys, values = packed
    scores = jnp.einsum('crhd,cshd->chrs', queries.astype(jnp.float32), keys.astype(jnp.float32)) * (1.0 / math.sqrt(HD))
    peak = lax.optimization_barrier(jnp.max(scores, axis=-1, keepdims=True))
    weights = jnp.exp(scores - peak)
    mass = lax.optimization_barrier(jnp.sum(weights, axis=-1))
    short = lax.optimization_barrier(weights.astype(jnp.bfloat16)).astype(jnp.float32)
    blended = jnp.einsum('chrs,cshd->crhd', short, values.astype(jnp.float32))
    return blended / mass.transpose(0, 2, 1)[..., None]

def reference(field, w_qkv, w_out, conv_w, w_in, w_back):
    field_wide = field.astype(jnp.float32)
    normed = rounded(layer_norm(field_wide))
    projected = rounded(jnp.dot(normed.reshape(-1, C), w_qkv, preferred_element_type=jnp.float32)).reshape(ROWS, COLS, QKV)
    zonal_q, merid_q, zonal_k, zonal_v, merid_k, merid_v = split_heads(projected)
    zonal = lax.map(zonal_row, (zonal_q, zonal_k, zonal_v))
    block = math.gcd(COLS, 512)

    def by_columns(values):
        moved = jnp.swapaxes(values, 0, 1)
        return moved.reshape((COLS // block, block) + moved.shape[1:])
    meridional = lax.map(merid_block, (by_columns(merid_q), by_columns(merid_k), by_columns(merid_v)))
    meridional = jnp.swapaxes(meridional.reshape(COLS, ROWS, MHEADS * HD), 0, 1)
    heads = rounded(jnp.concatenate([zonal, meridional], axis=-1))
    mixed = rounded(field_wide + jnp.dot(heads.reshape(-1, AW), w_out, preferred_element_type=jnp.float32).reshape(ROWS, COLS, C))
    wrapped = jnp.concatenate([mixed[:, -3:], mixed, mixed[:, :3]], axis=1).astype(jnp.float32)
    padded = jnp.pad(wrapped, ((3, 3), (0, 0), (0, 0)))
    conv = jnp.zeros((ROWS, COLS, C), jnp.float32)
    for row_off in range(7):
        for col_off in range(7):
            conv = conv + padded[row_off:row_off + ROWS, col_off:col_off + COLS] * conv_w[row_off, col_off]
    normed2 = rounded(layer_norm(conv))
    expanded = rounded(jax.nn.gelu(jnp.dot(normed2.reshape(-1, C), w_in, preferred_element_type=jnp.float32), approximate=False))
    back = jnp.dot(expanded, w_back, preferred_element_type=jnp.float32).reshape(ROWS, COLS, C)
    return (mixed.astype(jnp.float32) + back).astype(jnp.bfloat16)
```

```python
import math

import jax
import jax.numpy as jnp
from jax import lax
from jax.experimental import pallas as pl
from jax.experimental.pallas import tpu as pltpu
from jax.sharding import PartitionSpec as P

C = 512
HD = 64
LAT = 16
LON = 32
R = 4
W = 64
CELLS = R * W
G = 8
WIDE = W + 16
SLOT = W + 2 * G
BACK = 3 * G
F32 = jnp.float32
BF = jnp.bfloat16
VMEM = 48 * 1024 * 1024


def iota(shape, dim):
    return lax.broadcasted_iota(jnp.int32, shape, dim)


def one_hot(hit):
    return jnp.where(hit, 1.0, 0.0).astype(BF)


def mm(a, b):
    return jnp.dot(a, b, preferred_element_type=F32)


def mm_nt(a, b):
    return lax.dot_general(a, b, (((1,), (1,)), ((), ())), preferred_element_type=F32)


def layer_norm(values):
    center = values - jnp.mean(values, axis=-1, keepdims=True)
    spread = jnp.mean(center * center, axis=-1, keepdims=True)
    return center * lax.rsqrt(spread + 1e-06)


def call(kernel, out_shape, flops, **kw):
    return pl.pallas_call(
        kernel,
        out_shape=out_shape,
        compiler_params=pltpu.CompilerParams(vmem_limit_bytes=VMEM),
        cost_estimate=pl.CostEstimate(flops=flops, bytes_accessed=2_000_000, transcendentals=0),
        **kw,
    )


def project_kernel(field_ref, w_ref, zonal_ref, merid_ref):
    normed = layer_norm(field_ref[...].astype(F32)).astype(BF)
    t, s = iota((CELLS, CELLS), 0), iota((CELLS, CELLS), 1)
    j, r, g = t // 32, (t // 8) % 4, t % 8
    normed_q = mm(one_hot(s == r * W + g * 8 + j), normed).astype(BF)
    m, r, cc = t // 16, (t // 4) % 4, t % 4
    normed_m = mm(one_hot(s == r * W + m * 4 + cc), normed).astype(BF)
    kv = mm(normed, w_ref[:, 512:640]).astype(BF)
    q = mm(normed_q, w_ref[:, 0:256])
    q = jnp.concatenate(
        [q[:, 0:128].reshape(LON, G, 128), q[:, 128:256].reshape(LON, G, 128)], axis=1
    ).astype(BF)
    for row in range(R):
        piece = kv[row * W : (row + 1) * W]
        for chunk in range(LON // R):
            zonal_ref[chunk * R + row, 0:W, :] = piece
    zonal_ref[:, W:SLOT, :] = q
    merid_ref[:, :, 0:256] = mm(normed_m, w_ref[:, 256:512]).astype(BF).reshape(LAT, 16, 256)
    merid_ref[:, :, 256:768] = mm(normed_m, w_ref[:, 640:1152]).astype(BF).reshape(LAT, 16, 512)


def merid_kernel(in_ref, out_ref):
    x = in_ref[...].reshape(CELLS, 768)
    t, s = iota((CELLS, CELLS), 0), iota((CELLS, CELLS), 1)
    bias = jnp.where(t % 4 == s % 4, 0.0, -1e30)
    low = iota((CELLS, 128), 1) < HD
    scale = 1.0 / math.sqrt(HD)
    for pair in range(2):
        q = x[:, pair * 128 : (pair + 1) * 128]
        k = x[:, 256 + pair * 128 : 384 + pair * 128]
        v = x[:, 512 + pair * 128 : 640 + pair * 128]
        outs = []
        for side in (low, jnp.logical_not(low)):
            score = mm_nt(jnp.where(side, q, jnp.zeros_like(q)), k) * scale + bias
            weight = jnp.exp(score - jnp.max(score, axis=-1, keepdims=True))
            mass = jnp.sum(weight, axis=-1, keepdims=True)
            outs.append(mm(weight.astype(BF), v) / mass)
        both = jnp.where(low, outs[0], outs[1]).astype(BF)
        out_ref[:, :, pair * 128 : (pair + 1) * 128] = both.reshape(LAT, 16, 128)


def zonal_kernel(chunk_ref, in_ref, out_ref):
    kv = in_ref[:, 0:W, :].reshape(LON * W, 128)
    ones = iota((LON * W, 128), 1) < HD
    kv_one = jnp.where(ones, jnp.ones_like(kv), kv)
    low = iota((LON * G, 128), 1) < HD
    q_all = in_ref[:, W:SLOT, :].astype(F32) * (1.0 / math.sqrt(HD))
    pairs = []
    for pair in range(2):
        q = q_all[:, pair * G : (pair + 1) * G, :].reshape(LON * G, 128)
        outs = []
        for head in range(2):
            placed = q if head == 0 else pltpu.roll(q, HD, 1)
            placed = jnp.where(low, placed, 0.0).astype(BF)
            score = mm_nt(placed, kv)
            weight = jnp.exp(score - jnp.max(score, axis=-1, keepdims=True)).astype(BF)
            both = mm(weight, kv_one)
            outs.append(both)
        even, odd = outs
        even = pltpu.roll(even, HD, 1)
        blended = jnp.where(low, even, odd)
        mass = jnp.where(low, pltpu.roll(even, HD, 1), pltpu.roll(odd, HD, 1))
        pairs.append(blended / mass)
    chunk = chunk_ref[0]
    t, u = iota((LON * G, LON * G), 0), iota((LON * G, LON * G), 1)
    s = t // G
    ahead, behind = ((s + 1) % LON) * G, ((s + LON - 1) % LON) * G + G - 1
    source = jnp.where(chunk < 4, ahead, behind)
    halo = mm(one_hot((t % G == 0) & (u == source)), pairs[0].astype(BF))
    halo = halo + mm(one_hot((t % G == 1) & (u == source)), pairs[1].astype(BF))
    parts = [a.reshape(LON, G, 128) for a in (pairs[0], pairs[1], halo)]
    out_ref[...] = jnp.concatenate(parts, axis=1).astype(BF)


def mix_kernel(zonal_ref, merid_ref, ml_ref, mr_ref, field_ref, fl_ref, fr_ref, w_ref, mixed_ref, up_ref, down_ref):
    rows = R * WIDE
    x = zonal_ref[...].astype(F32)
    x0 = x[:, 0:G].reshape(CELLS, 128).astype(BF)
    x1 = x[:, G : 2 * G].reshape(CELLS, 128).astype(BF)
    xh = x[:, 2 * G :].reshape(CELLS, 128).astype(BF)
    u, t = iota((rows, CELLS), 0), iota((rows, CELLS), 1)
    r, c = u // WIDE, u % WIDE - 8
    inside = (c >= 0) & (c < W)
    own = one_hot(inside & (t == ((c % 8) * 4 + r) * 8 + c // 8))
    left, right = (c >= -3) & (c < 0), (c >= W) & (c < W + 3)
    slot = jnp.where(left, c + 8, c - W) * 4 + r
    halo0 = one_hot((left | right) & (t == slot * 8))
    halo1 = one_hot((left | right) & (t == slot * 8 + 1))
    z0 = mm(own, x0) + mm(halo0, xh)
    z1 = mm(own, x1) + mm(halo1, xh)
    own_m = one_hot(inside & (t == (c // 4) * 16 + r * 4 + c % 4))
    merid = mm(own_m, merid_ref[...].reshape(CELLS, 256))
    u, t = iota((rows, 16), 0), iota((rows, 16), 1)
    r, c = u // WIDE, u % WIDE - 8
    from_left = one_hot((c >= -3) & (c < 0) & (t == r * 4 + c + 4))
    from_right = one_hot((c >= W) & (c < W + 3) & (t == r * 4 + c - W))
    merid = merid + mm(from_left, ml_ref[...]) + mm(from_right, mr_ref[...])
    attended = mm(z0.astype(BF), w_ref[0:128]) + mm(z1.astype(BF), w_ref[128:256])
    attended = attended + mm(merid.astype(BF), w_ref[256:512])
    wide = jnp.concatenate(
        [fl_ref[...].astype(F32), field_ref[...].astype(F32), fr_ref[...].astype(F32)], axis=1
    )
    mixed = (wide + attended.reshape(R, WIDE, C)).astype(BF)
    mixed_ref[...] = mixed
    up_ref[...] = mixed[0:3]
    down_ref[...] = mixed[1:4]


def block_kernel(mixed_ref, before_ref, after_ref, conv_ref, w_in_ref, w_back_ref, out_ref, conv_out):
    for lane in range(0, C, 128):
        rows = [before_ref[i, :, lane : lane + 128].astype(F32) for i in range(3)]
        rows += [mixed_ref[i, :, lane : lane + 128].astype(F32) for i in range(R)]
        rows += [after_ref[i, :, lane : lane + 128].astype(F32) for i in range(3)]
        for r in range(R):
            total = None
            for b in range(7):
                part = None
                for a in range(7):
                    term = rows[r + a] * conv_ref[a * 7 + b, lane : lane + 128][None, :]
                    part = term if part is None else part + term
                moved = part[b + 5 : b + 5 + W]
                total = moved if total is None else total + moved
            conv_out[r * W : (r + 1) * W, lane : lane + 128] = total
    normed = layer_norm(conv_out[...]).astype(BF)
    hidden = mm(normed, w_in_ref[...])
    hidden = 0.5 * hidden * (1.0 + lax.erf(hidden * math.sqrt(0.5)))
    back = mm(hidden.astype(BF), w_back_ref[...])
    own = mixed_ref[...].astype(F32)[:, 8 : 8 + W].reshape(CELLS, C)
    out_ref[...] = (own + back).astype(BF).reshape(R, W, C)


def shape(*dims):
    return jax.ShapeDtypeStruct(dims, BF)


def per_device(field, w_qkv, w_out, conv_w, w_in, w_back):
    right = [(i, (i + 1) % LON) for i in range(LON)]
    left = [(j, i) for i, j in right]
    down = [(i, i + 1) for i in range(LAT - 1)]
    up = [(j, i) for i, j in down]
    zonal_in, merid_in = call(
        project_kernel, (shape(LON, SLOT, 128), shape(LAT, 16, 768)), 400_000_000
    )(field.reshape(CELLS, C), w_qkv)
    merid_in = lax.all_to_all(merid_in, "lat", 0, 0)
    zonal_in = lax.all_to_all(zonal_in, "lon", 0, 0)
    merid = call(merid_kernel, shape(LAT, 16, 256), 800_000_000)(merid_in)
    merid = lax.all_to_all(merid, "lat", 0, 0)
    chunk = (lax.axis_index("lon") // R).astype(jnp.int32).reshape(1)
    zonal = call(
        zonal_kernel,
        shape(LON, BACK, 128),
        4_000_000_000,
        in_specs=[pl.BlockSpec(memory_space=pltpu.SMEM), pl.BlockSpec(memory_space=pltpu.VMEM)],
    )(chunk, zonal_in)
    zonal = lax.all_to_all(zonal, "lon", 0, 0)
    merid_left = lax.ppermute(merid[LAT - 1], "lon", right)
    merid_right = lax.ppermute(merid[0], "lon", left)
    field_left = lax.ppermute(field[:, W - 8 :], "lon", right)
    field_right = lax.ppermute(field[:, :8], "lon", left)
    mixed, first, last = call(
        mix_kernel, (shape(R, WIDE, C), shape(3, WIDE, C), shape(3, WIDE, C)), 800_000_000
    )(zonal, merid, merid_left, merid_right, field, field_left, field_right, w_out)
    before = lax.ppermute(last, "lat", down)
    after = lax.ppermute(first, "lat", up)
    return call(
        block_kernel,
        shape(R, W, C),
        2_000_000_000,
        scratch_shapes=[pltpu.VMEM((CELLS, C), F32)],
    )(mixed, before, after, conv_w.reshape(49, C), w_in, w_back)


def solution(mesh):
    return jax.shard_map(
        per_device,
        mesh=mesh,
        in_specs=(P("lat", "lon", None), P(), P(), P(), P(), P()),
        out_specs=P("lat", "lon", None),
        check_vma=False,
    )
```

```python
import math

import jax
import jax.numpy as jnp
from jax import lax
from jax.experimental import pallas as pl
from jax.experimental.pallas import tpu as pltpu
from jax.sharding import PartitionSpec as P

C = 512
HD = 64
LAT = 16
LON = 32
R = 4
W = 64
CELLS = R * W
E = 8
YS = 8
ZS = 4
SPAN = ZS * W
GROUPS = 8
WIDE = W + 2 * E
KEYS = SPAN + 4 * E
F32 = jnp.float32
BF = jnp.bfloat16


def iota(shape, dim):
    return lax.broadcasted_iota(jnp.int32, shape, dim)


def mm(a, b):
    return jnp.dot(a, b, preferred_element_type=F32)


def mm_nt(a, b):
    return lax.dot_general(a, b, (((1,), (1,)), ((), ())), preferred_element_type=F32)


def layer_norm(values):
    center = values - jnp.mean(values, axis=-1, keepdims=True)
    spread = jnp.mean(center * center, axis=-1, keepdims=True)
    return center * lax.rsqrt(spread + 1e-06)


def call(kernel, out_shape, flops, vmem=16, **kw):
    return pl.pallas_call(
        kernel,
        out_shape=out_shape,
        compiler_params=pltpu.CompilerParams(vmem_limit_bytes=vmem * 1024 * 1024),
        cost_estimate=pl.CostEstimate(flops=flops, bytes_accessed=2_000_000, transcendentals=0),
        **kw,
    )


def by_group(values):
    split = values.reshape(R, GROUPS, E, values.shape[-1])
    return jnp.swapaxes(split, 0, 1).reshape(GROUPS, R * E, values.shape[-1])


def project_kernel(field_ref, w_hbm, zonal_ref, query_ref, kv_ref, w_ref, sem):
    load = pltpu.make_async_copy(w_hbm, w_ref, sem)
    load.start()
    normed = layer_norm(field_ref[...].astype(F32)).astype(BF)
    load.wait()
    kv_ref[...] = by_group(mm(normed, w_ref[:, 640:1152])).astype(BF)
    query_ref[...] = by_group(mm(normed, w_ref[:, 256:512])).astype(BF)
    zonal_ref[:, :, 0:256] = mm(normed, w_ref[:, 0:256]).astype(BF).reshape(R, W, 256)
    zonal_ref[:, :, 256:384] = mm(normed, w_ref[:, 512:640]).astype(BF).reshape(R, W, 128)


def spread_kernel(in_ref, out_ref):
    kv = in_ref[:, :, 256:384].reshape(SPAN, 128)
    first = in_ref[0, :, 0:256].astype(F32)[0:E]
    last = in_ref[ZS - 1, :, 0:256].astype(F32)[W - E : W]
    edges = [first[:, 0:128], first[:, 128:256], last[:, 0:128], last[:, 128:256]]
    edges = jnp.concatenate(edges, axis=0).astype(BF)
    for y in range(YS):
        out_ref[y, 0:SPAN, :] = kv
        out_ref[y, SPAN:KEYS, :] = edges


def zonal_kernel(y_ref, own_ref, all_ref, out_ref):
    y = y_ref[0]
    kv = all_ref[:, 0:SPAN, :].reshape(YS * SPAN, 128)
    ones = iota((YS * SPAN, 128), 1) < HD
    kv_one = jnp.where(ones, jnp.ones_like(kv), kv)
    behind = all_ref[lax.rem(y + YS - 1, YS), SPAN + 2 * E : KEYS, :].astype(F32)
    ahead = all_ref[lax.rem(y + 1, YS), SPAN : SPAN + 2 * E, :].astype(F32)
    count = SPAN + 2 * E
    low = iota((count, 128), 1) < HD
    for pair in range(2):
        lanes = slice(pair * 128, pair * 128 + 128)
        rows = slice(pair * E, pair * E + E)
        q = own_ref[:, :, lanes].astype(F32).reshape(SPAN, 128)
        q = jnp.concatenate([behind[rows], q, ahead[rows]], axis=0) * (1.0 / math.sqrt(HD))
        outs = []
        for head in range(2):
            placed = q if head == 0 else pltpu.roll(q, HD, 1)
            placed = jnp.where(low, placed, 0.0).astype(BF)
            score = mm_nt(placed, kv)
            weight = jnp.exp(score - jnp.max(score, axis=-1, keepdims=True)).astype(BF)
            outs.append(mm(weight, kv_one))
        even, odd = outs
        blended = jnp.where(low, pltpu.roll(even, HD, 1), odd)
        mass = jnp.where(low, even, pltpu.roll(odd, HD, 1))
        heads = blended / mass
        for z in range(ZS):
            out_ref[z, :, lanes] = heads[z * W : z * W + WIDE].astype(BF)


def merid_kernel(query_ref, kv_ref, field_ref, out_ref, edge_ref):
    step = pl.program_id(0)
    rows, keys = R * E, LAT * R * E
    t, s = iota((2 * rows, keys), 0), iota((2 * rows, keys), 1)
    bias = jnp.where(t % E == s % E, 0.0, -1e30)
    low = iota((rows, 128), 1) < HD
    scale = 1.0 / math.sqrt(HD)
    for group in range(2):
        for pair in range(2):
            lanes = slice(pair * 128, pair * 128 + 128)
            q = query_ref[group, :, lanes].astype(F32) * scale
            q = jnp.concatenate([jnp.where(low, q, 0.0), jnp.where(low, 0.0, q)], axis=0).astype(BF)
            k = kv_ref[:, group, :, pair * 128 : pair * 128 + 128].reshape(keys, 128)
            v = kv_ref[:, group, :, 256 + pair * 128 : 384 + pair * 128].reshape(keys, 128)
            score = mm_nt(q, k) + bias
            weight = jnp.exp(score - jnp.max(score, axis=-1, keepdims=True))
            mass = jnp.sum(weight, axis=-1, keepdims=True)
            both = mm(weight.astype(BF), v) / mass
            out_ref[group, :, lanes] = jnp.where(low, both[0:rows], both[rows:]).astype(BF)

    @pl.when(step == 0)
    def first():
        edge_ref[0, :, 0:256] = out_ref[0]
        edge_ref[0, :, 256:768] = field_ref[...].astype(F32)[:, 0:E].reshape(rows, C).astype(BF)

    @pl.when(step == GROUPS // 2 - 1)
    def last():
        edge_ref[1, :, 0:256] = out_ref[1]
        edge_ref[1, :, 256:768] = field_ref[...].astype(F32)[:, W - E :].reshape(rows, C).astype(BF)


def widened(left, own, right):
    left, right = (a.astype(F32).reshape(R, E, a.shape[-1]) for a in (left, right))
    return jnp.concatenate([left, own, right], axis=1)


def mix_kernel(zonal_ref, merid_ref, el_ref, er_ref, field_ref, w_ref, mixed_ref, up_ref, down_ref):
    own = merid_ref[...].astype(F32).reshape(GROUPS, R, E, 256)
    own = jnp.swapaxes(own, 0, 1).reshape(R, W, 256)
    merid = widened(el_ref[:, 0:256], own, er_ref[:, 0:256]).astype(BF)
    wide = widened(el_ref[:, 256:768], field_ref[...].astype(F32), er_ref[:, 256:768])
    attended = mm(zonal_ref[...].reshape(R * WIDE, 256), w_ref[0:256])
    attended = attended + mm(merid.reshape(R * WIDE, 256), w_ref[256:512])
    mixed = (wide + attended.reshape(R, WIDE, C)).astype(BF)
    mixed_ref[...] = mixed
    up_ref[...] = mixed[0:3]
    down_ref[...] = mixed[1:4]


def block_kernel(mixed_ref, before_ref, after_ref, conv_ref, w_in_ref, w_back_ref, out_ref, conv_out):
    for lane in range(0, C, 128):
        rows = [before_ref[i, :, lane : lane + 128].astype(F32) for i in range(3)]
        rows += [mixed_ref[i, :, lane : lane + 128].astype(F32) for i in range(R)]
        rows += [after_ref[i, :, lane : lane + 128].astype(F32) for i in range(3)]
        for r in range(R):
            total = None
            for b in range(7):
                part = None
                for a in range(7):
                    term = rows[r + a] * conv_ref[a * 7 + b, lane : lane + 128][None, :]
                    part = term if part is None else part + term
                moved = part[b + 5 : b + 5 + W]
                total = moved if total is None else total + moved
            conv_out[r * W : (r + 1) * W, lane : lane + 128] = total
    normed = layer_norm(conv_out[...]).astype(BF)
    hidden = mm(normed, w_in_ref[...])
    hidden = 0.5 * hidden * (1.0 + lax.erf(hidden * math.sqrt(0.5)))
    back = mm(hidden.astype(BF), w_back_ref[...])
    own = mixed_ref[...].astype(F32)[:, 8 : 8 + W].reshape(CELLS, C)
    out_ref[...] = (own + back).astype(BF).reshape(R, W, C)


def shape(*dims):
    return jax.ShapeDtypeStruct(dims, BF)


def per_device(field, w_qkv, w_out, conv_w, w_in, w_back):
    right = [(i, (i + 1) % LON) for i in range(LON)]
    left = [(j, i) for i, j in right]
    down = [(i, i + 1) for i in range(LAT - 1)]
    up = [(j, i) for i, j in down]
    along_y = [[y * ZS + z for y in range(YS)] for z in range(ZS)]
    along_z = [[y * ZS + z for z in range(ZS)] for y in range(YS)]
    vmem = pl.BlockSpec(memory_space=pltpu.VMEM)
    zonal_in, query, kv = call(
        project_kernel,
        (shape(R, W, 384), shape(GROUPS, R * E, 256), shape(GROUPS, R * E, 512)),
        400_000_000,
        in_specs=[vmem, pl.BlockSpec(memory_space=pl.ANY)],
        scratch_shapes=[pltpu.VMEM((C, 1152), BF), pltpu.SemaphoreType.DMA],
    )(field.reshape(CELLS, C), w_qkv)
    kv_all = lax.all_gather(kv, "lat")
    row = lax.all_to_all(zonal_in, "lon", 0, 0, axis_index_groups=along_z)
    slots = call(spread_kernel, shape(YS, KEYS, 128), 10_000_000)(row)
    slots = lax.all_to_all(slots, "lon", 0, 0, axis_index_groups=along_y)
    y = (lax.axis_index("lon") // ZS).astype(jnp.int32).reshape(1)
    zonal_out = call(
        zonal_kernel,
        shape(ZS, WIDE, 256),
        4_000_000_000,
        vmem=24,
        in_specs=[pl.BlockSpec(memory_space=pltpu.SMEM), vmem, vmem],
    )(y, row, slots)
    zonal = lax.all_to_all(zonal_out, "lon", 0, 0, axis_index_groups=along_z)
    kv_all = lax.optimization_barrier((kv_all, zonal_out))[0]
    merid, edges = call(
        merid_kernel,
        (shape(GROUPS, R * E, 256), shape(2, R * E, 768)),
        1_000_000_000,
        grid=(GROUPS // 2,),
        in_specs=[
            pl.BlockSpec((2, R * E, 256), lambda i: (i, 0, 0)),
            pl.BlockSpec((LAT, 2, R * E, 512), lambda i: (0, i, 0, 0)),
            pl.BlockSpec((R, W, C), lambda i: (0, 0, 0)),
        ],
        out_specs=[
            pl.BlockSpec((2, R * E, 256), lambda i: (i, 0, 0)),
            pl.BlockSpec((2, R * E, 768), lambda i: (0, 0, 0)),
        ],
    )(query, kv_all, field)
    edge_left = lax.ppermute(edges[1], "lon", right)
    edge_right = lax.ppermute(edges[0], "lon", left)
    mixed, first, last = call(
        mix_kernel, (shape(R, WIDE, C), shape(3, WIDE, C), shape(3, WIDE, C)), 400_000_000
    )(zonal, merid, edge_left, edge_right, field, w_out)
    before = lax.ppermute(last, "lat", down)
    after = lax.ppermute(first, "lat", up)
    return call(
        block_kernel,
        shape(R, W, C),
        2_000_000_000,
        scratch_shapes=[pltpu.VMEM((CELLS, C), F32)],
    )(mixed, before, after, conv_w.reshape(49, C), w_in, w_back)


def solution(mesh):
    return jax.shard_map(
        per_device,
        mesh=mesh,
        in_specs=(P("lat", "lon", None), P(), P(), P(), P(), P()),
        out_specs=P("lat", "lon", None),
        check_vma=False,
    )
```

```python
import math

import jax
import jax.numpy as jnp
from jax import lax
from jax.experimental import pallas as pl
from jax.experimental.pallas import tpu as pltpu
from jax.sharding import PartitionSpec as P

C = 512
HD = 64
LAT = 16
LON = 32
R = 4
W = 64
CELLS = R * W
E = 8
WIDE = W + 2 * E
MC = WIDE // LAT
MROWS = 24
YS = 8
ZS = 4
SPAN = ZS * W
KEYS = SPAN + 2 * E
F32 = jnp.float32
BF = jnp.bfloat16


def iota(shape, dim):
    return lax.broadcasted_iota(jnp.int32, shape, dim)


def one_hot(hit):
    return jnp.where(hit, 1.0, 0.0).astype(BF)


def mm(a, b):
    return jnp.dot(a, b, preferred_element_type=F32)


def mm_nt(a, b):
    return lax.dot_general(a, b, (((1,), (1,)), ((), ())), preferred_element_type=F32)


def layer_norm(values):
    center = values - jnp.mean(values, axis=-1, keepdims=True)
    spread = jnp.mean(center * center, axis=-1, keepdims=True)
    return center * lax.rsqrt(spread + 1e-06)


def shape(*dims):
    return jax.ShapeDtypeStruct(dims, BF)


VMEM = pl.BlockSpec(memory_space=pltpu.VMEM)
ANY = pl.BlockSpec(memory_space=pl.ANY)
SMEM = pl.BlockSpec(memory_space=pltpu.SMEM)


def call(kernel, out_shape, flops, vmem=16, **kw):
    return pl.pallas_call(
        kernel,
        out_shape=out_shape,
        compiler_params=pltpu.CompilerParams(vmem_limit_bytes=vmem * 1024 * 1024),
        cost_estimate=pl.CostEstimate(flops=flops, bytes_accessed=2_000_000, transcendentals=0),
        **kw,
    )


def in_hbm(array):
    return pltpu.with_memory_space_constraint(array, pltpu.HBM)


def zonal_project_kernel(field_hbm, w_hbm, out_ref, first_ref, last_ref, field_ref, wq_ref, wkv_ref, sems):
    loads = [
        pltpu.make_async_copy(field_hbm, field_ref, sems.at[0]),
        pltpu.make_async_copy(w_hbm.at[:, 512:640], wkv_ref, sems.at[1]),
        pltpu.make_async_copy(w_hbm.at[:, 0:256], wq_ref, sems.at[2]),
    ]
    for load in loads:
        load.start()
    loads[0].wait()
    field = field_ref[...].astype(F32)
    first_ref[...] = field[:, 0:E].reshape(R * E, C).astype(BF)
    last_ref[...] = field[:, W - E : W].reshape(R * E, C).astype(BF)
    normed = layer_norm(field.reshape(CELLS, C)).astype(BF)
    loads[1].wait()
    out_ref[:, :, 256:384] = mm(normed, wkv_ref[...]).astype(BF).reshape(R, W, 128)
    loads[2].wait()
    out_ref[:, :, 0:256] = mm(normed, wq_ref[...]).astype(BF).reshape(R, W, 256)


def spread_kernel(in_ref, out_ref):
    kv = in_ref[:, :, 256:384].reshape(SPAN, 128)
    first = in_ref[0, :, 0:256].astype(F32)[0:E]
    last = in_ref[ZS - 1, :, 0:256].astype(F32)[W - E : W]
    edge = jnp.where(iota((E, 256), 0) < E // 2, first, last)
    edge = jnp.concatenate([edge[:, 0:128], edge[:, 128:256]], axis=0).astype(BF)
    for y in range(YS):
        out_ref[y, 0:SPAN, :] = kv
        out_ref[y, SPAN:KEYS, :] = edge


def zonal_kernel(y_ref, own_ref, all_ref, out_ref):
    y = y_ref[0]
    kv = all_ref[:, 0:SPAN, :].reshape(YS * SPAN, 128)
    ones = iota((YS * SPAN, 128), 1) < HD
    kv_one = jnp.where(ones, jnp.ones_like(kv), kv)
    behind = all_ref[lax.rem(y + YS - 1, YS), SPAN:KEYS, :].astype(F32)
    ahead = all_ref[lax.rem(y + 1, YS), SPAN:KEYS, :].astype(F32)
    count = SPAN + 2 * E
    low = iota((count, 128), 1) < HD
    for pair in range(2):
        lanes = slice(pair * 128, pair * 128 + 128)
        rows = slice(pair * E, pair * E + E)
        q = own_ref[:, :, lanes].astype(F32).reshape(SPAN, 128)
        q = jnp.concatenate([behind[rows], q, ahead[rows]], axis=0) * (1.0 / math.sqrt(HD))
        outs = []
        for head in range(2):
            placed = q if head == 0 else pltpu.roll(q, HD, 1)
            placed = jnp.where(low, placed, 0.0).astype(BF)
            score = mm_nt(placed, kv)
            weight = jnp.exp(score - jnp.max(score, axis=-1, keepdims=True)).astype(BF)
            outs.append(mm(weight, kv_one))
        even, odd = outs
        blended = jnp.where(low, pltpu.roll(even, HD, 1), odd)
        mass = jnp.where(low, even, pltpu.roll(odd, HD, 1))
        heads = blended / mass
        for z in range(ZS):
            out_ref[z, :, lanes] = heads[z * W : z * W + WIDE].astype(BF)


def widened(left, own, right):
    left, right = (a.astype(F32).reshape(R, E, a.shape[-1]) for a in (left, right))
    return jnp.concatenate([left, own.astype(F32), right], axis=1)


def merid_slots():
    dims = (LAT, MROWS, R * WIDE)
    m, i, u = iota(dims, 0), iota(dims, 1), iota(dims, 2)
    cell = (i & 3) * WIDE + m * MC + (i >> 2)
    return one_hot((cell == u) & (i < R * MC)).reshape(LAT * MROWS, R * WIDE)


def merid_select_kernel(field_ref, left_ref, right_ref, out_ref):
    wide = widened(left_ref[...], field_ref[...], right_ref[...]).reshape(R * WIDE, C)
    normed = mm(merid_slots(), layer_norm(wide).astype(BF))
    out_ref[...] = normed.reshape(LAT, MROWS, C).astype(BF)


def merid_kernel(in_ref, w_ref, out_ref):
    count = LAT * MROWS
    normed = in_ref[...].astype(F32).reshape(count, C).astype(BF)
    queries = mm(normed, w_ref[:, 256:512]).astype(BF)
    keys = mm(normed, w_ref[:, 640:896]).astype(BF)
    values = mm(normed, w_ref[:, 896:1152]).astype(BF)
    row = iota((LAT, MROWS, count), 1).reshape(count, count) >> 2
    key = iota((count, count), 1)
    key = (key - ((key * 2731) >> 16) * MROWS) >> 2
    bias = jnp.where(row == key, 0.0, -1e30)
    low = iota((count, 128), 1) < HD
    scale = 1.0 / math.sqrt(HD)
    for pair in range(2):
        lanes = slice(pair * 128, pair * 128 + 128)
        q, k, v = queries[:, lanes], keys[:, lanes], values[:, lanes]
        outs = []
        for side in (low, jnp.logical_not(low)):
            score = mm_nt(jnp.where(side, q, jnp.zeros_like(q)), k) * scale + bias
            weight = jnp.exp(score - jnp.max(score, axis=-1, keepdims=True))
            mass = jnp.sum(weight, axis=-1, keepdims=True)
            outs.append(mm(weight.astype(BF), v) / mass)
        both = jnp.where(low, outs[0], outs[1]).reshape(LAT, MROWS, 128)
        out_ref[:, :, lanes] = both.astype(BF)


def mix_kernel(zonal_ref, merid_ref, left_ref, right_ref, field_ref, w_ref, mixed_ref, up_ref, down_ref):
    rows = R * WIDE
    merid = merid_ref[...].astype(F32).reshape(LAT * MROWS, 256).astype(BF)
    dims = (R, WIDE, LAT * MROWS)
    r, w, t = iota(dims, 0), iota(dims, 1), iota(dims, 2)
    m = (t * 2731) >> 16
    i = t - m * MROWS
    cell = one_hot((m * MC + (i >> 2) == w) & ((i & 3) == r) & (i < R * MC))
    merid = mm(cell.reshape(rows, LAT * MROWS), merid).astype(BF)
    attended = mm(zonal_ref[...].reshape(rows, 256), w_ref[0:256]) + mm(merid, w_ref[256:512])
    wide = widened(left_ref[...], field_ref[...], right_ref[...])
    mixed = (wide + attended.reshape(R, WIDE, C)).astype(BF)
    mixed_ref[...] = mixed
    up_ref[...] = mixed[0:3]
    down_ref[...] = mixed[1:4]


def block_kernel(
    mixed_hbm, before_ref, after_ref, conv_ref, w_in_hbm, w_back_hbm, out_ref,
    mixed_ref, w_in_ref, w_back_ref, conv_out, sems,
):
    pairs = ((mixed_hbm, mixed_ref), (w_in_hbm, w_in_ref), (w_back_hbm, w_back_ref))
    loads = [pltpu.make_async_copy(a, b, sems.at[i]) for i, (a, b) in enumerate(pairs)]
    for load in loads:
        load.start()
    for part in range(2):
        if part == 1:
            loads[0].wait()
        for lane in range(0, C, 128):
            lanes = slice(lane, lane + 128)
            if part == 0:
                rows = {i: before_ref[i, :, lanes].astype(F32) for i in range(3)}
                rows.update({7 + i: after_ref[i, :, lanes].astype(F32) for i in range(3)})
            else:
                rows = {3 + i: mixed_ref[i, :, lanes].astype(F32) for i in range(R)}
            for r in range(R):
                total = None
                for b in range(7):
                    column = None
                    for a in range(7):
                        if r + a in rows:
                            term = rows[r + a] * conv_ref[a * 7 + b, lanes][None, :]
                            column = term if column is None else column + term
                    moved = column[b + 5 : b + 5 + W]
                    total = moved if total is None else total + moved
                here = (slice(r * W, (r + 1) * W), lanes)
                conv_out[here] = total if part == 0 else conv_out[here] + total
    normed = layer_norm(conv_out[...]).astype(BF)
    loads[1].wait()
    hidden = mm(normed, w_in_ref[...])
    hidden = 0.5 * hidden * (1.0 + lax.erf(hidden * math.sqrt(0.5)))
    loads[2].wait()
    back = mm(hidden.astype(BF), w_back_ref[...])
    own = mixed_ref[...].astype(F32)[:, E : E + W].reshape(CELLS, C)
    out_ref[...] = (own + back).astype(BF).reshape(R, W, C)


def per_device(field, w_qkv, w_out, conv_w, w_in, w_back):
    right = [(i, (i + 1) % LON) for i in range(LON)]
    left = [(j, i) for i, j in right]
    down = [(i, i + 1) for i in range(LAT - 1)]
    up = [(j, i) for i, j in down]
    along_y = [[y * ZS + z for y in range(YS)] for z in range(ZS)]
    along_z = [[y * ZS + z for z in range(ZS)] for y in range(YS)]
    row, first, last = call(
        zonal_project_kernel,
        (shape(R, W, 384), shape(R * E, C), shape(R * E, C)),
        200_000_000,
        in_specs=[ANY, ANY],
        scratch_shapes=[
            pltpu.VMEM((R, W, C), BF),
            pltpu.VMEM((C, 256), BF),
            pltpu.VMEM((C, 128), BF),
            pltpu.SemaphoreType.DMA((3,)),
        ],
    )(in_hbm(field), in_hbm(w_qkv))
    row = lax.all_to_all(row, "lon", 0, 0, axis_index_groups=along_z)
    slots = call(spread_kernel, shape(YS, KEYS, 128), 10_000_000)(row)
    slots = lax.all_to_all(slots, "lon", 0, 0, axis_index_groups=along_y)
    field_left = lax.ppermute(last, "lon", right)
    field_right = lax.ppermute(first, "lon", left)
    merid = call(merid_select_kernel, shape(LAT, MROWS, C), 300_000_000)(
        field, field_left, field_right
    )
    slots, merid = lax.optimization_barrier((slots, merid))
    merid = lax.all_to_all(merid, "lat", 0, 0)
    y = (lax.axis_index("lon") // ZS).astype(jnp.int32).reshape(1)
    zonal = call(
        zonal_kernel, shape(ZS, WIDE, 256), 4_000_000_000, vmem=24, in_specs=[SMEM, VMEM, VMEM]
    )(y, row, slots)
    zonal = lax.all_to_all(zonal, "lon", 0, 0, axis_index_groups=along_z)
    merid = call(merid_kernel, shape(LAT, MROWS, 256), 1_000_000_000)(merid, w_qkv)
    merid = lax.all_to_all(merid, "lat", 0, 0)
    mixed, first, last = call(
        mix_kernel, (shape(R, WIDE, C), shape(3, WIDE, C), shape(3, WIDE, C)), 800_000_000
    )(zonal, merid, field_left, field_right, field, w_out)
    before = lax.ppermute(last, "lat", down)
    after = lax.ppermute(first, "lat", up)
    return call(
        block_kernel,
        shape(R, W, C),
        2_000_000_000,
        in_specs=[ANY, VMEM, VMEM, VMEM, ANY, ANY],
        scratch_shapes=[
            pltpu.VMEM((R, WIDE, C), BF),
            pltpu.VMEM(w_in.shape, BF),
            pltpu.VMEM(w_back.shape, BF),
            pltpu.VMEM((CELLS, C), F32),
            pltpu.SemaphoreType.DMA((3,)),
        ],
    )(mixed, before, after, conv_w.reshape(49, C), in_hbm(w_in), in_hbm(w_back))


def solution(mesh):
    return jax.shard_map(
        per_device,
        mesh=mesh,
        in_specs=(P("lat", "lon", None), P(), P(), P(), P(), P()),
        out_specs=P("lat", "lon", None),
        check_vma=False,
    )
```

```python
import math

import jax
import jax.numpy as jnp
from jax import lax
from jax.experimental import pallas as pl
from jax.experimental.pallas import tpu as pltpu
from jax.sharding import PartitionSpec as P

C = 512
HD = 64
LAT = 16
LON = 32
R = 4
W = 64
CELLS = R * W
E = 8
WIDE = W + 2 * E
MCELLS = 16
YS = 8
ZS = 4
SPAN = ZS * W
KEYS = SPAN + 2 * E
F32 = jnp.float32
BF = jnp.bfloat16


def iota(shape, dim):
    return lax.broadcasted_iota(jnp.int32, shape, dim)


def one_hot(hit):
    return jnp.where(hit, 1.0, 0.0).astype(BF)


def mm(a, b):
    return jnp.dot(a, b, preferred_element_type=F32)


def mm_nt(a, b):
    return lax.dot_general(a, b, (((1,), (1,)), ((), ())), preferred_element_type=F32)


def layer_norm(values):
    center = values - jnp.mean(values, axis=-1, keepdims=True)
    spread = jnp.mean(center * center, axis=-1, keepdims=True)
    return center * lax.rsqrt(spread + 1e-06)


def shape(*dims):
    return jax.ShapeDtypeStruct(dims, BF)


VMEM = pl.BlockSpec(memory_space=pltpu.VMEM)
ANY = pl.BlockSpec(memory_space=pl.ANY)
SMEM = pl.BlockSpec(memory_space=pltpu.SMEM)


def call(kernel, out_shape, flops, vmem=16, **kw):
    return pl.pallas_call(
        kernel,
        out_shape=out_shape,
        compiler_params=pltpu.CompilerParams(vmem_limit_bytes=vmem * 1024 * 1024),
        cost_estimate=pl.CostEstimate(flops=flops, bytes_accessed=2_000_000, transcendentals=0),
        **kw,
    )


def in_hbm(array):
    return pltpu.with_memory_space_constraint(array, pltpu.HBM)


def project_kernel(
    field_hbm, w_hbm, row_ref, merid_ref, first_ref, last_ref, field_ref, wq_ref, wkv_ref, sems
):
    loads = [
        pltpu.make_async_copy(field_hbm, field_ref, sems.at[0]),
        pltpu.make_async_copy(w_hbm.at[:, 512:640], wkv_ref, sems.at[1]),
        pltpu.make_async_copy(w_hbm.at[:, 0:256], wq_ref, sems.at[2]),
    ]
    for load in loads:
        load.start()
    t, s = iota((CELLS, CELLS), 0), iota((CELLS, CELLS), 1)
    select = one_hot(s == ((t >> 2) & 3) * W + (t >> 4) * 4 + (t & 3))
    loads[0].wait()
    field = field_ref[...].astype(F32).reshape(CELLS, C)
    normed = layer_norm(field).astype(BF)
    merid_ref[...] = mm(select, normed).astype(BF).reshape(LAT, MCELLS, C)
    edges = mm(jnp.concatenate([select[0:MCELLS], select[CELLS - MCELLS :]], axis=0), field.astype(BF))
    first_ref[...] = edges[0:MCELLS].astype(BF)
    last_ref[...] = edges[MCELLS:].astype(BF)
    loads[1].wait()
    row_ref[:, :, 256:384] = mm(normed, wkv_ref[...]).astype(BF).reshape(R, W, 128)
    loads[2].wait()
    row_ref[:, :, 0:256] = mm(normed, wq_ref[...]).astype(BF).reshape(R, W, 256)


def spread_kernel(in_ref, out_ref):
    kv = in_ref[:, :, 256:384].reshape(SPAN, 128)
    first = in_ref[0, :, 0:256].astype(F32)[0:E]
    last = in_ref[ZS - 1, :, 0:256].astype(F32)[W - E : W]
    edge = jnp.where(iota((E, 256), 0) < E // 2, first, last)
    edge = jnp.concatenate([edge[:, 0:128], edge[:, 128:256]], axis=0).astype(BF)
    for y in range(YS):
        out_ref[y, 0:SPAN, :] = kv
        out_ref[y, SPAN:KEYS, :] = edge


def zonal_kernel(y_ref, own_ref, all_ref, out_ref):
    y = y_ref[0]
    kv = all_ref[:, 0:SPAN, :].reshape(YS * SPAN, 128)
    ones = iota((YS * SPAN, 128), 1) < HD
    kv_one = jnp.where(ones, jnp.ones_like(kv), kv)
    behind = all_ref[lax.rem(y + YS - 1, YS), SPAN:KEYS, :].astype(F32)
    ahead = all_ref[lax.rem(y + 1, YS), SPAN:KEYS, :].astype(F32)
    count = SPAN + 2 * E
    low = iota((count, 128), 1) < HD
    for pair in range(2):
        lanes = slice(pair * 128, pair * 128 + 128)
        rows = slice(pair * E, pair * E + E)
        q = own_ref[:, :, lanes].astype(F32).reshape(SPAN, 128)
        q = jnp.concatenate([behind[rows], q, ahead[rows]], axis=0) * (1.0 / math.sqrt(HD))
        outs = []
        for head in range(2):
            placed = q if head == 0 else pltpu.roll(q, HD, 1)
            placed = jnp.where(low, placed, 0.0).astype(BF)
            score = mm_nt(placed, kv)
            weight = jnp.exp(score - jnp.max(score, axis=-1, keepdims=True)).astype(BF)
            outs.append(mm(weight, kv_one))
        even, odd = outs
        blended = jnp.where(low, pltpu.roll(even, HD, 1), odd)
        mass = jnp.where(low, even, pltpu.roll(odd, HD, 1))
        heads = blended / mass
        for z in range(ZS):
            out_ref[z, :, lanes] = heads[z * W : z * W + WIDE].astype(BF)


def merid_kernel(in_ref, w_ref, out_ref):
    normed = in_ref[...].reshape(CELLS, C)
    queries = mm(normed, w_ref[:, 256:512]).astype(BF)
    keys = mm(normed, w_ref[:, 640:896]).astype(BF)
    values = mm(normed, w_ref[:, 896:1152]).astype(BF)
    t, s = iota((CELLS, CELLS), 0), iota((CELLS, CELLS), 1)
    bias = jnp.where((t & 3) == (s & 3), 0.0, -1e30)
    low = iota((CELLS, 128), 1) < HD
    scale = 1.0 / math.sqrt(HD)
    for pair in range(2):
        lanes = slice(pair * 128, pair * 128 + 128)
        q, k, v = queries[:, lanes], keys[:, lanes], values[:, lanes]
        outs = []
        for side in (low, jnp.logical_not(low)):
            score = mm_nt(jnp.where(side, q, jnp.zeros_like(q)), k) * scale + bias
            weight = jnp.exp(score - jnp.max(score, axis=-1, keepdims=True))
            mass = jnp.sum(weight, axis=-1, keepdims=True)
            outs.append(mm(weight.astype(BF), v) / mass)
        both = jnp.where(low, outs[0], outs[1]).reshape(LAT, MCELLS, 128)
        out_ref[:, :, lanes] = both.astype(BF)


def mix_kernel(zonal_ref, merid_ref, left_ref, right_ref, field_ref, w_ref, mixed_ref, up_ref, down_ref):
    rows = R * WIDE
    dims = (R, WIDE, CELLS)
    r, c, t = iota(dims, 0), iota(dims, 1) - E, iota(dims, 2)
    own = ((c >> 2) << 4) + (r << 2) + (c & 3)
    own = one_hot((c >= 0) & (c < W) & (t == own)).reshape(rows, CELLS)
    dims = (R, WIDE, MCELLS)
    r, c, t = iota(dims, 0), iota(dims, 1) - E, iota(dims, 2)
    edge = t == (r << 2) + (c & 3)
    left = one_hot(edge & (c >= -4) & (c < 0)).reshape(rows, MCELLS)
    right = one_hot(edge & (c >= W) & (c < W + 4)).reshape(rows, MCELLS)
    edges = mm(left, left_ref[...]) + mm(right, right_ref[...])
    merid = mm(own, merid_ref[...].reshape(CELLS, 256)) + edges[:, 0:256]
    attended = mm(zonal_ref[...].reshape(rows, 256), w_ref[0:256])
    attended = attended + mm(merid.astype(BF), w_ref[256:512])
    blank = jnp.zeros((R, E, C), F32)
    wide = jnp.concatenate([blank, field_ref[...].astype(F32), blank], axis=1)
    wide = wide + edges[:, 256:].reshape(R, WIDE, C)
    mixed = (wide + attended.reshape(R, WIDE, C)).astype(BF)
    mixed_ref[...] = mixed
    up_ref[...] = mixed[0:3]
    down_ref[...] = mixed[1:4]


def block_kernel(
    mixed_hbm, before_ref, after_ref, conv_ref, w_in_hbm, w_back_hbm, out_ref,
    mixed_ref, w_in_ref, w_back_ref, conv_out, sems,
):
    pairs = ((mixed_hbm, mixed_ref), (w_in_hbm, w_in_ref), (w_back_hbm, w_back_ref))
    loads = [pltpu.make_async_copy(a, b, sems.at[i]) for i, (a, b) in enumerate(pairs)]
    for load in loads:
        load.start()
    for part in range(2):
        if part == 1:
            loads[0].wait()
        for lane in range(0, C, 128):
            lanes = slice(lane, lane + 128)
            if part == 0:
                rows = {i: before_ref[i, :, lanes].astype(F32) for i in range(3)}
                rows.update({7 + i: after_ref[i, :, lanes].astype(F32) for i in range(3)})
            else:
                rows = {3 + i: mixed_ref[i, :, lanes].astype(F32) for i in range(R)}
            for r in range(R):
                total = None
                for b in range(7):
                    column = None
                    for a in range(7):
                        if r + a in rows:
                            term = rows[r + a] * conv_ref[a * 7 + b, lanes][None, :]
                            column = term if column is None else column + term
                    moved = column[b + 5 : b + 5 + W]
                    total = moved if total is None else total + moved
                here = (slice(r * W, (r + 1) * W), lanes)
                conv_out[here] = total if part == 0 else conv_out[here] + total
    normed = layer_norm(conv_out[...]).astype(BF)
    loads[1].wait()
    hidden = mm(normed, w_in_ref[...])
    hidden = 0.5 * hidden * (1.0 + lax.erf(hidden * math.sqrt(0.5)))
    loads[2].wait()
    back = mm(hidden.astype(BF), w_back_ref[...])
    own = mixed_ref[...].astype(F32)[:, E : E + W].reshape(CELLS, C)
    out_ref[...] = (own + back).astype(BF).reshape(R, W, C)


def per_device(field, w_qkv, w_out, conv_w, w_in, w_back):
    right = [(i, (i + 1) % LON) for i in range(LON)]
    left = [(j, i) for i, j in right]
    down = [(i, i + 1) for i in range(LAT - 1)]
    up = [(j, i) for i, j in down]
    along_y = [[y * ZS + z for y in range(YS)] for z in range(ZS)]
    along_z = [[y * ZS + z for z in range(ZS)] for y in range(YS)]
    row, merid, first, last = call(
        project_kernel,
        (shape(R, W, 384), shape(LAT, MCELLS, C), shape(MCELLS, C), shape(MCELLS, C)),
        200_000_000,
        in_specs=[ANY, ANY],
        scratch_shapes=[
            pltpu.VMEM((R, W, C), BF),
            pltpu.VMEM((C, 256), BF),
            pltpu.VMEM((C, 128), BF),
            pltpu.SemaphoreType.DMA((3,)),
        ],
    )(in_hbm(field), in_hbm(w_qkv))
    merid = lax.all_to_all(merid, "lat", 0, 0)
    row, merid = lax.optimization_barrier((row, merid))
    row = lax.all_to_all(row, "lon", 0, 0, axis_index_groups=along_z)
    merid = call(merid_kernel, shape(LAT, MCELLS, 256), 1_000_000_000)(merid, w_qkv)
    merid = lax.all_to_all(merid, "lat", 0, 0)
    slots = call(spread_kernel, shape(YS, KEYS, 128), 300_000_000)(row)
    slots, merid = lax.optimization_barrier((slots, merid))
    slots = lax.all_to_all(slots, "lon", 0, 0, axis_index_groups=along_y)
    edge_left = lax.ppermute(jnp.concatenate([merid[LAT - 1], last], axis=1), "lon", right)
    edge_right = lax.ppermute(jnp.concatenate([merid[0], first], axis=1), "lon", left)
    slots, edge_left, edge_right = lax.optimization_barrier((slots, edge_left, edge_right))
    y = (lax.axis_index("lon") // ZS).astype(jnp.int32).reshape(1)
    zonal = call(
        zonal_kernel, shape(ZS, WIDE, 256), 4_000_000_000, vmem=24, in_specs=[SMEM, VMEM, VMEM]
    )(y, row, slots)
    zonal = lax.all_to_all(zonal, "lon", 0, 0, axis_index_groups=along_z)
    mixed, first, last = call(
        mix_kernel, (shape(R, WIDE, C), shape(3, WIDE, C), shape(3, WIDE, C)), 800_000_000
    )(zonal, merid, edge_left, edge_right, field, w_out)
    before = lax.ppermute(last, "lat", down)
    after = lax.ppermute(first, "lat", up)
    return call(
        block_kernel,
        shape(R, W, C),
        2_000_000_000,
        in_specs=[ANY, VMEM, VMEM, VMEM, ANY, ANY],
        scratch_shapes=[
            pltpu.VMEM((R, WIDE, C), BF),
            pltpu.VMEM(w_in.shape, BF),
            pltpu.VMEM(w_back.shape, BF),
            pltpu.VMEM((CELLS, C), F32),
            pltpu.SemaphoreType.DMA((3,)),
        ],
    )(mixed, before, after, conv_w.reshape(49, C), in_hbm(w_in), in_hbm(w_back))


def solution(mesh):
    return jax.shard_map(
        per_device,
        mesh=mesh,
        in_specs=(P("lat", "lon", None), P(), P(), P(), P(), P()),
        out_specs=P("lat", "lon", None),
        check_vma=False,
    )
```

```python
import math

import jax
import jax.numpy as jnp
from jax import lax
from jax.experimental import pallas as pl
from jax.experimental.pallas import tpu as pltpu
from jax.sharding import PartitionSpec as P

C = 512
HD = 64
LAT = 16
LON = 32
R = 4
W = 64
CELLS = R * W
E = 8
WIDE = W + 2 * E
MC = WIDE // LAT
MROWS = 24
YS = 8
ZS = 4
SPAN = ZS * W
KEYS = SPAN + 2 * E
F32 = jnp.float32
BF = jnp.bfloat16


def iota(shape, dim):
    return lax.broadcasted_iota(jnp.int32, shape, dim)


def one_hot(hit):
    return jnp.where(hit, 1.0, 0.0).astype(BF)


def mm(a, b):
    return jnp.dot(a, b, preferred_element_type=F32)


def mm_nt(a, b):
    return lax.dot_general(a, b, (((1,), (1,)), ((), ())), preferred_element_type=F32)


def layer_norm(values):
    center = values - jnp.mean(values, axis=-1, keepdims=True)
    spread = jnp.mean(center * center, axis=-1, keepdims=True)
    return center * lax.rsqrt(spread + 1e-06)


def shape(*dims):
    return jax.ShapeDtypeStruct(dims, BF)


VMEM = pl.BlockSpec(memory_space=pltpu.VMEM)
ANY = pl.BlockSpec(memory_space=pl.ANY)
SMEM = pl.BlockSpec(memory_space=pltpu.SMEM)


def call(kernel, out_shape, flops, vmem=16, **kw):
    return pl.pallas_call(
        kernel,
        out_shape=out_shape,
        compiler_params=pltpu.CompilerParams(vmem_limit_bytes=vmem * 1024 * 1024),
        cost_estimate=pl.CostEstimate(flops=flops, bytes_accessed=2_000_000, transcendentals=0),
        **kw,
    )


def in_hbm(array):
    return pltpu.with_memory_space_constraint(array, pltpu.HBM)


def zonal_project_kernel(field_hbm, w_hbm, out_ref, first_ref, last_ref, field_ref, wq_ref, wkv_ref, sems):
    loads = [
        pltpu.make_async_copy(field_hbm, field_ref, sems.at[0]),
        pltpu.make_async_copy(w_hbm.at[:, 512:640], wkv_ref, sems.at[1]),
        pltpu.make_async_copy(w_hbm.at[:, 0:256], wq_ref, sems.at[2]),
    ]
    for load in loads:
        load.start()
    loads[0].wait()
    field = field_ref[...].astype(F32)
    first_ref[...] = field[:, 0:E].reshape(R * E, C).astype(BF)
    last_ref[...] = field[:, W - E : W].reshape(R * E, C).astype(BF)
    normed = layer_norm(field.reshape(CELLS, C)).astype(BF)
    loads[1].wait()
    out_ref[:, :, 256:384] = mm(normed, wkv_ref[...]).astype(BF).reshape(R, W, 128)
    loads[2].wait()
    out_ref[:, :, 0:256] = mm(normed, wq_ref[...]).astype(BF).reshape(R, W, 256)


def spread_kernel(in_ref, out_ref):
    kv = in_ref[:, :, 256:384].reshape(SPAN, 128)
    first = in_ref[0, :, 0:256].astype(F32)[0:E]
    last = in_ref[ZS - 1, :, 0:256].astype(F32)[W - E : W]
    edge = jnp.where(iota((E, 256), 0) < E // 2, first, last)
    edge = jnp.concatenate([edge[:, 0:128], edge[:, 128:256]], axis=0).astype(BF)
    for y in range(YS):
        out_ref[y, 0:SPAN, :] = kv
        out_ref[y, SPAN:KEYS, :] = edge


def zonal_kernel(y_ref, own_ref, all_ref, out_ref):
    y = y_ref[0]
    kv = all_ref[:, 0:SPAN, :].reshape(YS * SPAN, 128)
    ones = iota((YS * SPAN, 128), 1) < HD
    kv_one = jnp.where(ones, jnp.ones_like(kv), kv)
    behind = all_ref[lax.rem(y + YS - 1, YS), SPAN:KEYS, :].astype(F32)
    ahead = all_ref[lax.rem(y + 1, YS), SPAN:KEYS, :].astype(F32)
    count = SPAN + 2 * E
    low = iota((count, 128), 1) < HD
    for pair in range(2):
        lanes = slice(pair * 128, pair * 128 + 128)
        rows = slice(pair * E, pair * E + E)
        q = own_ref[:, :, lanes].astype(F32).reshape(SPAN, 128)
        q = jnp.concatenate([behind[rows], q, ahead[rows]], axis=0) * (1.0 / math.sqrt(HD))
        outs = []
        for head in range(2):
            placed = q if head == 0 else pltpu.roll(q, HD, 1)
            placed = jnp.where(low, placed, 0.0).astype(BF)
            score = mm_nt(placed, kv)
            weight = jnp.exp(score - jnp.max(score, axis=-1, keepdims=True)).astype(BF)
            outs.append(mm(weight, kv_one))
        even, odd = outs
        blended = jnp.where(low, pltpu.roll(even, HD, 1), odd)
        mass = jnp.where(low, even, pltpu.roll(odd, HD, 1))
        heads = blended / mass
        for z in range(ZS):
            out_ref[z, :, lanes] = heads[z * W : z * W + WIDE].astype(BF)


def widened(left, own, right):
    left, right = (a.astype(F32).reshape(R, E, a.shape[-1]) for a in (left, right))
    return jnp.concatenate([left, own.astype(F32), right], axis=1)


def merid_slots():
    dims = (LAT, MROWS, R * WIDE)
    m, i, u = iota(dims, 0), iota(dims, 1), iota(dims, 2)
    cell = (i & 3) * WIDE + m * MC + (i >> 2)
    return one_hot((cell == u) & (i < R * MC)).reshape(LAT * MROWS, R * WIDE)


def merid_select_kernel(field_ref, left_ref, right_ref, out_ref):
    wide = widened(left_ref[...], field_ref[...], right_ref[...]).reshape(R * WIDE, C)
    normed = mm(merid_slots(), layer_norm(wide).astype(BF))
    out_ref[...] = normed.reshape(LAT, MROWS, C).astype(BF)


def merid_kernel(in_ref, w_ref, out_ref):
    count = LAT * MROWS
    normed = in_ref[...].astype(F32).reshape(count, C).astype(BF)
    queries = mm(normed, w_ref[:, 256:512]).astype(BF)
    keys = mm(normed, w_ref[:, 640:896]).astype(BF)
    values = mm(normed, w_ref[:, 896:1152]).astype(BF)
    row = iota((LAT, MROWS, count), 1).reshape(count, count) >> 2
    key = iota((count, count), 1)
    key = (key - ((key * 2731) >> 16) * MROWS) >> 2
    bias = jnp.where(row == key, 0.0, -1e30)
    low = iota((count, 128), 1) < HD
    scale = 1.0 / math.sqrt(HD)
    for pair in range(2):
        lanes = slice(pair * 128, pair * 128 + 128)
        q, k, v = queries[:, lanes], keys[:, lanes], values[:, lanes]
        outs = []
        for side in (low, jnp.logical_not(low)):
            score = mm_nt(jnp.where(side, q, jnp.zeros_like(q)), k) * scale + bias
            weight = jnp.exp(score - jnp.max(score, axis=-1, keepdims=True))
            mass = jnp.sum(weight, axis=-1, keepdims=True)
            outs.append(mm(weight.astype(BF), v) / mass)
        both = jnp.where(low, outs[0], outs[1]).reshape(LAT, MROWS, 128)
        out_ref[:, :, lanes] = both.astype(BF)


def mix_kernel(odd_ref, zonal_ref, merid_ref, left_ref, right_ref, field_ref, w_ref, mixed_ref, far_ref, near_ref):
    rows = R * WIDE
    merid = merid_ref[...].astype(F32).reshape(LAT * MROWS, 256).astype(BF)
    dims = (R, WIDE, LAT * MROWS)
    r, w, t = iota(dims, 0), iota(dims, 1), iota(dims, 2)
    m = (t * 2731) >> 16
    i = t - m * MROWS
    cell = one_hot((m * MC + (i >> 2) == w) & ((i & 3) == r) & (i < R * MC))
    merid = mm(cell.reshape(rows, LAT * MROWS), merid).astype(BF)
    attended = mm(zonal_ref[...].reshape(rows, 256), w_ref[0:256]) + mm(merid, w_ref[256:512])
    wide = widened(left_ref[...], field_ref[...], right_ref[...])
    mixed = (wide + attended.reshape(R, WIDE, C)).astype(BF)
    mixed_ref[...] = mixed
    odd = odd_ref[0] == 1

    @pl.when(odd)
    def after_is_far():
        far_ref[...] = mixed[1:4]
        near_ref[...] = mixed[0:3]

    @pl.when(jnp.logical_not(odd))
    def before_is_far():
        far_ref[...] = mixed[0:3]
        near_ref[...] = mixed[1:4]


def conv_part(rows, conv_ref, lanes, r):
    total = None
    for b in range(7):
        column = None
        for a in range(7):
            if r + a in rows:
                term = rows[r + a] * conv_ref[a * 7 + b, lanes][None, :]
                column = term if column is None else column + term
        moved = column[b + 5 : b + 5 + W]
        total = moved if total is None else total + moved
    return total


def own_conv_kernel(mixed_ref, conv_ref, out_ref):
    for lane in range(0, C, 128):
        lanes = slice(lane, lane + 128)
        rows = {3 + i: mixed_ref[i, :, lanes].astype(F32) for i in range(R)}
        for r in range(R):
            out_ref[r * W : (r + 1) * W, lanes] = conv_part(rows, conv_ref, lanes, r)


def block_kernel(
    odd_ref, mixed_hbm, own_ref, far_ref, near_ref, conv_ref, w_in_hbm, w_back_hbm, out_ref,
    mixed_ref, w_in_ref, w_back_ref, conv_out, sems,
):
    pairs = ((w_in_hbm, w_in_ref), (w_back_hbm, w_back_ref), (mixed_hbm, mixed_ref))
    loads = [pltpu.make_async_copy(a, b, sems.at[i]) for i, (a, b) in enumerate(pairs)]
    for load in loads:
        load.start()
    odd = odd_ref[0] == 1
    for lane in range(0, C, 128):
        lanes = slice(lane, lane + 128)
        rows = {}
        for i in range(3):
            far, near = far_ref[i, :, lanes].astype(F32), near_ref[i, :, lanes].astype(F32)
            rows[i] = jnp.where(odd, near, far)
            rows[7 + i] = jnp.where(odd, far, near)
        for r in range(R):
            here = (slice(r * W, (r + 1) * W), lanes)
            conv_out[here] = own_ref[here] + conv_part(rows, conv_ref, lanes, r)
    normed = layer_norm(conv_out[...]).astype(BF)
    loads[0].wait()
    hidden = mm(normed, w_in_ref[...])
    hidden = 0.5 * hidden * (1.0 + lax.erf(hidden * math.sqrt(0.5)))
    loads[1].wait()
    back = mm(hidden.astype(BF), w_back_ref[...])
    loads[2].wait()
    own = mixed_ref[...].astype(F32)[:, E : E + W].reshape(CELLS, C)
    out_ref[...] = (own + back).astype(BF).reshape(R, W, C)


def per_device(field, w_qkv, w_out, conv_w, w_in, w_back):
    right = [(i, (i + 1) % LON) for i in range(LON)]
    left = [(j, i) for i, j in right]
    near_pairs = [(i, i + 1) for i in range(0, LAT, 2)]
    far_pairs = [(i, i + 1) for i in range(1, LAT - 1, 2)]
    near_pairs, far_pairs = (pairs + [(j, i) for i, j in pairs] for pairs in (near_pairs, far_pairs))
    along_y = [[y * ZS + z for y in range(YS)] for z in range(ZS)]
    along_z = [[y * ZS + z for z in range(ZS)] for y in range(YS)]
    y = (lax.axis_index("lon").astype(jnp.int32) >> 2).reshape(1)
    odd = (lax.axis_index("lat").astype(jnp.int32) & 1).reshape(1)
    field, y, odd = lax.optimization_barrier((field, y, odd))
    row, first, last = call(
        zonal_project_kernel,
        (shape(R, W, 384), shape(R * E, C), shape(R * E, C)),
        200_000_000,
        in_specs=[ANY, ANY],
        scratch_shapes=[
            pltpu.VMEM((R, W, C), BF),
            pltpu.VMEM((C, 256), BF),
            pltpu.VMEM((C, 128), BF),
            pltpu.SemaphoreType.DMA((3,)),
        ],
    )(in_hbm(field), in_hbm(w_qkv))
    row = lax.all_to_all(row, "lon", 0, 0, axis_index_groups=along_z)
    slots = call(spread_kernel, shape(YS, KEYS, 128), 10_000_000)(row)
    slots = lax.all_to_all(slots, "lon", 0, 0, axis_index_groups=along_y)
    field_left = lax.ppermute(last, "lon", right)
    field_right = lax.ppermute(first, "lon", left)
    merid = call(merid_select_kernel, shape(LAT, MROWS, C), 300_000_000)(
        field, field_left, field_right
    )
    slots, merid = lax.optimization_barrier((slots, merid))
    merid = lax.all_to_all(merid, "lat", 0, 0)
    zonal = call(
        zonal_kernel, shape(ZS, WIDE, 256), 4_000_000_000, vmem=24, in_specs=[SMEM, VMEM, VMEM]
    )(y, row, slots)
    zonal = lax.all_to_all(zonal, "lon", 0, 0, axis_index_groups=along_z)
    merid = call(merid_kernel, shape(LAT, MROWS, 256), 1_000_000_000)(merid, w_qkv)
    merid = lax.all_to_all(merid, "lat", 0, 0)
    mixed, far, near = call(
        mix_kernel,
        (shape(R, WIDE, C), shape(3, WIDE, C), shape(3, WIDE, C)),
        800_000_000,
        in_specs=[SMEM] + [VMEM] * 6,
    )(odd, zonal, merid, field_left, field_right, field, w_out)
    near = lax.ppermute(near, "lat", near_pairs)
    far = lax.ppermute(far, "lat", far_pairs)
    conv_w = conv_w.reshape(49, C)
    own = call(own_conv_kernel, jax.ShapeDtypeStruct((CELLS, C), F32), 1_000_000_000)(mixed, conv_w)
    return call(
        block_kernel,
        shape(R, W, C),
        2_000_000_000,
        in_specs=[SMEM, ANY, VMEM, VMEM, VMEM, VMEM, ANY, ANY],
        scratch_shapes=[
            pltpu.VMEM((R, WIDE, C), BF),
            pltpu.VMEM(w_in.shape, BF),
            pltpu.VMEM(w_back.shape, BF),
            pltpu.VMEM((CELLS, C), F32),
            pltpu.SemaphoreType.DMA((3,)),
        ],
    )(odd, mixed, own, far, near, conv_w, in_hbm(w_in), in_hbm(w_back))


def solution(mesh):
    return jax.shard_map(
        per_device,
        mesh=mesh,
        in_specs=(P("lat", "lon", None), P(), P(), P(), P(), P()),
        out_specs=P("lat", "lon", None),
        check_vma=False,
    )
```

```python
import math

import jax
import jax.numpy as jnp
from jax import lax
from jax.experimental import pallas as pl
from jax.experimental.pallas import tpu as pltpu
from jax.sharding import PartitionSpec as P

C = 512
HD = 64
LAT = 16
LON = 32
R = 4
W = 64
CELLS = R * W
E = 8
WIDE = W + 2 * E
MC = WIDE // LAT
EDGES = (1, LAT - 2)
MROWS = 24
YS = 8
ZS = 4
SPAN = ZS * W
KEYS = SPAN + 2 * E
F32 = jnp.float32
BF = jnp.bfloat16


def iota(shape, dim):
    return lax.broadcasted_iota(jnp.int32, shape, dim)


def one_hot(hit):
    return jnp.where(hit, 1.0, 0.0).astype(BF)


def mm(a, b):
    return jnp.dot(a, b, preferred_element_type=F32)


def mm_nt(a, b):
    return lax.dot_general(a, b, (((1,), (1,)), ((), ())), preferred_element_type=F32)


def layer_norm(values):
    center = values - jnp.mean(values, axis=-1, keepdims=True)
    spread = jnp.mean(center * center, axis=-1, keepdims=True)
    return center * lax.rsqrt(spread + 1e-06)


def shape(*dims):
    return jax.ShapeDtypeStruct(dims, BF)


VMEM = pl.BlockSpec(memory_space=pltpu.VMEM)
ANY = pl.BlockSpec(memory_space=pl.ANY)
SMEM = pl.BlockSpec(memory_space=pltpu.SMEM)


def call(kernel, out_shape, flops, vmem=16, **kw):
    return pl.pallas_call(
        kernel,
        out_shape=out_shape,
        compiler_params=pltpu.CompilerParams(vmem_limit_bytes=vmem * 1024 * 1024),
        cost_estimate=pl.CostEstimate(flops=flops, bytes_accessed=2_000_000, transcendentals=0),
        **kw,
    )


def in_hbm(array):
    return pltpu.with_memory_space_constraint(array, pltpu.HBM)


def zonal_project_kernel(field_hbm, w_hbm, out_ref, first_ref, last_ref, field_ref, wq_ref, wkv_ref, sems):
    loads = [
        pltpu.make_async_copy(field_hbm, field_ref, sems.at[0]),
        pltpu.make_async_copy(w_hbm.at[:, 512:640], wkv_ref, sems.at[1]),
        pltpu.make_async_copy(w_hbm.at[:, 0:256], wq_ref, sems.at[2]),
    ]
    for load in loads:
        load.start()
    loads[0].wait()
    field = field_ref[...].astype(F32)
    first_ref[...] = field[:, 0:E].reshape(R * E, C).astype(BF)
    last_ref[...] = field[:, W - E : W].reshape(R * E, C).astype(BF)
    normed = layer_norm(field.reshape(CELLS, C)).astype(BF)
    loads[1].wait()
    out_ref[:, :, 256:384] = mm(normed, wkv_ref[...]).astype(BF).reshape(R, W, 128)
    loads[2].wait()
    out_ref[:, :, 0:256] = mm(normed, wq_ref[...]).astype(BF).reshape(R, W, 256)


def spread_kernel(in_ref, out_hbm, slot_ref, sems):
    slot_ref[0:SPAN, :] = in_ref[:, :, 256:384].reshape(SPAN, 128)
    first = in_ref[0, :, 0:256].astype(F32)[0:E]
    last = in_ref[ZS - 1, :, 0:256].astype(F32)[W - E : W]
    edge = jnp.where(iota((E, 256), 0) < E // 2, first, last)
    slot_ref[SPAN:KEYS, :] = jnp.concatenate([edge[:, 0:128], edge[:, 128:256]], axis=0).astype(BF)
    copies = [pltpu.make_async_copy(slot_ref, out_hbm.at[y], sems.at[y]) for y in range(YS)]
    for copy in copies:
        copy.start()
    for copy in copies:
        copy.wait()


def zonal_kernel(y_ref, own_ref, all_ref, out_ref):
    y = y_ref[0]
    kv = all_ref[:, 0:SPAN, :].reshape(YS * SPAN, 128)
    ones = iota((YS * SPAN, 128), 1) < HD
    kv_one = jnp.where(ones, jnp.ones_like(kv), kv)
    behind = all_ref[lax.rem(y + YS - 1, YS), SPAN:KEYS, :].astype(F32)
    ahead = all_ref[lax.rem(y + 1, YS), SPAN:KEYS, :].astype(F32)
    count = SPAN + 2 * E
    low = iota((count, 128), 1) < HD
    for pair in range(2):
        lanes = slice(pair * 128, pair * 128 + 128)
        rows = slice(pair * E, pair * E + E)
        q = own_ref[:, :, lanes].astype(F32).reshape(SPAN, 128)
        q = jnp.concatenate([behind[rows], q, ahead[rows]], axis=0) * (1.0 / math.sqrt(HD))
        outs = []
        for head in range(2):
            placed = q if head == 0 else pltpu.roll(q, HD, 1)
            placed = jnp.where(low, placed, 0.0).astype(BF)
            score = mm_nt(placed, kv)
            weight = jnp.exp(score - jnp.max(score, axis=-1, keepdims=True)).astype(BF)
            outs.append(mm(weight, kv_one))
        even, odd = outs
        blended = jnp.where(low, pltpu.roll(even, HD, 1), odd)
        mass = jnp.where(low, even, pltpu.roll(odd, HD, 1))
        heads = blended / mass
        for z in range(ZS):
            out_ref[z, :, lanes] = heads[z * W : z * W + WIDE].astype(BF)


def widened(left, own, right):
    left, right = (a.astype(F32).reshape(R, E, a.shape[-1]) for a in (left, right))
    return jnp.concatenate([left, own.astype(F32), right], axis=1)


def merid_own_kernel(field_ref, out_ref, edge_ref):
    normed = layer_norm(field_ref[...].astype(F32).reshape(CELLS, C)).astype(BF)
    dims = (LAT, MROWS, CELLS)
    m, i, u = iota(dims, 0), iota(dims, 1), iota(dims, 2)
    c = m * MC + (i >> 2) - E
    hit = ((i & 3) * W + c == u) & (c >= 0) & (c < W) & (i < R * MC)
    slots = mm(one_hot(hit).reshape(LAT * MROWS, CELLS), normed).reshape(LAT, MROWS, C).astype(BF)
    out_ref[...] = slots
    edge_ref[0] = slots[EDGES[0]]
    edge_ref[1] = slots[EDGES[1]]


def merid_edge_kernel(slots_hbm, edge_ref, left_ref, right_ref, out_hbm, done_ref, sems):
    copies = []
    for n, (m, ref) in enumerate(zip(EDGES, (left_ref, right_ref))):
        normed = layer_norm(ref[...].astype(F32)).astype(BF)
        i, u = iota((MROWS, R * E), 0), iota((MROWS, R * E), 1)
        c = m * MC + (i >> 2) - n * (W + E)
        hit = ((i & 3) * E + c == u) & (c >= 0) & (c < E) & (i < R * MC)
        done_ref[n] = (edge_ref[n].astype(F32) + mm(one_hot(hit), normed)).astype(BF)
        copies.append(pltpu.make_async_copy(done_ref.at[n], out_hbm.at[m], sems.at[n]))
        copies[n].start()
    for copy in copies:
        copy.wait()


def merid_kernel(in_ref, w_ref, out_ref):
    count = LAT * MROWS
    normed = in_ref[...].astype(F32).reshape(count, C).astype(BF)
    queries = mm(normed, w_ref[:, 256:512]).astype(BF)
    keys = mm(normed, w_ref[:, 640:896]).astype(BF)
    values = mm(normed, w_ref[:, 896:1152]).astype(BF)
    row = iota((LAT, MROWS, count), 1).reshape(count, count) >> 2
    key = iota((count, count), 1)
    key = (key - ((key * 2731) >> 16) * MROWS) >> 2
    bias = jnp.where(row == key, 0.0, -1e30)
    low = iota((count, 128), 1) < HD
    scale = 1.0 / math.sqrt(HD)
    for pair in range(2):
        lanes = slice(pair * 128, pair * 128 + 128)
        q, k, v = queries[:, lanes], keys[:, lanes], values[:, lanes]
        outs = []
        for side in (low, jnp.logical_not(low)):
            score = mm_nt(jnp.where(side, q, jnp.zeros_like(q)), k) * scale + bias
            weight = jnp.exp(score - jnp.max(score, axis=-1, keepdims=True))
            mass = jnp.sum(weight, axis=-1, keepdims=True)
            outs.append(mm(weight.astype(BF), v) / mass)
        both = jnp.where(low, outs[0], outs[1]).reshape(LAT, MROWS, 128)
        out_ref[:, :, lanes] = both.astype(BF)


def mix_kernel(odd_ref, zonal_ref, merid_ref, left_ref, right_ref, field_ref, w_ref, mixed_ref, far_ref, near_ref):
    rows = R * WIDE
    merid = merid_ref[...].astype(F32).reshape(LAT * MROWS, 256).astype(BF)
    dims = (R, WIDE, LAT * MROWS)
    r, w, t = iota(dims, 0), iota(dims, 1), iota(dims, 2)
    m = (t * 2731) >> 16
    i = t - m * MROWS
    cell = one_hot((m * MC + (i >> 2) == w) & ((i & 3) == r) & (i < R * MC))
    merid = mm(cell.reshape(rows, LAT * MROWS), merid).astype(BF)
    attended = mm(zonal_ref[...].reshape(rows, 256), w_ref[0:256]) + mm(merid, w_ref[256:512])
    wide = widened(left_ref[...], field_ref[...], right_ref[...])
    mixed = (wide + attended.reshape(R, WIDE, C)).astype(BF)
    mixed_ref[...] = mixed
    odd = odd_ref[0] == 1

    @pl.when(odd)
    def after_is_far():
        far_ref[...] = mixed[1:4]
        near_ref[...] = mixed[0:3]

    @pl.when(jnp.logical_not(odd))
    def before_is_far():
        far_ref[...] = mixed[0:3]
        near_ref[...] = mixed[1:4]


def conv_part(rows, conv_ref, lanes, r):
    total = None
    for b in range(7):
        column = None
        for a in range(7):
            if r + a in rows:
                term = rows[r + a] * conv_ref[a * 7 + b, lanes][None, :]
                column = term if column is None else column + term
        moved = column[b + 5 : b + 5 + W]
        total = moved if total is None else total + moved
    return total


def own_conv_kernel(
    mixed_ref, conv_ref, w_in_hbm, w_back_hbm, out_ref, w_in_ref, w_back_ref, sems
):
    pairs = ((w_in_hbm, w_in_ref), (w_back_hbm, w_back_ref))
    loads = [pltpu.make_async_copy(a, b, sems.at[i]) for i, (a, b) in enumerate(pairs)]
    for load in loads:
        load.start()
    for lane in range(0, C, 128):
        lanes = slice(lane, lane + 128)
        rows = {3 + i: mixed_ref[i, :, lanes].astype(F32) for i in range(R)}
        for r in range(R):
            out_ref[r * W : (r + 1) * W, lanes] = conv_part(rows, conv_ref, lanes, r)
    for load in loads:
        load.wait()


def block_kernel(
    odd_ref, mixed_ref, own_ref, far_ref, near_ref, conv_ref, w_in_ref, w_back_ref, out_ref, conv_out
):
    odd = odd_ref[0] == 1
    for lane in range(0, C, 128):
        lanes = slice(lane, lane + 128)
        rows = {}
        for i in range(3):
            far, near = far_ref[i, :, lanes].astype(F32), near_ref[i, :, lanes].astype(F32)
            rows[i] = jnp.where(odd, near, far)
            rows[7 + i] = jnp.where(odd, far, near)
        for r in range(R):
            here = (slice(r * W, (r + 1) * W), lanes)
            conv_out[here] = own_ref[here] + conv_part(rows, conv_ref, lanes, r)
    normed = layer_norm(conv_out[...]).astype(BF)
    hidden = mm(normed, w_in_ref[...])
    hidden = 0.5 * hidden * (1.0 + lax.erf(hidden * math.sqrt(0.5)))
    back = mm(hidden.astype(BF), w_back_ref[...])
    own = mixed_ref[...].astype(F32)[:, E : E + W].reshape(CELLS, C)
    out_ref[...] = (own + back).astype(BF).reshape(R, W, C)


def per_device(field, w_qkv, w_out, conv_w, w_in, w_back):
    right = [(i, (i + 1) % LON) for i in range(LON)]
    left = [(j, i) for i, j in right]
    near_pairs = [(i, i + 1) for i in range(0, LAT, 2)]
    far_pairs = [(i, i + 1) for i in range(1, LAT - 1, 2)]
    near_pairs, far_pairs = (pairs + [(j, i) for i, j in pairs] for pairs in (near_pairs, far_pairs))
    along_y = [[y * ZS + z for y in range(YS)] for z in range(ZS)]
    along_z = [[y * ZS + z for z in range(ZS)] for y in range(YS)]
    y = (lax.axis_index("lon").astype(jnp.int32) >> 2).reshape(1)
    odd = (lax.axis_index("lat").astype(jnp.int32) & 1).reshape(1)
    field, y, odd = lax.optimization_barrier((field, y, odd))
    row, first, last = call(
        zonal_project_kernel,
        (shape(R, W, 384), shape(R * E, C), shape(R * E, C)),
        200_000_000,
        in_specs=[ANY, ANY],
        scratch_shapes=[
            pltpu.VMEM((R, W, C), BF),
            pltpu.VMEM((C, 256), BF),
            pltpu.VMEM((C, 128), BF),
            pltpu.SemaphoreType.DMA((3,)),
        ],
    )(in_hbm(field), in_hbm(w_qkv))
    row = lax.all_to_all(row, "lon", 0, 0, axis_index_groups=along_z)
    slots = call(
        spread_kernel,
        shape(YS, KEYS, 128),
        10_000_000,
        out_specs=ANY,
        scratch_shapes=[pltpu.VMEM((KEYS, 128), BF), pltpu.SemaphoreType.DMA((YS,))],
    )(row)
    slots = lax.all_to_all(slots, "lon", 0, 0, axis_index_groups=along_y)
    field_left = lax.ppermute(last, "lon", right)
    field_right = lax.ppermute(first, "lon", left)
    merid, merid_edges = call(
        merid_own_kernel, (shape(LAT, MROWS, C), shape(2, MROWS, C)), 300_000_000
    )(field)
    merid = call(
        merid_edge_kernel,
        shape(LAT, MROWS, C),
        10_000_000,
        in_specs=[ANY, VMEM, VMEM, VMEM],
        out_specs=ANY,
        input_output_aliases={0: 0},
        scratch_shapes=[pltpu.VMEM((2, MROWS, C), BF), pltpu.SemaphoreType.DMA((2,))],
    )(merid, merid_edges, field_left, field_right)
    slots, merid = lax.optimization_barrier((slots, merid))
    merid = lax.all_to_all(merid, "lat", 0, 0)
    zonal = call(
        zonal_kernel, shape(ZS, WIDE, 256), 4_000_000_000, vmem=24, in_specs=[SMEM, VMEM, VMEM]
    )(y, row, slots)
    zonal = lax.all_to_all(zonal, "lon", 0, 0, axis_index_groups=along_z)
    merid = call(merid_kernel, shape(LAT, MROWS, 256), 1_000_000_000)(merid, w_qkv)
    merid = lax.all_to_all(merid, "lat", 0, 0)
    mixed, far, near = call(
        mix_kernel,
        (shape(R, WIDE, C), shape(3, WIDE, C), shape(3, WIDE, C)),
        800_000_000,
        in_specs=[SMEM] + [VMEM] * 6,
    )(odd, zonal, merid, field_left, field_right, field, w_out)
    near = lax.ppermute(near, "lat", near_pairs)
    far = lax.ppermute(far, "lat", far_pairs)
    conv_w = conv_w.reshape(49, C)
    own, w_in, w_back = call(
        own_conv_kernel,
        (jax.ShapeDtypeStruct((CELLS, C), F32), shape(*w_in.shape), shape(*w_back.shape)),
        1_000_000_000,
        in_specs=[VMEM, VMEM, ANY, ANY],
        scratch_shapes=[pltpu.SemaphoreType.DMA((2,))],
    )(mixed, conv_w, in_hbm(w_in), in_hbm(w_back))
    return call(
        block_kernel,
        shape(R, W, C),
        2_000_000_000,
        in_specs=[SMEM] + [VMEM] * 7,
        scratch_shapes=[pltpu.VMEM((CELLS, C), F32)],
    )(odd, mixed, own, far, near, conv_w, w_in, w_back)


def solution(mesh):
    return jax.shard_map(
        per_device,
        mesh=mesh,
        in_specs=(P("lat", "lon", None), P(), P(), P(), P(), P()),
        out_specs=P("lat", "lon", None),
        check_vma=False,
    )
```

```python
import math

import jax
import jax.numpy as jnp
from jax import lax
from jax.experimental import pallas as pl
from jax.experimental.pallas import tpu as pltpu
from jax.sharding import PartitionSpec as P

C = 512
HD = 64
LAT = 16
LON = 32
R = 4
W = 64
CELLS = R * W
E = 8
WIDE = W + 2 * E
MC = WIDE // LAT
EDGES = (1, LAT - 2)
ECELLS = 16
MROWS = 24
YS = 8
ZS = 4
SPAN = ZS * W
KEYS = SPAN + 2 * E
F32 = jnp.float32
BF = jnp.bfloat16


def iota(shape, dim):
    return lax.broadcasted_iota(jnp.int32, shape, dim)


def one_hot(hit):
    return jnp.where(hit, 1.0, 0.0).astype(BF)


def mm(a, b):
    return jnp.dot(a, b, preferred_element_type=F32)


def mm_nt(a, b):
    return lax.dot_general(a, b, (((1,), (1,)), ((), ())), preferred_element_type=F32)


def layer_norm(values):
    center = values - jnp.mean(values, axis=-1, keepdims=True)
    spread = jnp.mean(center * center, axis=-1, keepdims=True)
    return center * lax.rsqrt(spread + 1e-06)


def shape(*dims):
    return jax.ShapeDtypeStruct(dims, BF)


VMEM = pl.BlockSpec(memory_space=pltpu.VMEM)
ANY = pl.BlockSpec(memory_space=pl.ANY)
SMEM = pl.BlockSpec(memory_space=pltpu.SMEM)


def call(kernel, out_shape, flops, vmem=16, **kw):
    return pl.pallas_call(
        kernel,
        out_shape=out_shape,
        compiler_params=pltpu.CompilerParams(vmem_limit_bytes=vmem * 1024 * 1024),
        cost_estimate=pl.CostEstimate(flops=flops, bytes_accessed=2_000_000, transcendentals=0),
        **kw,
    )


def in_hbm(array):
    return pltpu.with_memory_space_constraint(array, pltpu.HBM)


def packed(edge):
    return jnp.concatenate([edge[:, lane : lane + 128] for lane in range(0, C, 128)], axis=0)


def unpacked(rows):
    return jnp.concatenate([rows[i : i + ECELLS] for i in range(0, W, ECELLS)], axis=1)


def zonal_project_kernel(
    z_ref, field_hbm, w_hbm, out_ref, border_ref, field_ref, wq_ref, wkv_ref, sems
):
    loads = [
        pltpu.make_async_copy(field_hbm, field_ref, sems.at[0]),
        pltpu.make_async_copy(w_hbm.at[:, 512:640], wkv_ref, sems.at[1]),
        pltpu.make_async_copy(w_hbm.at[:, 0:256], wq_ref, sems.at[2]),
    ]
    for load in loads:
        load.start()
    z = z_ref[0]
    i, u = iota((2 * ECELLS, CELLS), 0), iota((2 * ECELLS, CELLS), 1)
    select = one_hot(u == ((i >> 2) & 3) * W + (i & 3) + jnp.where(i < ECELLS, 0, W - 4))
    loads[0].wait()
    field = field_ref[...].astype(F32).reshape(CELLS, C)
    edges = mm(select, field.astype(BF)).astype(BF)
    first, last = edges[0:ECELLS], edges[ECELLS:]
    border_ref[...] = jnp.where(z == ZS - 1, last.astype(F32), first.astype(F32)).astype(BF)
    out_ref[:, :, 384:512] = jnp.zeros((R, W, 128), BF)
    out_ref[(z + 1) & 3, :, 384:512] = packed(last)
    out_ref[(z + 3) & 3, :, 384:512] = packed(first)
    normed = layer_norm(field).astype(BF)
    loads[1].wait()
    out_ref[:, :, 256:384] = mm(normed, wkv_ref[...]).astype(BF).reshape(R, W, 128)
    loads[2].wait()
    out_ref[:, :, 0:256] = mm(normed, wq_ref[...]).astype(BF).reshape(R, W, 256)


def spread_kernel(in_ref, out_hbm, slot_ref, sems):
    slot_ref[0:SPAN, :] = in_ref[:, :, 256:384].reshape(SPAN, 128)
    first = in_ref[0, :, 0:256].astype(F32)[0:E]
    last = in_ref[ZS - 1, :, 0:256].astype(F32)[W - E : W]
    edge = jnp.where(iota((E, 256), 0) < E // 2, first, last)
    slot_ref[SPAN:KEYS, :] = jnp.concatenate([edge[:, 0:128], edge[:, 128:256]], axis=0).astype(BF)
    copies = [pltpu.make_async_copy(slot_ref, out_hbm.at[y], sems.at[y]) for y in range(YS)]
    for copy in copies:
        copy.start()
    for copy in copies:
        copy.wait()


def zonal_kernel(y_ref, own_ref, all_ref, out_ref):
    y = y_ref[0]
    kv = all_ref[:, 0:SPAN, :].reshape(YS * SPAN, 128)
    ones = iota((YS * SPAN, 128), 1) < HD
    kv_one = jnp.where(ones, jnp.ones_like(kv), kv)
    behind = all_ref[lax.rem(y + YS - 1, YS), SPAN:KEYS, :].astype(F32)
    ahead = all_ref[lax.rem(y + 1, YS), SPAN:KEYS, :].astype(F32)
    count = SPAN + 2 * E
    low = iota((count, 128), 1) < HD
    for pair in range(2):
        lanes = slice(pair * 128, pair * 128 + 128)
        rows = slice(pair * E, pair * E + E)
        q = own_ref[:, :, lanes].astype(F32).reshape(SPAN, 128)
        q = jnp.concatenate([behind[rows], q, ahead[rows]], axis=0) * (1.0 / math.sqrt(HD))
        outs = []
        for head in range(2):
            placed = q if head == 0 else pltpu.roll(q, HD, 1)
            placed = jnp.where(low, placed, 0.0).astype(BF)
            score = mm_nt(placed, kv)
            weight = jnp.exp(score - jnp.max(score, axis=-1, keepdims=True)).astype(BF)
            outs.append(mm(weight, kv_one))
        even, odd = outs
        blended = jnp.where(low, pltpu.roll(even, HD, 1), odd)
        mass = jnp.where(low, even, pltpu.roll(odd, HD, 1))
        heads = blended / mass
        for z in range(ZS):
            out_ref[z, :, lanes] = heads[z * W : z * W + WIDE].astype(BF)


def merid_own_kernel(field_ref, out_ref, edge_ref):
    normed = layer_norm(field_ref[...].astype(F32).reshape(CELLS, C)).astype(BF)
    dims = (LAT, MROWS, CELLS)
    m, i, u = iota(dims, 0), iota(dims, 1), iota(dims, 2)
    c = m * MC + (i >> 2) - E
    hit = ((i & 3) * W + c == u) & (c >= 0) & (c < W) & (i < R * MC)
    slots = mm(one_hot(hit).reshape(LAT * MROWS, CELLS), normed).reshape(LAT, MROWS, C).astype(BF)
    out_ref[...] = slots
    edge_ref[0] = slots[EDGES[0]]
    edge_ref[1] = slots[EDGES[1]]


def merid_edge_kernel(
    z_ref, slots_hbm, edge_ref, row_ref, border_ref, out_hbm, left_ref, right_ref, done_ref, sems
):
    z = z_ref[0]
    border = border_ref[...].astype(F32)
    copies = []
    for n, (m, ref) in enumerate(zip(EDGES, (left_ref, right_ref))):
        beside, outer = ((z + 3) & 3, 0) if n == 0 else ((z + 1) & 3, ZS - 1)
        halo = unpacked(row_ref[beside, :, 384:512]).astype(F32)
        halo = jnp.where(z == outer, border, halo)
        ref[...] = halo.astype(BF)
        normed = layer_norm(halo).astype(BF)
        i, u = iota((MROWS, ECELLS), 0), iota((MROWS, ECELLS), 1)
        c = m * MC + (i >> 2) - (E // 2 if n == 0 else W + E)
        hit = ((i & 3) * 4 + c == u) & (c >= 0) & (c < 4) & (i < R * MC)
        done_ref[n] = (edge_ref[n].astype(F32) + mm(one_hot(hit), normed)).astype(BF)
        copies.append(pltpu.make_async_copy(done_ref.at[n], out_hbm.at[m], sems.at[n]))
        copies[n].start()
    for copy in copies:
        copy.wait()


def merid_kernel(in_ref, w_ref, out_ref):
    count = LAT * MROWS
    normed = in_ref[...].astype(F32).reshape(count, C).astype(BF)
    queries = mm(normed, w_ref[:, 256:512]).astype(BF)
    keys = mm(normed, w_ref[:, 640:896]).astype(BF)
    values = mm(normed, w_ref[:, 896:1152]).astype(BF)
    row = iota((LAT, MROWS, count), 1).reshape(count, count) >> 2
    key = iota((count, count), 1)
    key = (key - ((key * 2731) >> 16) * MROWS) >> 2
    bias = jnp.where(row == key, 0.0, -1e30)
    low = iota((count, 128), 1) < HD
    scale = 1.0 / math.sqrt(HD)
    for pair in range(2):
        lanes = slice(pair * 128, pair * 128 + 128)
        q, k, v = queries[:, lanes], keys[:, lanes], values[:, lanes]
        outs = []
        for side in (low, jnp.logical_not(low)):
            score = mm_nt(jnp.where(side, q, jnp.zeros_like(q)), k) * scale + bias
            weight = jnp.exp(score - jnp.max(score, axis=-1, keepdims=True))
            mass = jnp.sum(weight, axis=-1, keepdims=True)
            outs.append(mm(weight.astype(BF), v) / mass)
        both = jnp.where(low, outs[0], outs[1]).reshape(LAT, MROWS, 128)
        out_ref[:, :, lanes] = both.astype(BF)


def mix_kernel(odd_ref, zonal_ref, merid_ref, left_ref, right_ref, field_ref, w_ref, mixed_ref, far_ref, near_ref):
    rows = R * WIDE
    merid = merid_ref[...].astype(F32).reshape(LAT * MROWS, 256).astype(BF)
    dims = (R, WIDE, LAT * MROWS)
    r, w, t = iota(dims, 0), iota(dims, 1), iota(dims, 2)
    m = (t * 2731) >> 16
    i = t - m * MROWS
    cell = one_hot((m * MC + (i >> 2) == w) & ((i & 3) == r) & (i < R * MC))
    merid = mm(cell.reshape(rows, LAT * MROWS), merid).astype(BF)
    attended = mm(zonal_ref[...].reshape(rows, 256), w_ref[0:256]) + mm(merid, w_ref[256:512])
    dims = (R, WIDE, ECELLS)
    r, c, t = iota(dims, 0), iota(dims, 1) - E, iota(dims, 2)
    edge = t == (r << 2) + (c & 3)
    left = one_hot(edge & (c >= -4) & (c < 0)).reshape(rows, ECELLS)
    right = one_hot(edge & (c >= W) & (c < W + 4)).reshape(rows, ECELLS)
    halo = mm(left, left_ref[...]) + mm(right, right_ref[...])
    blank = jnp.zeros((R, E, C), F32)
    wide = jnp.concatenate([blank, field_ref[...].astype(F32), blank], axis=1)
    wide = wide + halo.reshape(R, WIDE, C)
    mixed = (wide + attended.reshape(R, WIDE, C)).astype(BF)
    mixed_ref[...] = mixed
    odd = odd_ref[0] == 1

    @pl.when(odd)
    def after_is_far():
        far_ref[...] = mixed[1:4]
        near_ref[...] = mixed[0:3]

    @pl.when(jnp.logical_not(odd))
    def before_is_far():
        far_ref[...] = mixed[0:3]
        near_ref[...] = mixed[1:4]


def conv_part(rows, conv_ref, lanes, r):
    total = None
    for b in range(7):
        column = None
        for a in range(7):
            if r + a in rows:
                term = rows[r + a] * conv_ref[a * 7 + b, lanes][None, :]
                column = term if column is None else column + term
        moved = column[b + 5 : b + 5 + W]
        total = moved if total is None else total + moved
    return total


def own_conv_kernel(
    mixed_ref, conv_ref, w_in_hbm, w_back_hbm, out_ref, w_in_ref, w_back_ref, sems
):
    pairs = ((w_in_hbm, w_in_ref), (w_back_hbm, w_back_ref))
    loads = [pltpu.make_async_copy(a, b, sems.at[i]) for i, (a, b) in enumerate(pairs)]
    for load in loads:
        load.start()
    for lane in range(0, C, 128):
        lanes = slice(lane, lane + 128)
        rows = {3 + i: mixed_ref[i, :, lanes].astype(F32) for i in range(R)}
        for r in range(R):
            out_ref[r * W : (r + 1) * W, lanes] = conv_part(rows, conv_ref, lanes, r)
    for load in loads:
        load.wait()


def block_kernel(
    odd_ref, mixed_ref, own_ref, far_ref, near_ref, conv_ref, w_in_ref, w_back_ref, out_ref, conv_out
):
    odd = odd_ref[0] == 1
    for lane in range(0, C, 128):
        lanes = slice(lane, lane + 128)
        rows = {}
        for i in range(3):
            far, near = far_ref[i, :, lanes].astype(F32), near_ref[i, :, lanes].astype(F32)
            rows[i] = jnp.where(odd, near, far)
            rows[7 + i] = jnp.where(odd, far, near)
        for r in range(R):
            here = (slice(r * W, (r + 1) * W), lanes)
            conv_out[here] = own_ref[here] + conv_part(rows, conv_ref, lanes, r)
    normed = layer_norm(conv_out[...]).astype(BF)
    hidden = mm(normed, w_in_ref[...])
    hidden = 0.5 * hidden * (1.0 + lax.erf(hidden * math.sqrt(0.5)))
    back = mm(hidden.astype(BF), w_back_ref[...])
    own = mixed_ref[...].astype(F32)[:, E : E + W].reshape(CELLS, C)
    out_ref[...] = (own + back).astype(BF).reshape(R, W, C)


def per_device(field, w_qkv, w_out, conv_w, w_in, w_back):
    near_pairs = [(i, i + 1) for i in range(0, LAT, 2)]
    far_pairs = [(i, i + 1) for i in range(1, LAT - 1, 2)]
    near_pairs, far_pairs = (pairs + [(j, i) for i, j in pairs] for pairs in (near_pairs, far_pairs))
    borders = [(y * ZS + ZS - 1, (y + 1) % YS * ZS) for y in range(YS)]
    borders = borders + [(j, i) for i, j in borders]
    along_y = [[y * ZS + z for y in range(YS)] for z in range(ZS)]
    along_z = [[y * ZS + z for z in range(ZS)] for y in range(YS)]
    lon = lax.axis_index("lon").astype(jnp.int32)
    y, z = (lon >> 2).reshape(1), (lon & 3).reshape(1)
    odd = (lax.axis_index("lat").astype(jnp.int32) & 1).reshape(1)
    field, y, z, odd = lax.optimization_barrier((field, y, z, odd))
    row, border = call(
        zonal_project_kernel,
        (shape(R, W, 512), shape(ECELLS, C)),
        200_000_000,
        in_specs=[SMEM, ANY, ANY],
        scratch_shapes=[
            pltpu.VMEM((R, W, C), BF),
            pltpu.VMEM((C, 256), BF),
            pltpu.VMEM((C, 128), BF),
            pltpu.SemaphoreType.DMA((3,)),
        ],
    )(z, in_hbm(field), in_hbm(w_qkv))
    row = lax.all_to_all(row, "lon", 0, 0, axis_index_groups=along_z)
    slots = call(
        spread_kernel,
        shape(YS, KEYS, 128),
        10_000_000,
        out_specs=ANY,
        scratch_shapes=[pltpu.VMEM((KEYS, 128), BF), pltpu.SemaphoreType.DMA((YS,))],
    )(row)
    slots = lax.all_to_all(slots, "lon", 0, 0, axis_index_groups=along_y)
    border = lax.ppermute(border, "lon", borders)
    merid, merid_edges = call(
        merid_own_kernel, (shape(LAT, MROWS, C), shape(2, MROWS, C)), 300_000_000
    )(field)
    merid, field_left, field_right = call(
        merid_edge_kernel,
        (shape(LAT, MROWS, C), shape(ECELLS, C), shape(ECELLS, C)),
        10_000_000,
        in_specs=[SMEM, ANY, VMEM, VMEM, VMEM],
        out_specs=[ANY, VMEM, VMEM],
        input_output_aliases={1: 0},
        scratch_shapes=[pltpu.VMEM((2, MROWS, C), BF), pltpu.SemaphoreType.DMA((2,))],
    )(z, merid, merid_edges, row, border)
    slots, merid = lax.optimization_barrier((slots, merid))
    merid = lax.all_to_all(merid, "lat", 0, 0)
    zonal = call(
        zonal_kernel, shape(ZS, WIDE, 256), 4_000_000_000, vmem=24, in_specs=[SMEM, VMEM, VMEM]
    )(y, row, slots)
    zonal = lax.all_to_all(zonal, "lon", 0, 0, axis_index_groups=along_z)
    merid = call(merid_kernel, shape(LAT, MROWS, 256), 1_000_000_000)(merid, w_qkv)
    merid = lax.all_to_all(merid, "lat", 0, 0)
    mixed, far, near = call(
        mix_kernel,
        (shape(R, WIDE, C), shape(3, WIDE, C), shape(3, WIDE, C)),
        800_000_000,
        in_specs=[SMEM] + [VMEM] * 6,
    )(odd, zonal, merid, field_left, field_right, field, w_out)
    near = lax.ppermute(near, "lat", near_pairs)
    far = lax.ppermute(far, "lat", far_pairs)
    conv_w = conv_w.reshape(49, C)
    own, w_in, w_back = call(
        own_conv_kernel,
        (jax.ShapeDtypeStruct((CELLS, C), F32), shape(*w_in.shape), shape(*w_back.shape)),
        1_000_000_000,
        in_specs=[VMEM, VMEM, ANY, ANY],
        scratch_shapes=[pltpu.SemaphoreType.DMA((2,))],
    )(mixed, conv_w, in_hbm(w_in), in_hbm(w_back))
    return call(
        block_kernel,
        shape(R, W, C),
        2_000_000_000,
        in_specs=[SMEM] + [VMEM] * 7,
        scratch_shapes=[pltpu.VMEM((CELLS, C), F32)],
    )(odd, mixed, own, far, near, conv_w, w_in, w_back)


def solution(mesh):
    return jax.shard_map(
        per_device,
        mesh=mesh,
        in_specs=(P("lat", "lon", None), P(), P(), P(), P(), P()),
        out_specs=P("lat", "lon", None),
        check_vma=False,
    )
```

```python
import math

import jax
import jax.numpy as jnp
from jax import lax
from jax.experimental import pallas as pl
from jax.experimental.pallas import tpu as pltpu
from jax.sharding import PartitionSpec as P

C = 512
HD = 64
LAT = 16
LON = 32
R = 4
W = 64
CELLS = R * W
E = 8
WIDE = W + 2 * E
MC = WIDE // LAT
EDGES = (1, LAT - 2)
HALO = 3
TALL = R + 2 * HALO
BROWS = 56
MROWS = 24
YS = 8
ZS = 4
SPAN = ZS * W
KEYS = SPAN + 2 * E
F32 = jnp.float32
BF = jnp.bfloat16


def iota(shape, dim):
    return lax.broadcasted_iota(jnp.int32, shape, dim)


def one_hot(hit):
    return jnp.where(hit, 1.0, 0.0).astype(BF)


def mm(a, b):
    return jnp.dot(a, b, preferred_element_type=F32)


def mm_nt(a, b):
    return lax.dot_general(a, b, (((1,), (1,)), ((), ())), preferred_element_type=F32)


def layer_norm(values):
    center = values - jnp.mean(values, axis=-1, keepdims=True)
    spread = jnp.mean(center * center, axis=-1, keepdims=True)
    return center * lax.rsqrt(spread + 1e-06)


def shape(*dims):
    return jax.ShapeDtypeStruct(dims, BF)


VMEM = pl.BlockSpec(memory_space=pltpu.VMEM)
ANY = pl.BlockSpec(memory_space=pl.ANY)
SMEM = pl.BlockSpec(memory_space=pltpu.SMEM)


def call(kernel, out_shape, flops, vmem=16, **kw):
    return pl.pallas_call(
        kernel,
        out_shape=out_shape,
        compiler_params=pltpu.CompilerParams(vmem_limit_bytes=vmem * 1024 * 1024),
        cost_estimate=pl.CostEstimate(flops=flops, bytes_accessed=2_000_000, transcendentals=0),
        **kw,
    )


def in_hbm(array):
    return pltpu.with_memory_space_constraint(array, pltpu.HBM)


def by_partner(odd, far, near):
    far, near = far.astype(F32), near.astype(F32)
    return jnp.where(odd, near, far), jnp.where(odd, far, near)


def for_partner(odd_ref, values, far_ref, near_ref):
    odd = odd_ref[0] == 1
    head, tail = values[0:HALO], values[R - HALO : R]

    @pl.when(odd)
    def after_is_far():
        far_ref[...] = tail
        near_ref[...] = head

    @pl.when(jnp.logical_not(odd))
    def before_is_far():
        far_ref[...] = head
        near_ref[...] = tail


def zonal_project_kernel(
    odd_ref, field_hbm, w_hbm, out_ref, first_ref, last_ref, far_ref, near_ref, field_ref, wq_ref, wkv_ref, sems
):
    loads = [
        pltpu.make_async_copy(field_hbm, field_ref, sems.at[0]),
        pltpu.make_async_copy(w_hbm.at[:, 512:640], wkv_ref, sems.at[1]),
        pltpu.make_async_copy(w_hbm.at[:, 0:256], wq_ref, sems.at[2]),
    ]
    for load in loads:
        load.start()
    loads[0].wait()
    field = field_ref[...].astype(F32)
    first_ref[...] = field[:, 0:E].reshape(R * E, C).astype(BF)
    last_ref[...] = field[:, W - E : W].reshape(R * E, C).astype(BF)
    for_partner(odd_ref, field_ref[...], far_ref, near_ref)
    normed = layer_norm(field.reshape(CELLS, C)).astype(BF)
    loads[1].wait()
    out_ref[:, :, 256:384] = mm(normed, wkv_ref[...]).astype(BF).reshape(R, W, 128)
    loads[2].wait()
    out_ref[:, :, 0:256] = mm(normed, wq_ref[...]).astype(BF).reshape(R, W, 256)


def spread_kernel(in_ref, out_hbm, slot_ref, sems):
    slot_ref[0:SPAN, :] = in_ref[:, :, 256:384].reshape(SPAN, 128)
    first = in_ref[0, :, 0:256].astype(F32)[0:E]
    last = in_ref[ZS - 1, :, 0:256].astype(F32)[W - E : W]
    edge = jnp.where(iota((E, 256), 0) < E // 2, first, last)
    slot_ref[SPAN:KEYS, :] = jnp.concatenate([edge[:, 0:128], edge[:, 128:256]], axis=0).astype(BF)
    copies = [pltpu.make_async_copy(slot_ref, out_hbm.at[y], sems.at[y]) for y in range(YS)]
    for copy in copies:
        copy.start()
    for copy in copies:
        copy.wait()


def zonal_kernel(y_ref, own_ref, all_ref, out_ref):
    y = y_ref[0]
    kv = all_ref[:, 0:SPAN, :].reshape(YS * SPAN, 128)
    ones = iota((YS * SPAN, 128), 1) < HD
    kv_one = jnp.where(ones, jnp.ones_like(kv), kv)
    behind = all_ref[lax.rem(y + YS - 1, YS), SPAN:KEYS, :].astype(F32)
    ahead = all_ref[lax.rem(y + 1, YS), SPAN:KEYS, :].astype(F32)
    count = SPAN + 2 * E
    low = iota((count, 128), 1) < HD
    for pair in range(2):
        lanes = slice(pair * 128, pair * 128 + 128)
        rows = slice(pair * E, pair * E + E)
        q = own_ref[:, :, lanes].astype(F32).reshape(SPAN, 128)
        q = jnp.concatenate([behind[rows], q, ahead[rows]], axis=0) * (1.0 / math.sqrt(HD))
        outs = []
        for head in range(2):
            placed = q if head == 0 else pltpu.roll(q, HD, 1)
            placed = jnp.where(low, placed, 0.0).astype(BF)
            score = mm_nt(placed, kv)
            weight = jnp.exp(score - jnp.max(score, axis=-1, keepdims=True)).astype(BF)
            outs.append(mm(weight, kv_one))
        even, odd = outs
        blended = jnp.where(low, pltpu.roll(even, HD, 1), odd)
        mass = jnp.where(low, even, pltpu.roll(odd, HD, 1))
        heads = blended / mass
        for z in range(ZS):
            out_ref[z, :, lanes] = heads[z * W : z * W + WIDE].astype(BF)


def widened(left, own, right):
    left, right = (a.astype(F32).reshape(R, E, a.shape[-1]) for a in (left, right))
    return jnp.concatenate([left, own.astype(F32), right], axis=1)


def merid_own_kernel(field_ref, out_ref, edge_ref):
    normed = layer_norm(field_ref[...].astype(F32).reshape(CELLS, C)).astype(BF)
    dims = (LAT, MROWS, CELLS)
    m, i, u = iota(dims, 0), iota(dims, 1), iota(dims, 2)
    c = m * MC + (i >> 2) - E
    hit = ((i & 3) * W + c == u) & (c >= 0) & (c < W) & (i < R * MC)
    slots = mm(one_hot(hit).reshape(LAT * MROWS, CELLS), normed).reshape(LAT, MROWS, C).astype(BF)
    out_ref[...] = slots
    edge_ref[0] = slots[EDGES[0]]
    edge_ref[1] = slots[EDGES[1]]


def merid_edge_kernel(slots_hbm, edge_ref, left_ref, right_ref, out_hbm, done_ref, sems):
    copies = []
    for n, (m, ref) in enumerate(zip(EDGES, (left_ref, right_ref))):
        normed = layer_norm(ref[...].astype(F32)).astype(BF)
        i, u = iota((MROWS, R * E), 0), iota((MROWS, R * E), 1)
        c = m * MC + (i >> 2) - n * (W + E)
        hit = ((i & 3) * E + c == u) & (c >= 0) & (c < E) & (i < R * MC)
        done_ref[n] = (edge_ref[n].astype(F32) + mm(one_hot(hit), normed)).astype(BF)
        copies.append(pltpu.make_async_copy(done_ref.at[n], out_hbm.at[m], sems.at[n]))
        copies[n].start()
    for copy in copies:
        copy.wait()


def merid_kernel(in_ref, w_ref, out_ref):
    count = LAT * MROWS
    normed = in_ref[...].astype(F32).reshape(count, C).astype(BF)
    queries = mm(normed, w_ref[:, 256:512]).astype(BF)
    keys = mm(normed, w_ref[:, 640:896]).astype(BF)
    values = mm(normed, w_ref[:, 896:1152]).astype(BF)
    row = iota((LAT, MROWS, count), 1).reshape(count, count) >> 2
    key = iota((count, count), 1)
    key = (key - ((key * 2731) >> 16) * MROWS) >> 2
    bias = jnp.where(row == key, 0.0, -1e30)
    dims = (LAT, BROWS, 1)
    j = iota(dims, 1)
    q = (j * 205) >> 10
    tall = iota(dims, 0) * R - HALO + q
    token = (tall >> 2) * MROWS + (j - q * MC) * R + (tall & 3)
    token = jnp.where(j < TALL * MC, token, -1)
    spread = one_hot(token == iota((LAT, BROWS, count), 2)).reshape(LAT * BROWS, count)
    low = iota((count, 128), 1) < HD
    scale = 1.0 / math.sqrt(HD)
    for pair in range(2):
        lanes = slice(pair * 128, pair * 128 + 128)
        q, k, v = queries[:, lanes], keys[:, lanes], values[:, lanes]
        outs = []
        for side in (low, jnp.logical_not(low)):
            score = mm_nt(jnp.where(side, q, jnp.zeros_like(q)), k) * scale + bias
            weight = jnp.exp(score - jnp.max(score, axis=-1, keepdims=True))
            mass = jnp.sum(weight, axis=-1, keepdims=True)
            outs.append(mm(weight.astype(BF), v) / mass)
        both = jnp.where(low, outs[0], outs[1]).astype(BF)
        out_ref[:, :, lanes] = mm(spread, both).reshape(LAT, BROWS, 128).astype(BF)


def zonal_halo_kernel(odd_ref, zonal_ref, left_ref, right_ref, far_ref, near_ref):
    parts = [zonal_ref[...].astype(F32)]
    for ref in (left_ref, right_ref):
        edge = ref[...].astype(F32).reshape(R, E, C)
        parts += [edge[:, :, 0:256], edge[:, :, 256:512]]
    for_partner(odd_ref, jnp.concatenate(parts, axis=1).astype(BF), far_ref, near_ref)


def conv_part(rows, conv_ref, lanes, r):
    total = None
    for b in range(7):
        column = None
        for a in range(7):
            if r + a in rows:
                term = rows[r + a] * conv_ref[a * 7 + b, lanes][None, :]
                column = term if column is None else column + term
        moved = column[b + 5 : b + 5 + W]
        total = moved if total is None else total + moved
    return total


def block_kernel(
    odd_ref, zonal_ref, far_z_ref, near_z_ref, merid_ref, left_ref, right_ref, field_ref, far_f_ref, near_f_ref,
    w_out_ref, conv_ref, w_in_hbm, w_back_hbm, out_ref, mixed_ref, conv_out, w_in_ref, w_back_ref, sems,
):
    pairs = ((w_in_hbm, w_in_ref), (w_back_hbm, w_back_ref))
    loads = [pltpu.make_async_copy(a, b, sems.at[i]) for i, (a, b) in enumerate(pairs)]
    for load in loads:
        load.start()
    odd = odd_ref[0] == 1
    rows = TALL * WIDE
    dims = (TALL, WIDE, 1)
    q, w = iota(dims, 0), iota(dims, 1)
    m = (w * 205) >> 10
    token = m * BROWS + q * MC + w - m * MC
    pick = one_hot(token == iota((TALL, WIDE, LAT * BROWS), 2)).reshape(rows, LAT * BROWS)
    merid = mm(pick, merid_ref[...].reshape(LAT * BROWS, 256)).astype(BF)
    halos = by_partner(odd, far_z_ref[...], near_z_ref[...])
    zonal = [halos[0][:, 0:WIDE], zonal_ref[...].astype(F32), halos[1][:, 0:WIDE]]
    zonal = jnp.concatenate(zonal, axis=0).astype(BF)
    attended = mm(zonal.reshape(rows, 256), w_out_ref[0:256]) + mm(merid, w_out_ref[256:512])
    wide = []
    for halo, rest in zip(halos, by_partner(odd, far_f_ref[...], near_f_ref[...])):
        corner = [halo[:, i : i + E] for i in range(WIDE, WIDE + 4 * E, E)]
        corner = [jnp.concatenate(corner[n : n + 2], axis=2) for n in (0, 2)]
        wide.append(jnp.concatenate([corner[0], rest, corner[1]], axis=1))
    wide.insert(1, widened(left_ref[...], field_ref[...], right_ref[...]))
    wide = jnp.concatenate(wide, axis=0)
    mixed_ref[...] = (wide + attended.reshape(TALL, WIDE, C)).astype(BF).astype(F32)
    for lane in range(0, C, 128):
        lanes = slice(lane, lane + 128)
        window = {i: mixed_ref[i, :, lanes] for i in range(TALL)}
        for r in range(R):
            conv_out[r * W : (r + 1) * W, lanes] = conv_part(window, conv_ref, lanes, r)
    normed = layer_norm(conv_out[...]).astype(BF)
    loads[0].wait()
    hidden = mm(normed, w_in_ref[...])
    hidden = 0.5 * hidden * (1.0 + lax.erf(hidden * math.sqrt(0.5)))
    loads[1].wait()
    back = mm(hidden.astype(BF), w_back_ref[...])
    own = mixed_ref[HALO : HALO + R, E : E + W, :].reshape(CELLS, C)
    out_ref[...] = (own + back).astype(BF).reshape(R, W, C)


def per_device(field, w_qkv, w_out, conv_w, w_in, w_back):
    right = [(i, (i + 1) % LON) for i in range(LON)]
    left = [(j, i) for i, j in right]
    near_pairs = [(i, i + 1) for i in range(0, LAT, 2)]
    far_pairs = [(i, i + 1) for i in range(1, LAT - 1, 2)]
    near_pairs, far_pairs = (pairs + [(j, i) for i, j in pairs] for pairs in (near_pairs, far_pairs))
    along_y = [[y * ZS + z for y in range(YS)] for z in range(ZS)]
    along_z = [[y * ZS + z for z in range(ZS)] for y in range(YS)]
    y = (lax.axis_index("lon").astype(jnp.int32) >> 2).reshape(1)
    odd = (lax.axis_index("lat").astype(jnp.int32) & 1).reshape(1)
    field, y, odd = lax.optimization_barrier((field, y, odd))
    row, first, last, far_f, near_f = call(
        zonal_project_kernel,
        (shape(R, W, 384), shape(R * E, C), shape(R * E, C), shape(HALO, W, C), shape(HALO, W, C)),
        200_000_000,
        in_specs=[SMEM, ANY, ANY],
        scratch_shapes=[
            pltpu.VMEM((R, W, C), BF),
            pltpu.VMEM((C, 256), BF),
            pltpu.VMEM((C, 128), BF),
            pltpu.SemaphoreType.DMA((3,)),
        ],
    )(odd, in_hbm(field), in_hbm(w_qkv))
    row = lax.all_to_all(row, "lon", 0, 0, axis_index_groups=along_z)
    slots = call(
        spread_kernel,
        shape(YS, KEYS, 128),
        10_000_000,
        out_specs=ANY,
        scratch_shapes=[pltpu.VMEM((KEYS, 128), BF), pltpu.SemaphoreType.DMA((YS,))],
    )(row)
    slots = lax.all_to_all(slots, "lon", 0, 0, axis_index_groups=along_y)
    field_left = lax.ppermute(last, "lon", right)
    field_right = lax.ppermute(first, "lon", left)
    merid, merid_edges = call(
        merid_own_kernel, (shape(LAT, MROWS, C), shape(2, MROWS, C)), 300_000_000
    )(field)
    merid = call(
        merid_edge_kernel,
        shape(LAT, MROWS, C),
        10_000_000,
        in_specs=[ANY, VMEM, VMEM, VMEM],
        out_specs=ANY,
        input_output_aliases={0: 0},
        scratch_shapes=[pltpu.VMEM((2, MROWS, C), BF), pltpu.SemaphoreType.DMA((2,))],
    )(merid, merid_edges, field_left, field_right)
    near_f = lax.ppermute(near_f, "lat", near_pairs)
    far_f = lax.ppermute(far_f, "lat", far_pairs)
    slots, merid, far_f, near_f = lax.optimization_barrier((slots, merid, far_f, near_f))
    merid = lax.all_to_all(merid, "lat", 0, 0)
    zonal = call(
        zonal_kernel, shape(ZS, WIDE, 256), 4_000_000_000, vmem=24, in_specs=[SMEM, VMEM, VMEM]
    )(y, row, slots)
    zonal = lax.all_to_all(zonal, "lon", 0, 0, axis_index_groups=along_z)
    merid = call(merid_kernel, shape(LAT, BROWS, 256), 1_000_000_000)(merid, w_qkv)
    merid = lax.all_to_all(merid, "lat", 0, 0)
    far_z, near_z = call(
        zonal_halo_kernel,
        (shape(HALO, WIDE + 4 * E, 256), shape(HALO, WIDE + 4 * E, 256)),
        10_000_000,
        in_specs=[SMEM] + [VMEM] * 3,
    )(odd, zonal, field_left, field_right)
    near_z = lax.ppermute(near_z, "lat", near_pairs)
    far_z = lax.ppermute(far_z, "lat", far_pairs)
    return call(
        block_kernel,
        shape(R, W, C),
        4_000_000_000,
        vmem=24,
        in_specs=[SMEM] + [VMEM] * 11 + [ANY, ANY],
        scratch_shapes=[
            pltpu.VMEM((TALL, WIDE, C), F32),
            pltpu.VMEM((CELLS, C), F32),
            pltpu.VMEM(w_in.shape, BF),
            pltpu.VMEM(w_back.shape, BF),
            pltpu.SemaphoreType.DMA((2,)),
        ],
    )(
        odd, zonal, far_z, near_z, merid, field_left, field_right, field, far_f, near_f,
        w_out, conv_w.reshape(49, C), in_hbm(w_in), in_hbm(w_back),
    )


def solution(mesh):
    return jax.shard_map(
        per_device,
        mesh=mesh,
        in_specs=(P("lat", "lon", None), P(), P(), P(), P(), P()),
        out_specs=P("lat", "lon", None),
        check_vma=False,
    )
```

```python
import math

import jax
import jax.numpy as jnp
from jax import lax
from jax.experimental import pallas as pl
from jax.experimental.pallas import tpu as pltpu
from jax.sharding import PartitionSpec as P

C = 512
HD = 64
LAT = 16
LON = 32
R = 4
W = 64
CELLS = R * W
E = 8
WIDE = W + E
MWIDE = W + 2 * E
MC = MWIDE // LAT
EDGES = (1, LAT - 2)
MROWS = 24
YS = 8
ZS = 4
SPAN = ZS * W
KEYS = SPAN + 2 * E
F32 = jnp.float32
BF = jnp.bfloat16


def iota(shape, dim):
    return lax.broadcasted_iota(jnp.int32, shape, dim)


def one_hot(hit):
    return jnp.where(hit, 1.0, 0.0).astype(BF)


def mm(a, b):
    return jnp.dot(a, b, preferred_element_type=F32)


def mm_nt(a, b):
    return lax.dot_general(a, b, (((1,), (1,)), ((), ())), preferred_element_type=F32)


def layer_norm(values):
    center = values - jnp.mean(values, axis=-1, keepdims=True)
    spread = jnp.mean(center * center, axis=-1, keepdims=True)
    return center * lax.rsqrt(spread + 1e-06)


def shape(*dims):
    return jax.ShapeDtypeStruct(dims, BF)


VMEM = pl.BlockSpec(memory_space=pltpu.VMEM)
ANY = pl.BlockSpec(memory_space=pl.ANY)
SMEM = pl.BlockSpec(memory_space=pltpu.SMEM)


def call(kernel, out_shape, flops, vmem=16, **kw):
    return pl.pallas_call(
        kernel,
        out_shape=out_shape,
        compiler_params=pltpu.CompilerParams(vmem_limit_bytes=vmem * 1024 * 1024),
        cost_estimate=pl.CostEstimate(flops=flops, bytes_accessed=2_000_000, transcendentals=0),
        **kw,
    )


def in_hbm(array):
    return pltpu.with_memory_space_constraint(array, pltpu.HBM)


def zonal_project_kernel(field_hbm, w_hbm, out_ref, first_ref, last_ref, field_ref, wq_ref, wkv_ref, sems):
    loads = [
        pltpu.make_async_copy(field_hbm, field_ref, sems.at[0]),
        pltpu.make_async_copy(w_hbm.at[:, 512:640], wkv_ref, sems.at[1]),
        pltpu.make_async_copy(w_hbm.at[:, 0:256], wq_ref, sems.at[2]),
    ]
    for load in loads:
        load.start()
    loads[0].wait()
    field = field_ref[...].astype(F32)
    first_ref[...] = field[:, 0:E].reshape(R * E, C).astype(BF)
    last_ref[...] = field[:, W - E : W].reshape(R * E, C).astype(BF)
    normed = layer_norm(field.reshape(CELLS, C)).astype(BF)
    loads[1].wait()
    out_ref[:, :, 256:384] = mm(normed, wkv_ref[...]).astype(BF).reshape(R, W, 128)
    loads[2].wait()
    out_ref[:, :, 0:256] = mm(normed, wq_ref[...]).astype(BF).reshape(R, W, 256)


def spread_kernel(in_ref, out_hbm, slot_ref, sems):
    slot_ref[0:SPAN, :] = in_ref[:, :, 256:384].reshape(SPAN, 128)
    first = in_ref[0, :, 0:256].astype(F32)[0:E]
    last = in_ref[ZS - 1, :, 0:256].astype(F32)[W - E : W]
    edge = jnp.where(iota((E, 256), 0) < E // 2, first, last)
    slot_ref[SPAN:KEYS, :] = jnp.concatenate([edge[:, 0:128], edge[:, 128:256]], axis=0).astype(BF)
    copies = [pltpu.make_async_copy(slot_ref, out_hbm.at[y], sems.at[y]) for y in range(YS)]
    for copy in copies:
        copy.start()
    for copy in copies:
        copy.wait()


def zonal_kernel(y_ref, own_ref, all_ref, out_ref):
    y = y_ref[0]
    kv = all_ref[:, 0:SPAN, :].reshape(YS * SPAN, 128)
    ones = iota((YS * SPAN, 128), 1) < HD
    kv_one = jnp.where(ones, jnp.ones_like(kv), kv)
    behind = all_ref[lax.rem(y + YS - 1, YS), SPAN:KEYS, :].astype(F32)
    ahead = all_ref[lax.rem(y + 1, YS), SPAN:KEYS, :].astype(F32)
    count = SPAN + E
    low = iota((count, 128), 1) < HD
    for pair in range(2):
        lanes = slice(pair * 128, pair * 128 + 128)
        before, after = slice(pair * E + E // 2, pair * E + E), slice(pair * E, pair * E + E // 2)
        q = own_ref[:, :, lanes].astype(F32).reshape(SPAN, 128)
        q = jnp.concatenate([behind[before], q, ahead[after]], axis=0) * (1.0 / math.sqrt(HD))
        outs = []
        for head in range(2):
            placed = q if head == 0 else pltpu.roll(q, HD, 1)
            placed = jnp.where(low, placed, 0.0).astype(BF)
            score = mm_nt(placed, kv)
            weight = jnp.exp(score - jnp.max(score, axis=-1, keepdims=True)).astype(BF)
            outs.append(mm(weight, kv_one))
        even, odd = outs
        blended = jnp.where(low, pltpu.roll(even, HD, 1), odd)
        mass = jnp.where(low, even, pltpu.roll(odd, HD, 1))
        heads = blended / mass
        for z in range(ZS):
            out_ref[z, :, lanes] = heads[z * W : z * W + WIDE].astype(BF)


def widened(left, own, right):
    left, right = (a.astype(F32).reshape(R, E, a.shape[-1]) for a in (left, right))
    return jnp.concatenate([left[:, E // 2 :], own.astype(F32), right[:, 0 : E // 2]], axis=1)


def merid_own_kernel(field_ref, out_ref, edge_ref):
    normed = layer_norm(field_ref[...].astype(F32).reshape(CELLS, C)).astype(BF)
    dims = (LAT, MROWS, CELLS)
    m, i, u = iota(dims, 0), iota(dims, 1), iota(dims, 2)
    c = m * MC + (i >> 2) - E
    hit = ((i & 3) * W + c == u) & (c >= 0) & (c < W) & (i < R * MC)
    slots = mm(one_hot(hit).reshape(LAT * MROWS, CELLS), normed).reshape(LAT, MROWS, C).astype(BF)
    out_ref[...] = slots
    edge_ref[0] = slots[EDGES[0]]
    edge_ref[1] = slots[EDGES[1]]


def merid_edge_kernel(slots_hbm, edge_ref, left_ref, right_ref, out_hbm, done_ref, sems):
    copies = []
    for n, (m, ref) in enumerate(zip(EDGES, (left_ref, right_ref))):
        normed = layer_norm(ref[...].astype(F32)).astype(BF)
        i, u = iota((MROWS, R * E), 0), iota((MROWS, R * E), 1)
        c = m * MC + (i >> 2) - n * (W + E)
        hit = ((i & 3) * E + c == u) & (c >= 0) & (c < E) & (i < R * MC)
        done_ref[n] = (edge_ref[n].astype(F32) + mm(one_hot(hit), normed)).astype(BF)
        copies.append(pltpu.make_async_copy(done_ref.at[n], out_hbm.at[m], sems.at[n]))
        copies[n].start()
    for copy in copies:
        copy.wait()


def merid_kernel(in_ref, w_ref, out_ref):
    count = LAT * MROWS
    normed = in_ref[...].astype(F32).reshape(count, C).astype(BF)
    queries = mm(normed, w_ref[:, 256:512]).astype(BF)
    keys = mm(normed, w_ref[:, 640:896]).astype(BF)
    values = mm(normed, w_ref[:, 896:1152]).astype(BF)
    row = iota((LAT, MROWS, count), 1).reshape(count, count) >> 2
    key = iota((count, count), 1)
    key = (key - ((key * 2731) >> 16) * MROWS) >> 2
    bias = jnp.where(row == key, 0.0, -1e30)
    low = iota((count, 128), 1) < HD
    scale = 1.0 / math.sqrt(HD)
    for pair in range(2):
        lanes = slice(pair * 128, pair * 128 + 128)
        q, k, v = queries[:, lanes], keys[:, lanes], values[:, lanes]
        outs = []
        for side in (low, jnp.logical_not(low)):
            score = mm_nt(jnp.where(side, q, jnp.zeros_like(q)), k) * scale + bias
            weight = jnp.exp(score - jnp.max(score, axis=-1, keepdims=True))
            mass = jnp.sum(weight, axis=-1, keepdims=True)
            outs.append(mm(weight.astype(BF), v) / mass)
        both = jnp.where(low, outs[0], outs[1]).reshape(LAT, MROWS, 128)
        out_ref[:, :, lanes] = both.astype(BF)


def mix_kernel(odd_ref, zonal_ref, merid_ref, left_ref, right_ref, field_ref, w_ref, mixed_ref, far_ref, near_ref):
    rows = R * WIDE
    merid = merid_ref[...].astype(F32).reshape(LAT * MROWS, 256).astype(BF)
    dims = (R, WIDE, LAT * MROWS)
    r, w, t = iota(dims, 0), iota(dims, 1) + E // 2, iota(dims, 2)
    m = (t * 2731) >> 16
    i = t - m * MROWS
    cell = one_hot((m * MC + (i >> 2) == w) & ((i & 3) == r) & (i < R * MC))
    merid = mm(cell.reshape(rows, LAT * MROWS), merid).astype(BF)
    attended = mm(zonal_ref[...].reshape(rows, 256), w_ref[0:256]) + mm(merid, w_ref[256:512])
    wide = widened(left_ref[...], field_ref[...], right_ref[...])
    mixed = (wide + attended.reshape(R, WIDE, C)).astype(BF)
    mixed_ref[...] = mixed
    odd = odd_ref[0] == 1

    @pl.when(odd)
    def after_is_far():
        far_ref[...] = mixed[1:4]
        near_ref[...] = mixed[0:3]

    @pl.when(jnp.logical_not(odd))
    def before_is_far():
        far_ref[...] = mixed[0:3]
        near_ref[...] = mixed[1:4]


def conv_part(rows, conv_ref, lanes, r):
    total = None
    for b in range(7):
        column = None
        for a in range(7):
            if r + a in rows:
                term = rows[r + a] * conv_ref[a * 7 + b, lanes][None, :]
                column = term if column is None else column + term
        moved = column[b + 1 : b + 1 + W]
        total = moved if total is None else total + moved
    return total


def own_conv_kernel(
    mixed_ref, conv_ref, w_in_hbm, w_back_hbm, out_ref, w_in_ref, w_back_ref, sems
):
    pairs = ((w_in_hbm, w_in_ref), (w_back_hbm, w_back_ref))
    loads = [pltpu.make_async_copy(a, b, sems.at[i]) for i, (a, b) in enumerate(pairs)]
    for load in loads:
        load.start()
    for lane in range(0, C, 128):
        lanes = slice(lane, lane + 128)
        rows = {3 + i: mixed_ref[i, :, lanes].astype(F32) for i in range(R)}
        for r in range(R):
            out_ref[r * W : (r + 1) * W, lanes] = conv_part(rows, conv_ref, lanes, r)
    for load in loads:
        load.wait()


def block_kernel(
    odd_ref, mixed_ref, own_ref, far_ref, near_ref, conv_ref, w_in_ref, w_back_ref, out_ref, conv_out
):
    odd = odd_ref[0] == 1
    for lane in range(0, C, 128):
        lanes = slice(lane, lane + 128)
        rows = {}
        for i in range(3):
            far, near = far_ref[i, :, lanes].astype(F32), near_ref[i, :, lanes].astype(F32)
            rows[i] = jnp.where(odd, near, far)
            rows[7 + i] = jnp.where(odd, far, near)
        for r in range(R):
            here = (slice(r * W, (r + 1) * W), lanes)
            conv_out[here] = own_ref[here] + conv_part(rows, conv_ref, lanes, r)
    normed = layer_norm(conv_out[...]).astype(BF)
    hidden = mm(normed, w_in_ref[...])
    hidden = 0.5 * hidden * (1.0 + lax.erf(hidden * math.sqrt(0.5)))
    back = mm(hidden.astype(BF), w_back_ref[...])
    own = mixed_ref[...].astype(F32)[:, E // 2 : E // 2 + W].reshape(CELLS, C)
    out_ref[...] = (own + back).astype(BF).reshape(R, W, C)


def per_device(field, w_qkv, w_out, conv_w, w_in, w_back):
    right = [(i, (i + 1) % LON) for i in range(LON)]
    left = [(j, i) for i, j in right]
    near_pairs = [(i, i + 1) for i in range(0, LAT, 2)]
    far_pairs = [(i, i + 1) for i in range(1, LAT - 1, 2)]
    near_pairs, far_pairs = (pairs + [(j, i) for i, j in pairs] for pairs in (near_pairs, far_pairs))
    along_y = [[y * ZS + z for y in range(YS)] for z in range(ZS)]
    along_z = [[y * ZS + z for z in range(ZS)] for y in range(YS)]
    y = (lax.axis_index("lon").astype(jnp.int32) >> 2).reshape(1)
    odd = (lax.axis_index("lat").astype(jnp.int32) & 1).reshape(1)
    field, y, odd = lax.optimization_barrier((field, y, odd))
    row, first, last = call(
        zonal_project_kernel,
        (shape(R, W, 384), shape(R * E, C), shape(R * E, C)),
        200_000_000,
        in_specs=[ANY, ANY],
        scratch_shapes=[
            pltpu.VMEM((R, W, C), BF),
            pltpu.VMEM((C, 256), BF),
            pltpu.VMEM((C, 128), BF),
            pltpu.SemaphoreType.DMA((3,)),
        ],
    )(in_hbm(field), in_hbm(w_qkv))
    row = lax.all_to_all(row, "lon", 0, 0, axis_index_groups=along_z)
    slots = call(
        spread_kernel,
        shape(YS, KEYS, 128),
        10_000_000,
        out_specs=ANY,
        scratch_shapes=[pltpu.VMEM((KEYS, 128), BF), pltpu.SemaphoreType.DMA((YS,))],
    )(row)
    slots = lax.all_to_all(slots, "lon", 0, 0, axis_index_groups=along_y)
    field_left = lax.ppermute(last, "lon", right)
    field_right = lax.ppermute(first, "lon", left)
    merid, merid_edges = call(
        merid_own_kernel, (shape(LAT, MROWS, C), shape(2, MROWS, C)), 300_000_000
    )(field)
    merid = call(
        merid_edge_kernel,
        shape(LAT, MROWS, C),
        10_000_000,
        in_specs=[ANY, VMEM, VMEM, VMEM],
        out_specs=ANY,
        input_output_aliases={0: 0},
        scratch_shapes=[pltpu.VMEM((2, MROWS, C), BF), pltpu.SemaphoreType.DMA((2,))],
    )(merid, merid_edges, field_left, field_right)
    slots, merid = lax.optimization_barrier((slots, merid))
    merid = lax.all_to_all(merid, "lat", 0, 0)
    zonal = call(
        zonal_kernel, shape(ZS, WIDE, 256), 4_000_000_000, vmem=24, in_specs=[SMEM, VMEM, VMEM]
    )(y, row, slots)
    zonal = lax.all_to_all(zonal, "lon", 0, 0, axis_index_groups=along_z)
    merid = call(merid_kernel, shape(LAT, MROWS, 256), 1_000_000_000)(merid, w_qkv)
    merid = lax.all_to_all(merid, "lat", 0, 0)
    mixed, far, near = call(
        mix_kernel,
        (shape(R, WIDE, C), shape(3, WIDE, C), shape(3, WIDE, C)),
        800_000_000,
        in_specs=[SMEM] + [VMEM] * 6,
    )(odd, zonal, merid, field_left, field_right, field, w_out)
    near = lax.ppermute(near, "lat", near_pairs)
    far = lax.ppermute(far, "lat", far_pairs)
    conv_w = conv_w.reshape(49, C)
    own, w_in, w_back = call(
        own_conv_kernel,
        (jax.ShapeDtypeStruct((CELLS, C), F32), shape(*w_in.shape), shape(*w_back.shape)),
        1_000_000_000,
        in_specs=[VMEM, VMEM, ANY, ANY],
        scratch_shapes=[pltpu.SemaphoreType.DMA((2,))],
    )(mixed, conv_w, in_hbm(w_in), in_hbm(w_back))
    return call(
        block_kernel,
        shape(R, W, C),
        2_000_000_000,
        in_specs=[SMEM] + [VMEM] * 7,
        scratch_shapes=[pltpu.VMEM((CELLS, C), F32)],
    )(odd, mixed, own, far, near, conv_w, w_in, w_back)


def solution(mesh):
    return jax.shard_map(
        per_device,
        mesh=mesh,
        in_specs=(P("lat", "lon", None), P(), P(), P(), P(), P()),
        out_specs=P("lat", "lon", None),
        check_vma=False,
    )
```

```python
import math

import jax
import jax.numpy as jnp
from jax import lax
from jax.experimental import pallas as pl
from jax.experimental.pallas import tpu as pltpu
from jax.sharding import PartitionSpec as P

C = 512
HD = 64
LAT = 16
LON = 32
R = 4
W = 64
CELLS = R * W
E = 8
WIDE = W + E
MWIDE = W + 2 * E
MC = MWIDE // LAT
EDGES = (1, LAT - 2)
MCELLS = 16
MLANES = 640
BROWS = 40
YS = 8
ZS = 4
SPAN = ZS * W
KEYS = SPAN + 2 * E
F32 = jnp.float32
BF = jnp.bfloat16


def iota(shape, dim):
    return lax.broadcasted_iota(jnp.int32, shape, dim)


def one_hot(hit):
    return jnp.where(hit, 1.0, 0.0).astype(BF)


def mm(a, b):
    return jnp.dot(a, b, preferred_element_type=F32)


def mm_nt(a, b):
    return lax.dot_general(a, b, (((1,), (1,)), ((), ())), preferred_element_type=F32)


def layer_norm(values):
    center = values - jnp.mean(values, axis=-1, keepdims=True)
    spread = jnp.mean(center * center, axis=-1, keepdims=True)
    return center * lax.rsqrt(spread + 1e-06)


def shape(*dims):
    return jax.ShapeDtypeStruct(dims, BF)


VMEM = pl.BlockSpec(memory_space=pltpu.VMEM)
ANY = pl.BlockSpec(memory_space=pl.ANY)
SMEM = pl.BlockSpec(memory_space=pltpu.SMEM)


def call(kernel, out_shape, flops, vmem=16, **kw):
    return pl.pallas_call(
        kernel,
        out_shape=out_shape,
        compiler_params=pltpu.CompilerParams(vmem_limit_bytes=vmem * 1024 * 1024),
        cost_estimate=pl.CostEstimate(flops=flops, bytes_accessed=2_000_000, transcendentals=0),
        **kw,
    )


def in_hbm(array):
    return pltpu.with_memory_space_constraint(array, pltpu.HBM)


def zonal_project_kernel(field_hbm, w_hbm, out_ref, first_ref, last_ref, field_ref, wq_ref, wkv_ref, sems):
    loads = [
        pltpu.make_async_copy(field_hbm, field_ref, sems.at[0]),
        pltpu.make_async_copy(w_hbm.at[:, 512:640], wkv_ref, sems.at[1]),
        pltpu.make_async_copy(w_hbm.at[:, 0:256], wq_ref, sems.at[2]),
    ]
    for load in loads:
        load.start()
    loads[0].wait()
    field = field_ref[...].astype(F32)
    first_ref[...] = field[:, 0:E].reshape(R * E, C).astype(BF)
    last_ref[...] = field[:, W - E : W].reshape(R * E, C).astype(BF)
    normed = layer_norm(field.reshape(CELLS, C)).astype(BF)
    loads[1].wait()
    out_ref[:, :, 256:384] = mm(normed, wkv_ref[...]).astype(BF).reshape(R, W, 128)
    loads[2].wait()
    out_ref[:, :, 0:256] = mm(normed, wq_ref[...]).astype(BF).reshape(R, W, 256)


def spread_kernel(in_ref, out_hbm, slot_ref, sems):
    slot_ref[0:SPAN, :] = in_ref[:, :, 256:384].reshape(SPAN, 128)
    first = in_ref[0, :, 0:256].astype(F32)[0:E]
    last = in_ref[ZS - 1, :, 0:256].astype(F32)[W - E : W]
    edge = jnp.where(iota((E, 256), 0) < E // 2, first, last)
    slot_ref[SPAN:KEYS, :] = jnp.concatenate([edge[:, 0:128], edge[:, 128:256]], axis=0).astype(BF)
    copies = [pltpu.make_async_copy(slot_ref, out_hbm.at[y], sems.at[y]) for y in range(YS)]
    for copy in copies:
        copy.start()
    for copy in copies:
        copy.wait()


def zonal_kernel(y_ref, own_ref, all_ref, out_ref):
    y = y_ref[0]
    kv = all_ref[:, 0:SPAN, :].reshape(YS * SPAN, 128)
    ones = iota((YS * SPAN, 128), 1) < HD
    kv_one = jnp.where(ones, jnp.ones_like(kv), kv)
    behind = all_ref[lax.rem(y + YS - 1, YS), SPAN:KEYS, :].astype(F32)
    ahead = all_ref[lax.rem(y + 1, YS), SPAN:KEYS, :].astype(F32)
    count = SPAN + E
    low = iota((count, 128), 1) < HD
    for pair in range(2):
        lanes = slice(pair * 128, pair * 128 + 128)
        before, after = slice(pair * E + E // 2, pair * E + E), slice(pair * E, pair * E + E // 2)
        q = own_ref[:, :, lanes].astype(F32).reshape(SPAN, 128)
        q = jnp.concatenate([behind[before], q, ahead[after]], axis=0) * (1.0 / math.sqrt(HD))
        outs = []
        for head in range(2):
            placed = q if head == 0 else pltpu.roll(q, HD, 1)
            placed = jnp.where(low, placed, 0.0).astype(BF)
            score = mm_nt(placed, kv)
            weight = jnp.exp(score - jnp.max(score, axis=-1, keepdims=True)).astype(BF)
            outs.append(mm(weight, kv_one))
        even, odd = outs
        blended = jnp.where(low, pltpu.roll(even, HD, 1), odd)
        mass = jnp.where(low, even, pltpu.roll(odd, HD, 1))
        heads = blended / mass
        for z in range(ZS):
            out_ref[z, :, lanes] = heads[z * W : z * W + WIDE].astype(BF)


def widened(left, own, right):
    left, right = (a.astype(F32).reshape(R, E, a.shape[-1]) for a in (left, right))
    return jnp.concatenate([left[:, E // 2 :], own.astype(F32), right[:, 0 : E // 2]], axis=1)


def merid_slots(normed, first, row_step, width):
    dims = first.shape[:-2] + (MCELLS, normed.shape[0])
    i, u = iota(dims, len(dims) - 2), iota(dims, len(dims) - 1)
    c = first + (i >> 2)
    main = one_hot(((i & 3) * row_step + c == u) & (c >= 0) & (c < width))
    c = first + MC - 1
    last = one_hot(((i & 3) * row_step + c == u) & (c >= 0) & (c < width))
    shape_2d, shape_out = (-1, normed.shape[0]), dims[:-1] + (C,)
    main = mm(main.reshape(shape_2d), normed).reshape(shape_out)
    last = mm(last.reshape(shape_2d), normed).reshape(shape_out)
    block = iota(dims[:-1] + (128,), len(dims) - 2) >> 2
    tail = sum(jnp.where(block == b, last[..., b * 128 : b * 128 + 128], 0.0) for b in range(4))
    return jnp.concatenate([main, tail], axis=-1)


def merid_own_kernel(field_ref, out_ref, edge_ref):
    normed = layer_norm(field_ref[...].astype(F32).reshape(CELLS, C)).astype(BF)
    first = iota((LAT, MCELLS, CELLS), 0) * MC - E
    slots = merid_slots(normed, first, W, W).astype(BF)
    out_ref[...] = slots
    edge_ref[0] = slots[EDGES[0]]
    edge_ref[1] = slots[EDGES[1]]


def merid_edge_kernel(slots_hbm, edge_ref, left_ref, right_ref, out_hbm, done_ref, sems):
    copies = []
    for n, (m, ref) in enumerate(zip(EDGES, (left_ref, right_ref))):
        normed = layer_norm(ref[...].astype(F32)).astype(BF)
        first = jnp.full((MCELLS, R * E), m * MC - n * (W + E), jnp.int32)
        done_ref[n] = (edge_ref[n].astype(F32) + merid_slots(normed, first, E, E)).astype(BF)
        copies.append(pltpu.make_async_copy(done_ref.at[n], out_hbm.at[m], sems.at[n]))
        copies[n].start()
    for copy in copies:
        copy.wait()


def merid_kernel(in_ref, w_ref, out_ref):
    last = in_ref[:, :, C:MLANES].reshape(CELLS, 128)
    t, u = iota((LAT * R, CELLS), 0), iota((LAT * R, CELLS), 1)
    place = ((t >> 2) << 4) + (t & 3)
    last = [mm(one_hot(u == place + b * R), last) for b in range(4)]
    last = jnp.concatenate(last, axis=1).astype(BF)
    normed = jnp.concatenate([in_ref[:, :, 0:C].reshape(CELLS, C), last], axis=0)
    count = CELLS + LAT * R
    queries = mm(normed, w_ref[:, 256:512]).astype(BF)
    keys = mm(normed, w_ref[:, 640:896]).astype(BF)
    values = mm(normed, w_ref[:, 896:1152]).astype(BF)
    t, s = iota((count, count), 0), iota((count, count), 1)
    row = jnp.where(t < CELLS, (t >> 2) & 3, 4)
    key = jnp.where(s < CELLS, (s >> 2) & 3, 4)
    bias = jnp.where(row == key, 0.0, -1e30)
    low = iota((count, 128), 1) < HD
    scale = 1.0 / math.sqrt(HD)
    parts, tail = [], None
    t, u = iota((LAT * 2 * R, LAT * R), 0), iota((LAT * 2 * R, LAT * R), 1)
    same = u == ((t >> 3) << 2) + (t & 3)
    for pair in range(2):
        lanes = slice(pair * 128, pair * 128 + 128)
        q, k, v = queries[:, lanes], keys[:, lanes], values[:, lanes]
        outs = []
        for side in (low, jnp.logical_not(low)):
            score = mm_nt(jnp.where(side, q, jnp.zeros_like(q)), k) * scale + bias
            weight = jnp.exp(score - jnp.max(score, axis=-1, keepdims=True))
            mass = jnp.sum(weight, axis=-1, keepdims=True)
            outs.append(mm(weight.astype(BF), v) / mass)
        both = jnp.where(low, outs[0], outs[1])
        parts.append(both[0:CELLS].reshape(LAT, MCELLS, 128))
        placed = mm(one_hot(same & (((t >> 2) & 1) == pair)), both[CELLS:].astype(BF))
        tail = placed if tail is None else tail + placed
    parts.append(tail.reshape(LAT, 2 * R, 128))
    out_ref[...] = jnp.concatenate(parts, axis=1).astype(BF)


def mix_kernel(odd_ref, zonal_ref, merid_ref, left_ref, right_ref, field_ref, w_ref, mixed_ref, far_ref, near_ref):
    rows = R * WIDE
    x = merid_ref[...].astype(F32)
    pairs = [x[:, p * MCELLS : (p + 1) * MCELLS].reshape(CELLS, 128).astype(BF) for p in range(2)]
    last = x[:, 2 * MCELLS :].reshape(LAT * 2 * R, 128).astype(BF)
    dims = (R, WIDE, 1)
    r, w = iota(dims, 0), iota(dims, 1) + E // 2
    m = (w * 205) >> 10
    cc = w - m * MC
    place = jnp.where(cc < MC - 1, m * MCELLS + cc * R + r, -1)
    place = one_hot(place == iota((R, WIDE, CELLS), 2)).reshape(rows, CELLS)
    attended = mm(zonal_ref[...].reshape(rows, 256), w_ref[0:256])
    for p in range(2):
        place_last = jnp.where(cc == MC - 1, m * 2 * R + p * R + r, -1)
        place_last = one_hot(place_last == iota((R, WIDE, LAT * 2 * R), 2)).reshape(rows, LAT * 2 * R)
        merid = mm(place, pairs[p]) + mm(place_last, last)
        attended = attended + mm(merid.astype(BF), w_ref[256 + p * 128 : 384 + p * 128])
    wide = widened(left_ref[...], field_ref[...], right_ref[...])
    mixed = (wide + attended.reshape(R, WIDE, C)).astype(BF)
    mixed_ref[...] = mixed
    odd = odd_ref[0] == 1

    @pl.when(odd)
    def after_is_far():
        far_ref[...] = mixed[1:4]
        near_ref[...] = mixed[0:3]

    @pl.when(jnp.logical_not(odd))
    def before_is_far():
        far_ref[...] = mixed[0:3]
        near_ref[...] = mixed[1:4]


def conv_part(rows, conv_ref, lanes, r):
    total = None
    for b in range(7):
        column = None
        for a in range(7):
            if r + a in rows:
                term = rows[r + a] * conv_ref[a * 7 + b, lanes][None, :]
                column = term if column is None else column + term
        moved = column[b + 1 : b + 1 + W]
        total = moved if total is None else total + moved
    return total


def own_conv_kernel(
    mixed_ref, conv_ref, w_in_hbm, w_back_hbm, out_ref, w_in_ref, w_back_ref, sems
):
    pairs = ((w_in_hbm, w_in_ref), (w_back_hbm, w_back_ref))
    loads = [pltpu.make_async_copy(a, b, sems.at[i]) for i, (a, b) in enumerate(pairs)]
    for load in loads:
        load.start()
    for lane in range(0, C, 128):
        lanes = slice(lane, lane + 128)
        rows = {3 + i: mixed_ref[i, :, lanes].astype(F32) for i in range(R)}
        for r in range(R):
            out_ref[r * W : (r + 1) * W, lanes] = conv_part(rows, conv_ref, lanes, r)
    for load in loads:
        load.wait()


def block_kernel(
    odd_ref, mixed_ref, own_ref, far_ref, near_ref, conv_ref, w_in_ref, w_back_ref, out_ref, conv_out
):
    odd = odd_ref[0] == 1
    for lane in range(0, C, 128):
        lanes = slice(lane, lane + 128)
        rows = {}
        for i in range(3):
            far, near = far_ref[i, :, lanes].astype(F32), near_ref[i, :, lanes].astype(F32)
            rows[i] = jnp.where(odd, near, far)
            rows[7 + i] = jnp.where(odd, far, near)
        for r in range(R):
            here = (slice(r * W, (r + 1) * W), lanes)
            conv_out[here] = own_ref[here] + conv_part(rows, conv_ref, lanes, r)
    normed = layer_norm(conv_out[...]).astype(BF)
    hidden = mm(normed, w_in_ref[...])
    hidden = 0.5 * hidden * (1.0 + lax.erf(hidden * math.sqrt(0.5)))
    back = mm(hidden.astype(BF), w_back_ref[...])
    own = mixed_ref[...].astype(F32)[:, E // 2 : E // 2 + W].reshape(CELLS, C)
    out_ref[...] = (own + back).astype(BF).reshape(R, W, C)


def per_device(field, w_qkv, w_out, conv_w, w_in, w_back):
    right = [(i, (i + 1) % LON) for i in range(LON)]
    left = [(j, i) for i, j in right]
    near_pairs = [(i, i + 1) for i in range(0, LAT, 2)]
    far_pairs = [(i, i + 1) for i in range(1, LAT - 1, 2)]
    near_pairs, far_pairs = (pairs + [(j, i) for i, j in pairs] for pairs in (near_pairs, far_pairs))
    along_y = [[y * ZS + z for y in range(YS)] for z in range(ZS)]
    along_z = [[y * ZS + z for z in range(ZS)] for y in range(YS)]
    y = (lax.axis_index("lon").astype(jnp.int32) >> 2).reshape(1)
    odd = (lax.axis_index("lat").astype(jnp.int32) & 1).reshape(1)
    field, y, odd = lax.optimization_barrier((field, y, odd))
    row, first, last = call(
        zonal_project_kernel,
        (shape(R, W, 384), shape(R * E, C), shape(R * E, C)),
        200_000_000,
        in_specs=[ANY, ANY],
        scratch_shapes=[
            pltpu.VMEM((R, W, C), BF),
            pltpu.VMEM((C, 256), BF),
            pltpu.VMEM((C, 128), BF),
            pltpu.SemaphoreType.DMA((3,)),
        ],
    )(in_hbm(field), in_hbm(w_qkv))
    row = lax.all_to_all(row, "lon", 0, 0, axis_index_groups=along_z)
    slots = call(
        spread_kernel,
        shape(YS, KEYS, 128),
        10_000_000,
        out_specs=ANY,
        scratch_shapes=[pltpu.VMEM((KEYS, 128), BF), pltpu.SemaphoreType.DMA((YS,))],
    )(row)
    slots = lax.all_to_all(slots, "lon", 0, 0, axis_index_groups=along_y)
    field_left = lax.ppermute(last, "lon", right)
    field_right = lax.ppermute(first, "lon", left)
    merid, merid_edges = call(
        merid_own_kernel, (shape(LAT, MCELLS, MLANES), shape(2, MCELLS, MLANES)), 300_000_000
    )(field)
    merid = call(
        merid_edge_kernel,
        shape(LAT, MCELLS, MLANES),
        10_000_000,
        in_specs=[ANY, VMEM, VMEM, VMEM],
        out_specs=ANY,
        input_output_aliases={0: 0},
        scratch_shapes=[pltpu.VMEM((2, MCELLS, MLANES), BF), pltpu.SemaphoreType.DMA((2,))],
    )(merid, merid_edges, field_left, field_right)
    slots, merid = lax.optimization_barrier((slots, merid))
    merid = lax.all_to_all(merid, "lat", 0, 0)
    zonal = call(
        zonal_kernel, shape(ZS, WIDE, 256), 4_000_000_000, vmem=24, in_specs=[SMEM, VMEM, VMEM]
    )(y, row, slots)
    zonal = lax.all_to_all(zonal, "lon", 0, 0, axis_index_groups=along_z)
    merid = call(merid_kernel, shape(LAT, BROWS, 128), 1_000_000_000)(merid, w_qkv)
    merid = lax.all_to_all(merid, "lat", 0, 0)
    mixed, far, near = call(
        mix_kernel,
        (shape(R, WIDE, C), shape(3, WIDE, C), shape(3, WIDE, C)),
        800_000_000,
        in_specs=[SMEM] + [VMEM] * 6,
    )(odd, zonal, merid, field_left, field_right, field, w_out)
    near = lax.ppermute(near, "lat", near_pairs)
    far = lax.ppermute(far, "lat", far_pairs)
    conv_w = conv_w.reshape(49, C)
    own, w_in, w_back = call(
        own_conv_kernel,
        (jax.ShapeDtypeStruct((CELLS, C), F32), shape(*w_in.shape), shape(*w_back.shape)),
        1_000_000_000,
        in_specs=[VMEM, VMEM, ANY, ANY],
        scratch_shapes=[pltpu.SemaphoreType.DMA((2,))],
    )(mixed, conv_w, in_hbm(w_in), in_hbm(w_back))
    return call(
        block_kernel,
        shape(R, W, C),
        2_000_000_000,
        in_specs=[SMEM] + [VMEM] * 7,
        scratch_shapes=[pltpu.VMEM((CELLS, C), F32)],
    )(odd, mixed, own, far, near, conv_w, w_in, w_back)


def solution(mesh):
    return jax.shard_map(
        per_device,
        mesh=mesh,
        in_specs=(P("lat", "lon", None), P(), P(), P(), P(), P()),
        out_specs=P("lat", "lon", None),
        check_vma=False,
    )
```

```python
import math

import jax
import jax.numpy as jnp
from jax import lax
from jax.experimental import pallas as pl
from jax.experimental.pallas import tpu as pltpu
from jax.sharding import PartitionSpec as P

C = 512
HD = 64
LAT = 16
LON = 32
R = 4
W = 64
CELLS = R * W
E = 8
WIDE = W + E
MWIDE = W + 2 * E
MC = MWIDE // LAT
EDGES = (1, LAT - 2)
MCELLS = 16
MLANES = 640
BROWS = 40
YS = 8
ZS = 4
SPAN = ZS * W
KEYS = SPAN + 2 * E
F32 = jnp.float32
BF = jnp.bfloat16


def iota(shape, dim):
    return lax.broadcasted_iota(jnp.int32, shape, dim)


def one_hot(hit):
    return jnp.where(hit, 1.0, 0.0).astype(BF)


def mm(a, b):
    return jnp.dot(a, b, preferred_element_type=F32)


def mm_nt(a, b):
    return lax.dot_general(a, b, (((1,), (1,)), ((), ())), preferred_element_type=F32)


def layer_norm(values):
    center = values - jnp.mean(values, axis=-1, keepdims=True)
    spread = jnp.mean(center * center, axis=-1, keepdims=True)
    return center * lax.rsqrt(spread + 1e-06)


def shape(*dims):
    return jax.ShapeDtypeStruct(dims, BF)


VMEM = pl.BlockSpec(memory_space=pltpu.VMEM)
ANY = pl.BlockSpec(memory_space=pl.ANY)
SMEM = pl.BlockSpec(memory_space=pltpu.SMEM)


def call(kernel, out_shape, flops, vmem=16, **kw):
    return pl.pallas_call(
        kernel,
        out_shape=out_shape,
        compiler_params=pltpu.CompilerParams(vmem_limit_bytes=vmem * 1024 * 1024),
        cost_estimate=pl.CostEstimate(flops=flops, bytes_accessed=2_000_000, transcendentals=0),
        **kw,
    )


def in_hbm(array):
    return pltpu.with_memory_space_constraint(array, pltpu.HBM)


def zonal_project_kernel(field_hbm, w_hbm, out_ref, first_ref, last_ref, field_ref, wq_ref, wkv_ref, sems):
    loads = [
        pltpu.make_async_copy(field_hbm, field_ref, sems.at[0]),
        pltpu.make_async_copy(w_hbm.at[:, 512:640], wkv_ref, sems.at[1]),
        pltpu.make_async_copy(w_hbm.at[:, 0:256], wq_ref, sems.at[2]),
    ]
    for load in loads:
        load.start()
    loads[0].wait()
    field = field_ref[...].astype(F32)
    first_ref[...] = field[:, 0:E].reshape(R * E, C).astype(BF)
    last_ref[...] = field[:, W - E : W].reshape(R * E, C).astype(BF)
    normed = layer_norm(field.reshape(CELLS, C)).astype(BF)
    loads[1].wait()
    out_ref[:, :, 256:384] = mm(normed, wkv_ref[...]).astype(BF).reshape(R, W, 128)
    loads[2].wait()
    out_ref[:, :, 0:256] = mm(normed, wq_ref[...]).astype(BF).reshape(R, W, 256)


def spread_kernel(in_ref, out_hbm, slot_ref, sems):
    slot_ref[0:SPAN, :] = in_ref[:, :, 256:384].reshape(SPAN, 128)
    first = in_ref[0, :, 0:256].astype(F32)[0:E]
    last = in_ref[ZS - 1, :, 0:256].astype(F32)[W - E : W]
    edge = jnp.where(iota((E, 256), 0) < E // 2, first, last)
    slot_ref[SPAN:KEYS, :] = jnp.concatenate([edge[:, 0:128], edge[:, 128:256]], axis=0).astype(BF)
    copies = [pltpu.make_async_copy(slot_ref, out_hbm.at[y], sems.at[y]) for y in range(YS)]
    for copy in copies:
        copy.start()
    for copy in copies:
        copy.wait()


def zonal_kernel(y_ref, z_ref, own_ref, all_ref, *outs_ref):
    *outs_ref, heads_ref = outs_ref
    y = y_ref[0]
    kv = all_ref[:, 0:SPAN, :].reshape(YS * SPAN, 128)
    ones = iota((YS * SPAN, 128), 1) < HD
    kv_one = jnp.where(ones, jnp.ones_like(kv), kv)
    behind = all_ref[lax.rem(y + YS - 1, YS), SPAN:KEYS, :].astype(F32)
    ahead = all_ref[lax.rem(y + 1, YS), SPAN:KEYS, :].astype(F32)
    count = SPAN + E
    low = iota((count, 128), 1) < HD
    for pair in range(2):
        lanes = slice(pair * 128, pair * 128 + 128)
        before, after = slice(pair * E + E // 2, pair * E + E), slice(pair * E, pair * E + E // 2)
        q = own_ref[:, :, lanes].astype(F32).reshape(SPAN, 128)
        q = jnp.concatenate([behind[before], q, ahead[after]], axis=0) * (1.0 / math.sqrt(HD))
        outs = []
        for head in range(2):
            placed = q if head == 0 else pltpu.roll(q, HD, 1)
            placed = jnp.where(low, placed, 0.0).astype(BF)
            score = mm_nt(placed, kv)
            weight = jnp.exp(score - jnp.max(score, axis=-1, keepdims=True)).astype(BF)
            outs.append(mm(weight, kv_one))
        even, odd = outs
        blended = jnp.where(low, pltpu.roll(even, HD, 1), odd)
        mass = jnp.where(low, even, pltpu.roll(odd, HD, 1))
        heads_ref[:, lanes] = blended / mass
    for k, out_ref in enumerate(outs_ref):
        start = pl.multiple_of((z_ref[0] ^ k) * W, W)
        out_ref[...] = heads_ref[pl.ds(start, WIDE), :].astype(BF)


def widened(left, own, right):
    left, right = (a.astype(F32).reshape(R, E, a.shape[-1]) for a in (left, right))
    return jnp.concatenate([left[:, E // 2 :], own.astype(F32), right[:, 0 : E // 2]], axis=1)


def merid_slots(normed, first, row_step, width):
    dims = first.shape[:-2] + (MCELLS, normed.shape[0])
    i, u = iota(dims, len(dims) - 2), iota(dims, len(dims) - 1)
    c = first + (i >> 2)
    main = one_hot(((i & 3) * row_step + c == u) & (c >= 0) & (c < width))
    c = first + MC - 1
    last = one_hot(((i & 3) * row_step + c == u) & (c >= 0) & (c < width))
    shape_2d, shape_out = (-1, normed.shape[0]), dims[:-1] + (C,)
    main = mm(main.reshape(shape_2d), normed).reshape(shape_out)
    last = mm(last.reshape(shape_2d), normed).reshape(shape_out)
    block = iota(dims[:-1] + (128,), len(dims) - 2) >> 2
    tail = sum(jnp.where(block == b, last[..., b * 128 : b * 128 + 128], 0.0) for b in range(4))
    return jnp.concatenate([main, tail], axis=-1)


def merid_own_kernel(field_ref, out_ref, edge_ref):
    normed = layer_norm(field_ref[...].astype(F32).reshape(CELLS, C)).astype(BF)
    first = iota((LAT, MCELLS, CELLS), 0) * MC - E
    slots = merid_slots(normed, first, W, W).astype(BF)
    out_ref[...] = slots
    edge_ref[0] = slots[EDGES[0]]
    edge_ref[1] = slots[EDGES[1]]


def merid_edge_kernel(slots_hbm, edge_ref, left_ref, right_ref, out_hbm, done_ref, sems):
    copies = []
    for n, (m, ref) in enumerate(zip(EDGES, (left_ref, right_ref))):
        normed = layer_norm(ref[...].astype(F32)).astype(BF)
        first = jnp.full((MCELLS, R * E), m * MC - n * (W + E), jnp.int32)
        done_ref[n] = (edge_ref[n].astype(F32) + merid_slots(normed, first, E, E)).astype(BF)
        copies.append(pltpu.make_async_copy(done_ref.at[n], out_hbm.at[m], sems.at[n]))
        copies[n].start()
    for copy in copies:
        copy.wait()


def merid_kernel(in_ref, w_ref, out_ref):
    last = in_ref[:, :, C:MLANES].reshape(CELLS, 128)
    t, u = iota((LAT * R, CELLS), 0), iota((LAT * R, CELLS), 1)
    place = ((t >> 2) << 4) + (t & 3)
    last = [mm(one_hot(u == place + b * R), last) for b in range(4)]
    last = jnp.concatenate(last, axis=1).astype(BF)
    normed = jnp.concatenate([in_ref[:, :, 0:C].reshape(CELLS, C), last], axis=0)
    count = CELLS + LAT * R
    queries = mm(normed, w_ref[:, 256:512]).astype(BF)
    keys = mm(normed, w_ref[:, 640:896]).astype(BF)
    values = mm(normed, w_ref[:, 896:1152]).astype(BF)
    t, s = iota((count, count), 0), iota((count, count), 1)
    row = jnp.where(t < CELLS, (t >> 2) & 3, 4)
    key = jnp.where(s < CELLS, (s >> 2) & 3, 4)
    bias = jnp.where(row == key, 0.0, -1e30)
    low = iota((count, 128), 1) < HD
    scale = 1.0 / math.sqrt(HD)
    parts, tail = [], None
    t, u = iota((LAT * 2 * R, LAT * R), 0), iota((LAT * 2 * R, LAT * R), 1)
    same = u == ((t >> 3) << 2) + (t & 3)
    for pair in range(2):
        lanes = slice(pair * 128, pair * 128 + 128)
        q, k, v = queries[:, lanes], keys[:, lanes], values[:, lanes]
        outs = []
        for side in (low, jnp.logical_not(low)):
            score = mm_nt(jnp.where(side, q, jnp.zeros_like(q)), k) * scale + bias
            weight = jnp.exp(score - jnp.max(score, axis=-1, keepdims=True))
            mass = jnp.sum(weight, axis=-1, keepdims=True)
            outs.append(mm(weight.astype(BF), v) / mass)
        both = jnp.where(low, outs[0], outs[1])
        parts.append(both[0:CELLS].reshape(LAT, MCELLS, 128))
        placed = mm(one_hot(same & (((t >> 2) & 1) == pair)), both[CELLS:].astype(BF))
        tail = placed if tail is None else tail + placed
    parts.append(tail.reshape(LAT, 2 * R, 128))
    out_ref[...] = jnp.concatenate(parts, axis=1).astype(BF)


def mix_kernel(
    odd_ref, z_ref, z0_ref, z1_ref, z2_ref, z3_ref, merid_ref, left_ref, right_ref, field_ref, w_ref,
    mixed_ref, far_ref, near_ref, zonal_ref,
):
    for k, ref in enumerate((z0_ref, z1_ref, z2_ref, z3_ref)):
        zonal_ref[z_ref[0] ^ k] = ref[...]
    rows = R * WIDE
    x = merid_ref[...].astype(F32)
    pairs = [x[:, p * MCELLS : (p + 1) * MCELLS].reshape(CELLS, 128).astype(BF) for p in range(2)]
    last = x[:, 2 * MCELLS :].reshape(LAT * 2 * R, 128).astype(BF)
    dims = (R, WIDE, 1)
    r, w = iota(dims, 0), iota(dims, 1) + E // 2
    m = (w * 205) >> 10
    cc = w - m * MC
    place = jnp.where(cc < MC - 1, m * MCELLS + cc * R + r, -1)
    place = one_hot(place == iota((R, WIDE, CELLS), 2)).reshape(rows, CELLS)
    attended = mm(zonal_ref[...].reshape(rows, 256), w_ref[0:256])
    for p in range(2):
        place_last = jnp.where(cc == MC - 1, m * 2 * R + p * R + r, -1)
        place_last = one_hot(place_last == iota((R, WIDE, LAT * 2 * R), 2)).reshape(rows, LAT * 2 * R)
        merid = mm(place, pairs[p]) + mm(place_last, last)
        attended = attended + mm(merid.astype(BF), w_ref[256 + p * 128 : 384 + p * 128])
    wide = widened(left_ref[...], field_ref[...], right_ref[...])
    mixed = (wide + attended.reshape(R, WIDE, C)).astype(BF)
    mixed_ref[...] = mixed
    odd = odd_ref[0] == 1

    @pl.when(odd)
    def after_is_far():
        far_ref[...] = mixed[1:4]
        near_ref[...] = mixed[0:3]

    @pl.when(jnp.logical_not(odd))
    def before_is_far():
        far_ref[...] = mixed[0:3]
        near_ref[...] = mixed[1:4]


def conv_part(rows, conv_ref, lanes, r):
    total = None
    for b in range(7):
        column = None
        for a in range(7):
            if r + a in rows:
                term = rows[r + a] * conv_ref[a * 7 + b, lanes][None, :]
                column = term if column is None else column + term
        moved = column[b + 1 : b + 1 + W]
        total = moved if total is None else total + moved
    return total


def own_conv_kernel(
    mixed_ref, conv_ref, w_in_hbm, w_back_hbm, out_ref, w_in_ref, w_back_ref, sems
):
    pairs = ((w_in_hbm, w_in_ref), (w_back_hbm, w_back_ref))
    loads = [pltpu.make_async_copy(a, b, sems.at[i]) for i, (a, b) in enumerate(pairs)]
    for load in loads:
        load.start()
    for lane in range(0, C, 128):
        lanes = slice(lane, lane + 128)
        rows = {3 + i: mixed_ref[i, :, lanes].astype(F32) for i in range(R)}
        for r in range(R):
            out_ref[r * W : (r + 1) * W, lanes] = conv_part(rows, conv_ref, lanes, r)
    for load in loads:
        load.wait()


def block_kernel(
    odd_ref, mixed_ref, own_ref, far_ref, near_ref, conv_ref, w_in_ref, w_back_ref, out_ref, conv_out
):
    odd = odd_ref[0] == 1
    for lane in range(0, C, 128):
        lanes = slice(lane, lane + 128)
        rows = {}
        for i in range(3):
            far, near = far_ref[i, :, lanes].astype(F32), near_ref[i, :, lanes].astype(F32)
            rows[i] = jnp.where(odd, near, far)
            rows[7 + i] = jnp.where(odd, far, near)
        for r in range(R):
            here = (slice(r * W, (r + 1) * W), lanes)
            conv_out[here] = own_ref[here] + conv_part(rows, conv_ref, lanes, r)
    normed = layer_norm(conv_out[...]).astype(BF)
    hidden = mm(normed, w_in_ref[...])
    hidden = 0.5 * hidden * (1.0 + lax.erf(hidden * math.sqrt(0.5)))
    back = mm(hidden.astype(BF), w_back_ref[...])
    own = mixed_ref[...].astype(F32)[:, E // 2 : E // 2 + W].reshape(CELLS, C)
    out_ref[...] = (own + back).astype(BF).reshape(R, W, C)


def per_device(field, w_qkv, w_out, conv_w, w_in, w_back):
    right = [(i, (i + 1) % LON) for i in range(LON)]
    left = [(j, i) for i, j in right]
    near_pairs = [(i, i + 1) for i in range(0, LAT, 2)]
    far_pairs = [(i, i + 1) for i in range(1, LAT - 1, 2)]
    near_pairs, far_pairs = (pairs + [(j, i) for i, j in pairs] for pairs in (near_pairs, far_pairs))
    along_y = [[y * ZS + z for y in range(YS)] for z in range(ZS)]
    along_z = [[y * ZS + z for z in range(ZS)] for y in range(YS)]
    lon = lax.axis_index("lon").astype(jnp.int32)
    y, z = (lon >> 2).reshape(1), (lon & 3).reshape(1)
    odd = (lax.axis_index("lat").astype(jnp.int32) & 1).reshape(1)
    field, y, z, odd = lax.optimization_barrier((field, y, z, odd))
    row, first, last = call(
        zonal_project_kernel,
        (shape(R, W, 384), shape(R * E, C), shape(R * E, C)),
        200_000_000,
        in_specs=[ANY, ANY],
        scratch_shapes=[
            pltpu.VMEM((R, W, C), BF),
            pltpu.VMEM((C, 256), BF),
            pltpu.VMEM((C, 128), BF),
            pltpu.SemaphoreType.DMA((3,)),
        ],
    )(in_hbm(field), in_hbm(w_qkv))
    row = lax.all_to_all(row, "lon", 0, 0, axis_index_groups=along_z)
    slots = call(
        spread_kernel,
        shape(YS, KEYS, 128),
        10_000_000,
        out_specs=ANY,
        scratch_shapes=[pltpu.VMEM((KEYS, 128), BF), pltpu.SemaphoreType.DMA((YS,))],
    )(row)
    slots = lax.all_to_all(slots, "lon", 0, 0, axis_index_groups=along_y)
    field_left = lax.ppermute(last, "lon", right)
    field_right = lax.ppermute(first, "lon", left)
    merid, merid_edges = call(
        merid_own_kernel, (shape(LAT, MCELLS, MLANES), shape(2, MCELLS, MLANES)), 300_000_000
    )(field)
    merid = call(
        merid_edge_kernel,
        shape(LAT, MCELLS, MLANES),
        10_000_000,
        in_specs=[ANY, VMEM, VMEM, VMEM],
        out_specs=ANY,
        input_output_aliases={0: 0},
        scratch_shapes=[pltpu.VMEM((2, MCELLS, MLANES), BF), pltpu.SemaphoreType.DMA((2,))],
    )(merid, merid_edges, field_left, field_right)
    slots, merid = lax.optimization_barrier((slots, merid))
    merid = lax.all_to_all(merid, "lat", 0, 0)
    zonal = call(
        zonal_kernel,
        (shape(WIDE, 256),) * ZS,
        4_000_000_000,
        vmem=24,
        in_specs=[SMEM, SMEM, VMEM, VMEM],
        scratch_shapes=[pltpu.VMEM((SPAN + E, 256), F32)],
    )(y, z, row, slots)
    zonal = list(zonal)
    for k in range(1, ZS):
        zonal[k] = lax.ppermute(zonal[k], "lon", [(i, i ^ k) for i in range(LON)])
    merid = call(merid_kernel, shape(LAT, BROWS, 128), 1_000_000_000)(merid, w_qkv)
    merid, zonal[2] = lax.optimization_barrier((merid, zonal[2]))
    merid = lax.all_to_all(merid, "lat", 0, 0)
    mixed, far, near = call(
        mix_kernel,
        (shape(R, WIDE, C), shape(3, WIDE, C), shape(3, WIDE, C)),
        800_000_000,
        in_specs=[SMEM, SMEM] + [VMEM] * 9,
        scratch_shapes=[pltpu.VMEM((R, WIDE, 256), BF)],
    )(odd, z, *zonal, merid, field_left, field_right, field, w_out)
    near = lax.ppermute(near, "lat", near_pairs)
    far = lax.ppermute(far, "lat", far_pairs)
    conv_w = conv_w.reshape(49, C)
    own, w_in, w_back = call(
        own_conv_kernel,
        (jax.ShapeDtypeStruct((CELLS, C), F32), shape(*w_in.shape), shape(*w_back.shape)),
        1_000_000_000,
        in_specs=[VMEM, VMEM, ANY, ANY],
        scratch_shapes=[pltpu.SemaphoreType.DMA((2,))],
    )(mixed, conv_w, in_hbm(w_in), in_hbm(w_back))
    return call(
        block_kernel,
        shape(R, W, C),
        2_000_000_000,
        in_specs=[SMEM] + [VMEM] * 7,
        scratch_shapes=[pltpu.VMEM((CELLS, C), F32)],
    )(odd, mixed, own, far, near, conv_w, w_in, w_back)


def solution(mesh):
    return jax.shard_map(
        per_device,
        mesh=mesh,
        in_specs=(P("lat", "lon", None), P(), P(), P(), P(), P()),
        out_specs=P("lat", "lon", None),
        check_vma=False,
    )
```

```python
import math

import jax
import jax.numpy as jnp
from jax import lax
from jax.experimental import pallas as pl
from jax.experimental.pallas import tpu as pltpu
from jax.sharding import PartitionSpec as P

C = 512
HD = 64
LAT = 16
LON = 32
R = 4
W = 64
CELLS = R * W
E = 8
WIDE = W + E
MWIDE = W + 2 * E
MC = MWIDE // LAT
EDGES = (1, LAT - 2)
MCELLS = 16
MLANES = 640
BROWS = 40
YS = 8
ZS = 4
SPAN = ZS * W
KEYS = SPAN + 2 * E
F32 = jnp.float32
BF = jnp.bfloat16


def iota(shape, dim):
    return lax.broadcasted_iota(jnp.int32, shape, dim)


def one_hot(hit):
    return jnp.where(hit, 1.0, 0.0).astype(BF)


def mm(a, b):
    return jnp.dot(a, b, preferred_element_type=F32)


def mm_nt(a, b):
    return lax.dot_general(a, b, (((1,), (1,)), ((), ())), preferred_element_type=F32)


def layer_norm(values):
    center = values - jnp.mean(values, axis=-1, keepdims=True)
    spread = jnp.mean(center * center, axis=-1, keepdims=True)
    return center * lax.rsqrt(spread + 1e-06)


def shape(*dims):
    return jax.ShapeDtypeStruct(dims, BF)


VMEM = pl.BlockSpec(memory_space=pltpu.VMEM)
ANY = pl.BlockSpec(memory_space=pl.ANY)
SMEM = pl.BlockSpec(memory_space=pltpu.SMEM)


def call(kernel, out_shape, flops, vmem=16, **kw):
    return pl.pallas_call(
        kernel,
        out_shape=out_shape,
        compiler_params=pltpu.CompilerParams(vmem_limit_bytes=vmem * 1024 * 1024),
        cost_estimate=pl.CostEstimate(flops=flops, bytes_accessed=2_000_000, transcendentals=0),
        **kw,
    )


def in_hbm(array):
    return pltpu.with_memory_space_constraint(array, pltpu.HBM)


def zonal_project_kernel(field_hbm, w_hbm, out_ref, first_ref, last_ref, field_ref, wq_ref, wkv_ref, sems):
    loads = [
        pltpu.make_async_copy(field_hbm, field_ref, sems.at[0]),
        pltpu.make_async_copy(w_hbm.at[:, 512:640], wkv_ref, sems.at[1]),
        pltpu.make_async_copy(w_hbm.at[:, 0:256], wq_ref, sems.at[2]),
    ]
    for load in loads:
        load.start()
    loads[0].wait()
    field = field_ref[...].astype(F32)
    first_ref[...] = field[:, 0:E].reshape(R * E, C).astype(BF)
    last_ref[...] = field[:, W - E : W].reshape(R * E, C).astype(BF)
    normed = layer_norm(field.reshape(CELLS, C)).astype(BF)
    loads[1].wait()
    out_ref[:, :, 256:384] = mm(normed, wkv_ref[...]).astype(BF).reshape(R, W, 128)
    loads[2].wait()
    out_ref[:, :, 0:256] = mm(normed, wq_ref[...]).astype(BF).reshape(R, W, 256)


def spread_kernel(in_ref, out_hbm, slot_ref, sems):
    slot_ref[0:SPAN, :] = in_ref[:, :, 256:384].reshape(SPAN, 128)
    first = in_ref[0, :, 0:256].astype(F32)[0:E]
    last = in_ref[ZS - 1, :, 0:256].astype(F32)[W - E : W]
    edge = jnp.where(iota((E, 256), 0) < E // 2, first, last)
    slot_ref[SPAN:KEYS, :] = jnp.concatenate([edge[:, 0:128], edge[:, 128:256]], axis=0).astype(BF)
    copies = [pltpu.make_async_copy(slot_ref, out_hbm.at[y], sems.at[y]) for y in range(YS)]
    for copy in copies:
        copy.start()
    for copy in copies:
        copy.wait()


def zonal_kernel(y_ref, z_ref, own_ref, all_ref, *outs_ref):
    *outs_ref, heads_ref = outs_ref
    y = y_ref[0]
    kv = all_ref[:, 0:SPAN, :].reshape(YS * SPAN, 128)
    ones = iota((YS * SPAN, 128), 1) < HD
    kv_one = jnp.where(ones, jnp.ones_like(kv), kv)
    behind = all_ref[lax.rem(y + YS - 1, YS), SPAN:KEYS, :].astype(F32)
    ahead = all_ref[lax.rem(y + 1, YS), SPAN:KEYS, :].astype(F32)
    count = SPAN + E
    low = iota((count, 128), 1) < HD
    for pair in range(2):
        lanes = slice(pair * 128, pair * 128 + 128)
        before, after = slice(pair * E + E // 2, pair * E + E), slice(pair * E, pair * E + E // 2)
        q = own_ref[:, :, lanes].astype(F32).reshape(SPAN, 128)
        q = jnp.concatenate([behind[before], q, ahead[after]], axis=0) * (1.0 / math.sqrt(HD))
        outs = []
        for head in range(2):
            placed = q if head == 0 else pltpu.roll(q, HD, 1)
            placed = jnp.where(low, placed, 0.0).astype(BF)
            score = mm_nt(placed, kv)
            weight = jnp.exp(score - jnp.max(score, axis=-1, keepdims=True)).astype(BF)
            outs.append(mm(weight, kv_one))
        even, odd = outs
        blended = jnp.where(low, pltpu.roll(even, HD, 1), odd)
        mass = jnp.where(low, even, pltpu.roll(odd, HD, 1))
        heads_ref[:, lanes] = blended / mass
    for k, out_ref in enumerate(outs_ref):
        start = pl.multiple_of((z_ref[0] ^ k) * W, W)
        out_ref[...] = heads_ref[pl.ds(start, WIDE), :].astype(BF)


def widened(left, own, right):
    left, right = (a.astype(F32).reshape(R, E, a.shape[-1]) for a in (left, right))
    return jnp.concatenate([left[:, E // 2 :], own.astype(F32), right[:, 0 : E // 2]], axis=1)


def merid_slots(normed, first, row_step, width):
    dims = first.shape[:-2] + (MCELLS, normed.shape[0])
    i, u = iota(dims, len(dims) - 2), iota(dims, len(dims) - 1)
    c = first + (i >> 2)
    main = one_hot(((i & 3) * row_step + c == u) & (c >= 0) & (c < width))
    c = first + MC - 1
    last = one_hot(((i & 3) * row_step + c == u) & (c >= 0) & (c < width))
    shape_2d, shape_out = (-1, normed.shape[0]), dims[:-1] + (C,)
    main = mm(main.reshape(shape_2d), normed).reshape(shape_out)
    last = mm(last.reshape(shape_2d), normed).reshape(shape_out)
    block = iota(dims[:-1] + (128,), len(dims) - 2) >> 2
    tail = sum(jnp.where(block == b, last[..., b * 128 : b * 128 + 128], 0.0) for b in range(4))
    return jnp.concatenate([main, tail], axis=-1)


def merid_own_kernel(field_ref, out_ref, edge_ref):
    normed = layer_norm(field_ref[...].astype(F32).reshape(CELLS, C)).astype(BF)
    first = iota((LAT, MCELLS, CELLS), 0) * MC - E
    slots = merid_slots(normed, first, W, W).astype(BF)
    out_ref[...] = slots
    edge_ref[0] = slots[EDGES[0]]
    edge_ref[1] = slots[EDGES[1]]


def merid_edge_kernel(slots_hbm, edge_ref, left_ref, right_ref, out_hbm, done_ref, sems):
    copies = []
    for n, (m, ref) in enumerate(zip(EDGES, (left_ref, right_ref))):
        normed = layer_norm(ref[...].astype(F32)).astype(BF)
        first = jnp.full((MCELLS, R * E), m * MC - n * (W + E), jnp.int32)
        done_ref[n] = (edge_ref[n].astype(F32) + merid_slots(normed, first, E, E)).astype(BF)
        copies.append(pltpu.make_async_copy(done_ref.at[n], out_hbm.at[m], sems.at[n]))
        copies[n].start()
    for copy in copies:
        copy.wait()


def merid_kernel(in_ref, w_ref, out_ref):
    last = in_ref[:, :, C:MLANES].reshape(CELLS, 128)
    t, u = iota((LAT * R, CELLS), 0), iota((LAT * R, CELLS), 1)
    place = ((t >> 2) << 4) + (t & 3)
    last = [mm(one_hot(u == place + b * R), last) for b in range(4)]
    last = jnp.concatenate(last, axis=1).astype(BF)
    normed = jnp.concatenate([in_ref[:, :, 0:C].reshape(CELLS, C), last], axis=0)
    count = CELLS + LAT * R
    queries = mm(normed, w_ref[:, 256:512]).astype(BF)
    keys = mm(normed, w_ref[:, 640:896]).astype(BF)
    values = mm(normed, w_ref[:, 896:1152]).astype(BF)
    t, s = iota((count, count), 0), iota((count, count), 1)
    row = jnp.where(t < CELLS, (t >> 2) & 3, 4)
    key = jnp.where(s < CELLS, (s >> 2) & 3, 4)
    bias = jnp.where(row == key, 0.0, -1e30)
    low = iota((count, 128), 1) < HD
    scale = 1.0 / math.sqrt(HD)
    parts, tail = [], None
    t, u = iota((LAT * 2 * R, LAT * R), 0), iota((LAT * 2 * R, LAT * R), 1)
    same = u == ((t >> 3) << 2) + (t & 3)
    for pair in range(2):
        lanes = slice(pair * 128, pair * 128 + 128)
        q, k, v = queries[:, lanes], keys[:, lanes], values[:, lanes]
        outs = []
        for side in (low, jnp.logical_not(low)):
            score = mm_nt(jnp.where(side, q, jnp.zeros_like(q)), k) * scale + bias
            weight = jnp.exp(score - jnp.max(score, axis=-1, keepdims=True))
            mass = jnp.sum(weight, axis=-1, keepdims=True)
            outs.append(mm(weight.astype(BF), v) / mass)
        both = jnp.where(low, outs[0], outs[1])
        parts.append(both[0:CELLS].reshape(LAT, MCELLS, 128))
        placed = mm(one_hot(same & (((t >> 2) & 1) == pair)), both[CELLS:].astype(BF))
        tail = placed if tail is None else tail + placed
    parts.append(tail.reshape(LAT, 2 * R, 128))
    out_ref[...] = jnp.concatenate(parts, axis=1).astype(BF)


def mix_kernel(
    odd_ref, z_ref, z0_ref, z1_ref, z2_ref, z3_ref, merid_ref, left_ref, right_ref, field_ref, w_ref,
    mixed_ref, far_ref, near_ref, zonal_ref,
):
    for k, ref in enumerate((z0_ref, z1_ref, z2_ref, z3_ref)):
        zonal_ref[z_ref[0] ^ k] = ref[...]
    rows = R * WIDE
    x = merid_ref[...].astype(F32)
    pairs = [x[:, p * MCELLS : (p + 1) * MCELLS].reshape(CELLS, 128).astype(BF) for p in range(2)]
    last = x[:, 2 * MCELLS :].reshape(LAT * 2 * R, 128).astype(BF)
    dims = (R, WIDE, 1)
    r, w = iota(dims, 0), iota(dims, 1) + E // 2
    m = (w * 205) >> 10
    cc = w - m * MC
    place = jnp.where(cc < MC - 1, m * MCELLS + cc * R + r, -1)
    place = one_hot(place == iota((R, WIDE, CELLS), 2)).reshape(rows, CELLS)
    attended = mm(zonal_ref[...].reshape(rows, 256), w_ref[0:256])
    for p in range(2):
        place_last = jnp.where(cc == MC - 1, m * 2 * R + p * R + r, -1)
        place_last = one_hot(place_last == iota((R, WIDE, LAT * 2 * R), 2)).reshape(rows, LAT * 2 * R)
        merid = mm(place, pairs[p]) + mm(place_last, last)
        attended = attended + mm(merid.astype(BF), w_ref[256 + p * 128 : 384 + p * 128])
    wide = widened(left_ref[...], field_ref[...], right_ref[...])
    mixed = (wide + attended.reshape(R, WIDE, C)).astype(BF)
    mixed_ref[...] = mixed
    odd = odd_ref[0] == 1

    @pl.when(odd)
    def after_is_far():
        far_ref[...] = mixed[1:4]
        near_ref[...] = mixed[0:3]

    @pl.when(jnp.logical_not(odd))
    def before_is_far():
        far_ref[...] = mixed[0:3]
        near_ref[...] = mixed[1:4]


def conv_part(rows, conv_ref, lanes, r):
    total = None
    for b in range(7):
        column = None
        for a in range(7):
            if r + a in rows:
                term = rows[r + a] * conv_ref[a * 7 + b, lanes][None, :]
                column = term if column is None else column + term
        moved = column[b + 1 : b + 1 + W]
        total = moved if total is None else total + moved
    return total


def own_conv_kernel(
    mixed_ref, conv_ref, w_in_hbm, w_back_hbm, out_ref, w_in_ref, w_back_ref, sems
):
    pairs = ((w_in_hbm, w_in_ref), (w_back_hbm, w_back_ref))
    loads = [pltpu.make_async_copy(a, b, sems.at[i]) for i, (a, b) in enumerate(pairs)]
    for load in loads:
        load.start()
    for lane in range(0, C, 128):
        lanes = slice(lane, lane + 128)
        rows = {3 + i: mixed_ref[i, :, lanes].astype(F32) for i in range(R)}
        for r in range(R):
            out_ref[r * W : (r + 1) * W, lanes] = conv_part(rows, conv_ref, lanes, r)
    for load in loads:
        load.wait()


def block_kernel(
    odd_ref, mixed_ref, own_ref, far_ref, near_ref, conv_ref, w_in_ref, w_back_ref, out_ref, conv_out
):
    odd = odd_ref[0] == 1
    for lane in range(0, C, 128):
        lanes = slice(lane, lane + 128)
        rows = {}
        for i in range(3):
            far, near = far_ref[i, :, lanes].astype(F32), near_ref[i, :, lanes].astype(F32)
            rows[i] = jnp.where(odd, near, far)
            rows[7 + i] = jnp.where(odd, far, near)
        for r in range(R):
            here = (slice(r * W, (r + 1) * W), lanes)
            conv_out[here] = own_ref[here] + conv_part(rows, conv_ref, lanes, r)
    normed = layer_norm(conv_out[...]).astype(BF)
    hidden = mm(normed, w_in_ref[...])
    hidden = 0.5 * hidden * (1.0 + lax.erf(hidden * math.sqrt(0.5)))
    back = mm(hidden.astype(BF), w_back_ref[...])
    own = mixed_ref[...].astype(F32)[:, E // 2 : E // 2 + W].reshape(CELLS, C)
    out_ref[...] = (own + back).astype(BF).reshape(R, W, C)


def per_device(field, w_qkv, w_out, conv_w, w_in, w_back):
    right = [(i, (i + 1) % LON) for i in range(LON)]
    left = [(j, i) for i, j in right]
    near_pairs = [(i, i + 1) for i in range(0, LAT, 2)]
    far_pairs = [(i, i + 1) for i in range(1, LAT - 1, 2)]
    near_pairs, far_pairs = (pairs + [(j, i) for i, j in pairs] for pairs in (near_pairs, far_pairs))
    along_y = [[y * ZS + z for y in range(YS)] for z in range(ZS)]
    along_z = [[y * ZS + z for z in range(ZS)] for y in range(YS)]
    lon = lax.axis_index("lon").astype(jnp.int32)
    y, z = (lon >> 2).reshape(1), (lon & 3).reshape(1)
    odd = (lax.axis_index("lat").astype(jnp.int32) & 1).reshape(1)
    field, y, z, odd = lax.optimization_barrier((field, y, z, odd))
    row, first, last = call(
        zonal_project_kernel,
        (shape(R, W, 384), shape(R * E, C), shape(R * E, C)),
        200_000_000,
        in_specs=[ANY, ANY],
        scratch_shapes=[
            pltpu.VMEM((R, W, C), BF),
            pltpu.VMEM((C, 256), BF),
            pltpu.VMEM((C, 128), BF),
            pltpu.SemaphoreType.DMA((3,)),
        ],
    )(in_hbm(field), in_hbm(w_qkv))
    row = lax.all_to_all(row, "lon", 0, 0, axis_index_groups=along_z)
    slots = call(
        spread_kernel,
        shape(YS, KEYS, 128),
        10_000_000,
        out_specs=ANY,
        scratch_shapes=[pltpu.VMEM((KEYS, 128), BF), pltpu.SemaphoreType.DMA((YS,))],
    )(row)
    slots = lax.all_to_all(slots, "lon", 0, 0, axis_index_groups=along_y)
    field_left = lax.ppermute(last, "lon", right)
    field_right = lax.ppermute(first, "lon", left)
    merid, merid_edges = call(
        merid_own_kernel, (shape(LAT, MCELLS, MLANES), shape(2, MCELLS, MLANES)), 300_000_000
    )(field)
    merid = call(
        merid_edge_kernel,
        shape(LAT, MCELLS, MLANES),
        10_000_000,
        in_specs=[ANY, VMEM, VMEM, VMEM],
        out_specs=ANY,
        input_output_aliases={0: 0},
        scratch_shapes=[pltpu.VMEM((2, MCELLS, MLANES), BF), pltpu.SemaphoreType.DMA((2,))],
    )(merid, merid_edges, field_left, field_right)
    slots, merid = lax.optimization_barrier((slots, merid))
    merid = lax.all_to_all(merid, "lat", 0, 0)
    zonal = call(
        zonal_kernel,
        (shape(WIDE, 256),) * ZS,
        4_000_000_000,
        vmem=24,
        in_specs=[SMEM, SMEM, VMEM, VMEM],
        scratch_shapes=[pltpu.VMEM((SPAN + E, 256), F32)],
    )(y, z, row, slots)
    zonal = list(zonal)
    for k in range(1, ZS):
        zonal[k] = lax.ppermute(zonal[k], "lon", [(i, i ^ k) for i in range(LON)])
    merid = call(merid_kernel, shape(LAT, BROWS, 128), 1_000_000_000)(merid, w_qkv)
    merid, *zonal = lax.optimization_barrier((merid, *zonal))
    merid = lax.all_to_all(merid, "lat", 0, 0)
    mixed, far, near = call(
        mix_kernel,
        (shape(R, WIDE, C), shape(3, WIDE, C), shape(3, WIDE, C)),
        800_000_000,
        in_specs=[SMEM, SMEM] + [VMEM] * 9,
        scratch_shapes=[pltpu.VMEM((R, WIDE, 256), BF)],
    )(odd, z, *zonal, merid, field_left, field_right, field, w_out)
    near = lax.ppermute(near, "lat", near_pairs)
    far = lax.ppermute(far, "lat", far_pairs)
    conv_w = conv_w.reshape(49, C)
    own, w_in, w_back = call(
        own_conv_kernel,
        (jax.ShapeDtypeStruct((CELLS, C), F32), shape(*w_in.shape), shape(*w_back.shape)),
        1_000_000_000,
        in_specs=[VMEM, VMEM, ANY, ANY],
        scratch_shapes=[pltpu.SemaphoreType.DMA((2,))],
    )(mixed, conv_w, in_hbm(w_in), in_hbm(w_back))
    return call(
        block_kernel,
        shape(R, W, C),
        2_000_000_000,
        in_specs=[SMEM] + [VMEM] * 7,
        scratch_shapes=[pltpu.VMEM((CELLS, C), F32)],
    )(odd, mixed, own, far, near, conv_w, w_in, w_back)


def solution(mesh):
    return jax.shard_map(
        per_device,
        mesh=mesh,
        in_specs=(P("lat", "lon", None), P(), P(), P(), P(), P()),
        out_specs=P("lat", "lon", None),
        check_vma=False,
    )
```

```python
import math

import jax
import jax.numpy as jnp
from jax import lax
from jax.experimental import pallas as pl
from jax.experimental.pallas import tpu as pltpu
from jax.sharding import PartitionSpec as P

C = 512
HD = 64
LAT = 16
LON = 32
R = 4
W = 64
CELLS = R * W
E = 8
WIDE = W + E
MWIDE = W + 2 * E
MC = MWIDE // LAT
EDGES = (1, LAT - 2)
MCELLS = 16
MLANES = 640
BROWS = 40
YS = 8
ZS = 4
SPAN = ZS * W
KEYS = SPAN + 2 * E
F32 = jnp.float32
BF = jnp.bfloat16


def iota(shape, dim):
    return lax.broadcasted_iota(jnp.int32, shape, dim)


def one_hot(hit):
    return jnp.where(hit, 1.0, 0.0).astype(BF)


def mm(a, b):
    return jnp.dot(a, b, preferred_element_type=F32)


def mm_nt(a, b):
    return lax.dot_general(a, b, (((1,), (1,)), ((), ())), preferred_element_type=F32)


def layer_norm(values):
    center = values - jnp.mean(values, axis=-1, keepdims=True)
    spread = jnp.mean(center * center, axis=-1, keepdims=True)
    return center * lax.rsqrt(spread + 1e-06)


def shape(*dims):
    return jax.ShapeDtypeStruct(dims, BF)


VMEM = pl.BlockSpec(memory_space=pltpu.VMEM)
ANY = pl.BlockSpec(memory_space=pl.ANY)
SMEM = pl.BlockSpec(memory_space=pltpu.SMEM)


def call(kernel, out_shape, flops, vmem=16, **kw):
    return pl.pallas_call(
        kernel,
        out_shape=out_shape,
        compiler_params=pltpu.CompilerParams(vmem_limit_bytes=vmem * 1024 * 1024),
        cost_estimate=pl.CostEstimate(flops=flops, bytes_accessed=2_000_000, transcendentals=0),
        **kw,
    )


def in_hbm(array):
    return pltpu.with_memory_space_constraint(array, pltpu.HBM)


def zonal_project_kernel(
    side_ref, field_hbm, w_hbm, out_ref, outer_ref, inner_ref, field_ref, wq_ref, wkv_ref, sems
):
    loads = [
        pltpu.make_async_copy(field_hbm, field_ref, sems.at[0]),
        pltpu.make_async_copy(w_hbm.at[:, 512:640], wkv_ref, sems.at[1]),
        pltpu.make_async_copy(w_hbm.at[:, 0:256], wq_ref, sems.at[2]),
    ]
    for load in loads:
        load.start()
    loads[0].wait()
    field = field_ref[...].astype(F32)
    side = side_ref[0] == 1
    first = field[:, 0:E].reshape(R * E, C)
    last = field[:, W - E : W].reshape(R * E, C)
    outer_ref[...] = jnp.where(side, last, first).astype(BF)
    inner_ref[...] = jnp.where(side, first, last).astype(BF)
    normed = layer_norm(field.reshape(CELLS, C)).astype(BF)
    loads[1].wait()
    out_ref[:, :, 256:384] = mm(normed, wkv_ref[...]).astype(BF).reshape(R, W, 128)
    loads[2].wait()
    out_ref[:, :, 0:256] = mm(normed, wq_ref[...]).astype(BF).reshape(R, W, 256)


def spread_kernel(in_ref, out_hbm, slot_ref, sems):
    slot_ref[0:SPAN, :] = in_ref[:, :, 256:384].reshape(SPAN, 128)
    first = in_ref[0, :, 0:256].astype(F32)[0:E]
    last = in_ref[ZS - 1, :, 0:256].astype(F32)[W - E : W]
    edge = jnp.where(iota((E, 256), 0) < E // 2, first, last)
    slot_ref[SPAN:KEYS, :] = jnp.concatenate([edge[:, 0:128], edge[:, 128:256]], axis=0).astype(BF)
    copies = [pltpu.make_async_copy(slot_ref, out_hbm.at[y], sems.at[y]) for y in range(YS)]
    for copy in copies:
        copy.start()
    for copy in copies:
        copy.wait()


def zonal_kernel(y_ref, own_ref, all_ref, out_ref):
    y = y_ref[0]
    kv = all_ref[:, 0:SPAN, :].reshape(YS * SPAN, 128)
    ones = iota((YS * SPAN, 128), 1) < HD
    kv_one = jnp.where(ones, jnp.ones_like(kv), kv)
    behind = all_ref[lax.rem(y + YS - 1, YS), SPAN:KEYS, :].astype(F32)
    ahead = all_ref[lax.rem(y + 1, YS), SPAN:KEYS, :].astype(F32)
    count = SPAN + E
    low = iota((count, 128), 1) < HD
    for pair in range(2):
        lanes = slice(pair * 128, pair * 128 + 128)
        before, after = slice(pair * E + E // 2, pair * E + E), slice(pair * E, pair * E + E // 2)
        q = own_ref[:, :, lanes].astype(F32).reshape(SPAN, 128)
        q = jnp.concatenate([behind[before], q, ahead[after]], axis=0) * (1.0 / math.sqrt(HD))
        outs = []
        for head in range(2):
            placed = q if head == 0 else pltpu.roll(q, HD, 1)
            placed = jnp.where(low, placed, 0.0).astype(BF)
            score = mm_nt(placed, kv)
            weight = jnp.exp(score - jnp.max(score, axis=-1, keepdims=True)).astype(BF)
            outs.append(mm(weight, kv_one))
        even, odd = outs
        blended = jnp.where(low, pltpu.roll(even, HD, 1), odd)
        mass = jnp.where(low, even, pltpu.roll(odd, HD, 1))
        heads = blended / mass
        for z in range(ZS):
            out_ref[z, :, lanes] = heads[z * W : z * W + WIDE].astype(BF)


def widened(left, own, right):
    left, right = (a.astype(F32).reshape(R, E, a.shape[-1]) for a in (left, right))
    return jnp.concatenate([left[:, E // 2 :], own.astype(F32), right[:, 0 : E // 2]], axis=1)


def merid_slots(normed, first, row_step, width):
    dims = first.shape[:-2] + (MCELLS, normed.shape[0])
    i, u = iota(dims, len(dims) - 2), iota(dims, len(dims) - 1)
    c = first + (i >> 2)
    main = one_hot(((i & 3) * row_step + c == u) & (c >= 0) & (c < width))
    c = first + MC - 1
    last = one_hot(((i & 3) * row_step + c == u) & (c >= 0) & (c < width))
    shape_2d, shape_out = (-1, normed.shape[0]), dims[:-1] + (C,)
    main = mm(main.reshape(shape_2d), normed).reshape(shape_out)
    last = mm(last.reshape(shape_2d), normed).reshape(shape_out)
    block = iota(dims[:-1] + (128,), len(dims) - 2) >> 2
    tail = sum(jnp.where(block == b, last[..., b * 128 : b * 128 + 128], 0.0) for b in range(4))
    return jnp.concatenate([main, tail], axis=-1)


def merid_own_kernel(field_ref, out_ref, edge_ref):
    normed = layer_norm(field_ref[...].astype(F32).reshape(CELLS, C)).astype(BF)
    first = iota((LAT, MCELLS, CELLS), 0) * MC - E
    slots = merid_slots(normed, first, W, W).astype(BF)
    out_ref[...] = slots
    edge_ref[0] = slots[EDGES[0]]
    edge_ref[1] = slots[EDGES[1]]


def merid_edge_kernel(
    side_ref, slots_hbm, edge_ref, outer_ref, inner_ref, out_hbm, left_ref, right_ref, done_ref, sems
):
    side = side_ref[0] == 1
    outer, inner = outer_ref[...].astype(F32), inner_ref[...].astype(F32)
    halos = (jnp.where(side, inner, outer), jnp.where(side, outer, inner))
    copies = []
    for n, (m, ref, halo) in enumerate(zip(EDGES, (left_ref, right_ref), halos)):
        ref[...] = halo.astype(BF)
        normed = layer_norm(halo).astype(BF)
        first = jnp.full((MCELLS, R * E), m * MC - n * (W + E), jnp.int32)
        done_ref[n] = (edge_ref[n].astype(F32) + merid_slots(normed, first, E, E)).astype(BF)
        copies.append(pltpu.make_async_copy(done_ref.at[n], out_hbm.at[m], sems.at[n]))
        copies[n].start()
    for copy in copies:
        copy.wait()


def merid_kernel(in_ref, w_ref, out_ref):
    last = in_ref[:, :, C:MLANES].reshape(CELLS, 128)
    t, u = iota((LAT * R, CELLS), 0), iota((LAT * R, CELLS), 1)
    place = ((t >> 2) << 4) + (t & 3)
    last = [mm(one_hot(u == place + b * R), last) for b in range(4)]
    last = jnp.concatenate(last, axis=1).astype(BF)
    normed = jnp.concatenate([in_ref[:, :, 0:C].reshape(CELLS, C), last], axis=0)
    count = CELLS + LAT * R
    queries = mm(normed, w_ref[:, 256:512]).astype(BF)
    keys = mm(normed, w_ref[:, 640:896]).astype(BF)
    values = mm(normed, w_ref[:, 896:1152]).astype(BF)
    t, s = iota((count, count), 0), iota((count, count), 1)
    row = jnp.where(t < CELLS, (t >> 2) & 3, 4)
    key = jnp.where(s < CELLS, (s >> 2) & 3, 4)
    bias = jnp.where(row == key, 0.0, -1e30)
    low = iota((count, 128), 1) < HD
    scale = 1.0 / math.sqrt(HD)
    parts, tail = [], None
    t, u = iota((LAT * 2 * R, LAT * R), 0), iota((LAT * 2 * R, LAT * R), 1)
    same = u == ((t >> 3) << 2) + (t & 3)
    for pair in range(2):
        lanes = slice(pair * 128, pair * 128 + 128)
        q, k, v = queries[:, lanes], keys[:, lanes], values[:, lanes]
        outs = []
        for side in (low, jnp.logical_not(low)):
            score = mm_nt(jnp.where(side, q, jnp.zeros_like(q)), k) * scale + bias
            weight = jnp.exp(score - jnp.max(score, axis=-1, keepdims=True))
            mass = jnp.sum(weight, axis=-1, keepdims=True)
            outs.append(mm(weight.astype(BF), v) / mass)
        both = jnp.where(low, outs[0], outs[1])
        parts.append(both[0:CELLS].reshape(LAT, MCELLS, 128))
        placed = mm(one_hot(same & (((t >> 2) & 1) == pair)), both[CELLS:].astype(BF))
        tail = placed if tail is None else tail + placed
    parts.append(tail.reshape(LAT, 2 * R, 128))
    out_ref[...] = jnp.concatenate(parts, axis=1).astype(BF)


def mix_kernel(odd_ref, zonal_ref, merid_ref, left_ref, right_ref, field_ref, w_ref, mixed_ref, far_ref, near_ref):
    rows = R * WIDE
    x = merid_ref[...].astype(F32)
    pairs = [x[:, p * MCELLS : (p + 1) * MCELLS].reshape(CELLS, 128).astype(BF) for p in range(2)]
    last = x[:, 2 * MCELLS :].reshape(LAT * 2 * R, 128).astype(BF)
    dims = (R, WIDE, 1)
    r, w = iota(dims, 0), iota(dims, 1) + E // 2
    m = (w * 205) >> 10
    cc = w - m * MC
    place = jnp.where(cc < MC - 1, m * MCELLS + cc * R + r, -1)
    place = one_hot(place == iota((R, WIDE, CELLS), 2)).reshape(rows, CELLS)
    attended = mm(zonal_ref[...].reshape(rows, 256), w_ref[0:256])
    for p in range(2):
        place_last = jnp.where(cc == MC - 1, m * 2 * R + p * R + r, -1)
        place_last = one_hot(place_last == iota((R, WIDE, LAT * 2 * R), 2)).reshape(rows, LAT * 2 * R)
        merid = mm(place, pairs[p]) + mm(place_last, last)
        attended = attended + mm(merid.astype(BF), w_ref[256 + p * 128 : 384 + p * 128])
    wide = widened(left_ref[...], field_ref[...], right_ref[...])
    mixed = (wide + attended.reshape(R, WIDE, C)).astype(BF)
    mixed_ref[...] = mixed
    odd = odd_ref[0] == 1

    @pl.when(odd)
    def after_is_far():
        far_ref[...] = mixed[1:4]
        near_ref[...] = mixed[0:3]

    @pl.when(jnp.logical_not(odd))
    def before_is_far():
        far_ref[...] = mixed[0:3]
        near_ref[...] = mixed[1:4]


def conv_part(rows, conv_ref, lanes, r):
    total = None
    for b in range(7):
        column = None
        for a in range(7):
            if r + a in rows:
                term = rows[r + a] * conv_ref[a * 7 + b, lanes][None, :]
                column = term if column is None else column + term
        moved = column[b + 1 : b + 1 + W]
        total = moved if total is None else total + moved
    return total


def own_conv_kernel(
    mixed_ref, conv_ref, w_in_hbm, w_back_hbm, out_ref, w_in_ref, w_back_ref, sems
):
    pairs = ((w_in_hbm, w_in_ref), (w_back_hbm, w_back_ref))
    loads = [pltpu.make_async_copy(a, b, sems.at[i]) for i, (a, b) in enumerate(pairs)]
    for load in loads:
        load.start()
    for lane in range(0, C, 128):
        lanes = slice(lane, lane + 128)
        rows = {3 + i: mixed_ref[i, :, lanes].astype(F32) for i in range(R)}
        for r in range(R):
            out_ref[r * W : (r + 1) * W, lanes] = conv_part(rows, conv_ref, lanes, r)
    for load in loads:
        load.wait()


def block_kernel(
    odd_ref, mixed_ref, own_ref, far_ref, near_ref, conv_ref, w_in_ref, w_back_ref, out_ref, conv_out
):
    odd = odd_ref[0] == 1
    for lane in range(0, C, 128):
        lanes = slice(lane, lane + 128)
        rows = {}
        for i in range(3):
            far, near = far_ref[i, :, lanes].astype(F32), near_ref[i, :, lanes].astype(F32)
            rows[i] = jnp.where(odd, near, far)
            rows[7 + i] = jnp.where(odd, far, near)
        for r in range(R):
            here = (slice(r * W, (r + 1) * W), lanes)
            conv_out[here] = own_ref[here] + conv_part(rows, conv_ref, lanes, r)
    normed = layer_norm(conv_out[...]).astype(BF)
    hidden = mm(normed, w_in_ref[...])
    hidden = 0.5 * hidden * (1.0 + lax.erf(hidden * math.sqrt(0.5)))
    back = mm(hidden.astype(BF), w_back_ref[...])
    own = mixed_ref[...].astype(F32)[:, E // 2 : E // 2 + W].reshape(CELLS, C)
    out_ref[...] = (own + back).astype(BF).reshape(R, W, C)


def per_device(field, w_qkv, w_out, conv_w, w_in, w_back):
    inner_pairs = [(i, i + 1) for i in range(0, LON, 2)]
    outer_pairs = [(i, (i + 1) % LON) for i in range(1, LON, 2)]
    inner_pairs, outer_pairs = (pairs + [(j, i) for i, j in pairs] for pairs in (inner_pairs, outer_pairs))
    near_pairs = [(i, i + 1) for i in range(0, LAT, 2)]
    far_pairs = [(i, i + 1) for i in range(1, LAT - 1, 2)]
    near_pairs, far_pairs = (pairs + [(j, i) for i, j in pairs] for pairs in (near_pairs, far_pairs))
    along_y = [[y * ZS + z for y in range(YS)] for z in range(ZS)]
    along_z = [[y * ZS + z for z in range(ZS)] for y in range(YS)]
    lon = lax.axis_index("lon").astype(jnp.int32)
    y, side = (lon >> 2).reshape(1), (lon & 1).reshape(1)
    odd = (lax.axis_index("lat").astype(jnp.int32) & 1).reshape(1)
    field, y, side, odd = lax.optimization_barrier((field, y, side, odd))
    row, outer, inner = call(
        zonal_project_kernel,
        (shape(R, W, 384), shape(R * E, C), shape(R * E, C)),
        200_000_000,
        in_specs=[SMEM, ANY, ANY],
        scratch_shapes=[
            pltpu.VMEM((R, W, C), BF),
            pltpu.VMEM((C, 256), BF),
            pltpu.VMEM((C, 128), BF),
            pltpu.SemaphoreType.DMA((3,)),
        ],
    )(side, in_hbm(field), in_hbm(w_qkv))
    row = lax.all_to_all(row, "lon", 0, 0, axis_index_groups=along_z)
    slots = call(
        spread_kernel,
        shape(YS, KEYS, 128),
        10_000_000,
        out_specs=ANY,
        scratch_shapes=[pltpu.VMEM((KEYS, 128), BF), pltpu.SemaphoreType.DMA((YS,))],
    )(row)
    slots = lax.all_to_all(slots, "lon", 0, 0, axis_index_groups=along_y)
    inner = lax.ppermute(inner, "lon", inner_pairs)
    outer = lax.ppermute(outer, "lon", outer_pairs)
    merid, merid_edges = call(
        merid_own_kernel, (shape(LAT, MCELLS, MLANES), shape(2, MCELLS, MLANES)), 300_000_000
    )(field)
    merid, field_left, field_right = call(
        merid_edge_kernel,
        (shape(LAT, MCELLS, MLANES), shape(R * E, C), shape(R * E, C)),
        10_000_000,
        in_specs=[SMEM, ANY, VMEM, VMEM, VMEM],
        out_specs=[ANY, VMEM, VMEM],
        input_output_aliases={1: 0},
        scratch_shapes=[pltpu.VMEM((2, MCELLS, MLANES), BF), pltpu.SemaphoreType.DMA((2,))],
    )(side, merid, merid_edges, outer, inner)
    slots, merid = lax.optimization_barrier((slots, merid))
    merid = lax.all_to_all(merid, "lat", 0, 0)
    zonal = call(
        zonal_kernel, shape(ZS, WIDE, 256), 4_000_000_000, vmem=24, in_specs=[SMEM, VMEM, VMEM]
    )(y, row, slots)
    zonal = lax.all_to_all(zonal, "lon", 0, 0, axis_index_groups=along_z)
    merid = call(merid_kernel, shape(LAT, BROWS, 128), 1_000_000_000)(merid, w_qkv)
    merid = lax.all_to_all(merid, "lat", 0, 0)
    mixed, far, near = call(
        mix_kernel,
        (shape(R, WIDE, C), shape(3, WIDE, C), shape(3, WIDE, C)),
        800_000_000,
        in_specs=[SMEM] + [VMEM] * 6,
    )(odd, zonal, merid, field_left, field_right, field, w_out)
    near = lax.ppermute(near, "lat", near_pairs)
    far = lax.ppermute(far, "lat", far_pairs)
    conv_w = conv_w.reshape(49, C)
    own, w_in, w_back = call(
        own_conv_kernel,
        (jax.ShapeDtypeStruct((CELLS, C), F32), shape(*w_in.shape), shape(*w_back.shape)),
        1_000_000_000,
        in_specs=[VMEM, VMEM, ANY, ANY],
        scratch_shapes=[pltpu.SemaphoreType.DMA((2,))],
    )(mixed, conv_w, in_hbm(w_in), in_hbm(w_back))
    return call(
        block_kernel,
        shape(R, W, C),
        2_000_000_000,
        in_specs=[SMEM] + [VMEM] * 7,
        scratch_shapes=[pltpu.VMEM((CELLS, C), F32)],
    )(odd, mixed, own, far, near, conv_w, w_in, w_back)


def solution(mesh):
    return jax.shard_map(
        per_device,
        mesh=mesh,
        in_specs=(P("lat", "lon", None), P(), P(), P(), P(), P()),
        out_specs=P("lat", "lon", None),
        check_vma=False,
    )
```

```python
import math

import jax
import jax.numpy as jnp
from jax import lax
from jax.experimental import pallas as pl
from jax.experimental.pallas import tpu as pltpu
from jax.sharding import PartitionSpec as P

C = 512
HD = 64
LAT = 16
LON = 32
R = 4
W = 64
CELLS = R * W
E = 8
WIDE = W + E
MWIDE = W + 2 * E
MC = MWIDE // LAT
EDGES = (1, LAT - 2)
MCELLS = 16
MLANES = 640
BROWS = 40
YS = 8
ZS = 4
SPAN = ZS * W
KEYS = SPAN + 2 * E
F32 = jnp.float32
BF = jnp.bfloat16


def iota(shape, dim):
    return lax.broadcasted_iota(jnp.int32, shape, dim)


def one_hot(hit):
    return jnp.where(hit, 1.0, 0.0).astype(BF)


def mm(a, b):
    return jnp.dot(a, b, preferred_element_type=F32)


def mm_nt(a, b):
    return lax.dot_general(a, b, (((1,), (1,)), ((), ())), preferred_element_type=F32)


def layer_norm(values):
    center = values - jnp.mean(values, axis=-1, keepdims=True)
    spread = jnp.mean(center * center, axis=-1, keepdims=True)
    return center * lax.rsqrt(spread + 1e-06)


def shape(*dims):
    return jax.ShapeDtypeStruct(dims, BF)


VMEM = pl.BlockSpec(memory_space=pltpu.VMEM)
ANY = pl.BlockSpec(memory_space=pl.ANY)
SMEM = pl.BlockSpec(memory_space=pltpu.SMEM)


def call(kernel, out_shape, flops, vmem=16, **kw):
    return pl.pallas_call(
        kernel,
        out_shape=out_shape,
        compiler_params=pltpu.CompilerParams(vmem_limit_bytes=vmem * 1024 * 1024),
        cost_estimate=pl.CostEstimate(flops=flops, bytes_accessed=2_000_000, transcendentals=0),
        **kw,
    )


def in_hbm(array):
    return pltpu.with_memory_space_constraint(array, pltpu.HBM)


def zonal_project_kernel(
    side_ref, field_hbm, w_hbm, out_ref, outer_ref, inner_ref, field_ref, wq_ref, wkv_ref, sems
):
    loads = [
        pltpu.make_async_copy(field_hbm, field_ref, sems.at[0]),
        pltpu.make_async_copy(w_hbm.at[:, 512:640], wkv_ref, sems.at[1]),
        pltpu.make_async_copy(w_hbm.at[:, 0:256], wq_ref, sems.at[2]),
    ]
    for load in loads:
        load.start()
    loads[0].wait()
    field = field_ref[...].astype(F32)
    side = side_ref[0] == 1
    first = field[:, 0:E].reshape(R * E, C)
    last = field[:, W - E : W].reshape(R * E, C)
    outer_ref[...] = jnp.where(side, last, first).astype(BF)
    inner_ref[...] = jnp.where(side, first, last).astype(BF)
    normed = layer_norm(field.reshape(CELLS, C)).astype(BF)
    loads[1].wait()
    out_ref[:, :, 256:384] = mm(normed, wkv_ref[...]).astype(BF).reshape(R, W, 128)
    loads[2].wait()
    out_ref[:, :, 0:256] = mm(normed, wq_ref[...]).astype(BF).reshape(R, W, 256)


def spread_kernel(in_ref, out_hbm, slot_ref, sems):
    slot_ref[0:SPAN, :] = in_ref[:, :, 256:384].reshape(SPAN, 128)
    first = in_ref[0, :, 0:256].astype(F32)[0:E]
    last = in_ref[ZS - 1, :, 0:256].astype(F32)[W - E : W]
    edge = jnp.where(iota((E, 256), 0) < E // 2, first, last)
    slot_ref[SPAN:KEYS, :] = jnp.concatenate([edge[:, 0:128], edge[:, 128:256]], axis=0).astype(BF)
    copies = [pltpu.make_async_copy(slot_ref, out_hbm.at[y], sems.at[y]) for y in range(YS)]
    for copy in copies:
        copy.start()
    for copy in copies:
        copy.wait()


def zonal_kernel(y_ref, own_ref, all_ref, out_ref):
    y = y_ref[0]
    kv = all_ref[:, 0:SPAN, :].reshape(YS * SPAN, 128)
    ones = iota((YS * SPAN, 128), 1) < HD
    kv_one = jnp.where(ones, jnp.ones_like(kv), kv)
    behind = all_ref[lax.rem(y + YS - 1, YS), SPAN:KEYS, :].astype(F32)
    ahead = all_ref[lax.rem(y + 1, YS), SPAN:KEYS, :].astype(F32)
    count = SPAN + E
    low = iota((count, 128), 1) < HD
    for pair in range(2):
        lanes = slice(pair * 128, pair * 128 + 128)
        before, after = slice(pair * E + E // 2, pair * E + E), slice(pair * E, pair * E + E // 2)
        q = own_ref[:, :, lanes].astype(F32).reshape(SPAN, 128)
        q = jnp.concatenate([behind[before], q, ahead[after]], axis=0) * (1.0 / math.sqrt(HD))
        outs = []
        for head in range(2):
            placed = q if head == 0 else pltpu.roll(q, HD, 1)
            placed = jnp.where(low, placed, 0.0).astype(BF)
            score = mm_nt(placed, kv)
            weight = jnp.exp(score - jnp.max(score, axis=-1, keepdims=True)).astype(BF)
            outs.append(mm(weight, kv_one))
        even, odd = outs
        blended = jnp.where(low, pltpu.roll(even, HD, 1), odd)
        mass = jnp.where(low, even, pltpu.roll(odd, HD, 1))
        heads = blended / mass
        for z in range(ZS):
            out_ref[z, :, lanes] = heads[z * W : z * W + WIDE].astype(BF)


def widened(left, own, right):
    left, right = (a.astype(F32).reshape(R, E, a.shape[-1]) for a in (left, right))
    return jnp.concatenate([left[:, E // 2 :], own.astype(F32), right[:, 0 : E // 2]], axis=1)


def merid_slots(normed, first, row_step, width):
    dims = first.shape[:-2] + (MCELLS, normed.shape[0])
    i, u = iota(dims, len(dims) - 2), iota(dims, len(dims) - 1)
    c = first + (i >> 2)
    main = one_hot(((i & 3) * row_step + c == u) & (c >= 0) & (c < width))
    c = first + MC - 1
    last = one_hot(((i & 3) * row_step + c == u) & (c >= 0) & (c < width))
    shape_2d, shape_out = (-1, normed.shape[0]), dims[:-1] + (C,)
    main = mm(main.reshape(shape_2d), normed).reshape(shape_out)
    last = mm(last.reshape(shape_2d), normed).reshape(shape_out)
    block = iota(dims[:-1] + (128,), len(dims) - 2) >> 2
    tail = sum(jnp.where(block == b, last[..., b * 128 : b * 128 + 128], 0.0) for b in range(4))
    return jnp.concatenate([main, tail], axis=-1)


def merid_own_kernel(field_ref, out_ref, edge_ref):
    normed = layer_norm(field_ref[...].astype(F32).reshape(CELLS, C)).astype(BF)
    first = iota((LAT, MCELLS, CELLS), 0) * MC - E
    slots = merid_slots(normed, first, W, W).astype(BF)
    out_ref[...] = slots
    edge_ref[0] = slots[EDGES[0]]
    edge_ref[1] = slots[EDGES[1]]


def merid_edge_kernel(
    side_ref, slots_hbm, edge_ref, outer_ref, inner_ref, out_hbm, left_ref, right_ref, done_ref, sems
):
    side = side_ref[0] == 1
    outer, inner = outer_ref[...].astype(F32), inner_ref[...].astype(F32)
    halos = (jnp.where(side, inner, outer), jnp.where(side, outer, inner))
    copies = []
    for n, (m, ref, halo) in enumerate(zip(EDGES, (left_ref, right_ref), halos)):
        ref[...] = halo.astype(BF)
        normed = layer_norm(halo).astype(BF)
        first = jnp.full((MCELLS, R * E), m * MC - n * (W + E), jnp.int32)
        done_ref[n] = (edge_ref[n].astype(F32) + merid_slots(normed, first, E, E)).astype(BF)
        copies.append(pltpu.make_async_copy(done_ref.at[n], out_hbm.at[m], sems.at[n]))
        copies[n].start()
    for copy in copies:
        copy.wait()


def merid_kernel(in_ref, w_ref, out_ref):
    last = in_ref[:, :, C:MLANES].reshape(CELLS, 128)
    t, u = iota((LAT * R, CELLS), 0), iota((LAT * R, CELLS), 1)
    place = ((t >> 2) << 4) + (t & 3)
    last = [mm(one_hot(u == place + b * R), last) for b in range(4)]
    last = jnp.concatenate(last, axis=1).astype(BF)
    normed = jnp.concatenate([in_ref[:, :, 0:C].reshape(CELLS, C), last], axis=0)
    count = CELLS + LAT * R
    queries = mm(normed, w_ref[:, 256:512]).astype(BF)
    keys = mm(normed, w_ref[:, 640:896]).astype(BF)
    values = mm(normed, w_ref[:, 896:1152]).astype(BF)
    t, s = iota((count, count), 0), iota((count, count), 1)
    row = jnp.where(t < CELLS, (t >> 2) & 3, 4)
    key = jnp.where(s < CELLS, (s >> 2) & 3, 4)
    bias = jnp.where(row == key, 0.0, -1e30)
    low = iota((count, 128), 1) < HD
    scale = 1.0 / math.sqrt(HD)
    parts, tail = [], None
    t, u = iota((LAT * 2 * R, LAT * R), 0), iota((LAT * 2 * R, LAT * R), 1)
    same = u == ((t >> 3) << 2) + (t & 3)
    for pair in range(2):
        lanes = slice(pair * 128, pair * 128 + 128)
        q, k, v = queries[:, lanes], keys[:, lanes], values[:, lanes]
        outs = []
        for side in (low, jnp.logical_not(low)):
            score = mm_nt(jnp.where(side, q, jnp.zeros_like(q)), k) * scale + bias
            weight = jnp.exp(score - jnp.max(score, axis=-1, keepdims=True))
            mass = jnp.sum(weight, axis=-1, keepdims=True)
            outs.append(mm(weight.astype(BF), v) / mass)
        both = jnp.where(low, outs[0], outs[1])
        parts.append(both[0:CELLS].reshape(LAT, MCELLS, 128))
        placed = mm(one_hot(same & (((t >> 2) & 1) == pair)), both[CELLS:].astype(BF))
        tail = placed if tail is None else tail + placed
    parts.append(tail.reshape(LAT, 2 * R, 128))
    out_ref[...] = jnp.concatenate(parts, axis=1).astype(BF)


def mix_kernel(odd_ref, zonal_ref, merid_ref, left_ref, right_ref, field_ref, w_ref, mixed_ref, far_ref, near_ref):
    rows = R * WIDE
    x = merid_ref[...].astype(F32)
    pairs = [x[:, p * MCELLS : (p + 1) * MCELLS].reshape(CELLS, 128).astype(BF) for p in range(2)]
    last = x[:, 2 * MCELLS :].reshape(LAT * 2 * R, 128).astype(BF)
    dims = (R, WIDE, 1)
    r, w = iota(dims, 0), iota(dims, 1) + E // 2
    m = (w * 205) >> 10
    cc = w - m * MC
    place = jnp.where(cc < MC - 1, m * MCELLS + cc * R + r, -1)
    place = one_hot(place == iota((R, WIDE, CELLS), 2)).reshape(rows, CELLS)
    attended = mm(zonal_ref[...].reshape(rows, 256), w_ref[0:256])
    for p in range(2):
        place_last = jnp.where(cc == MC - 1, m * 2 * R + p * R + r, -1)
        place_last = one_hot(place_last == iota((R, WIDE, LAT * 2 * R), 2)).reshape(rows, LAT * 2 * R)
        merid = mm(place, pairs[p]) + mm(place_last, last)
        attended = attended + mm(merid.astype(BF), w_ref[256 + p * 128 : 384 + p * 128])
    wide = widened(left_ref[...], field_ref[...], right_ref[...])
    mixed = (wide + attended.reshape(R, WIDE, C)).astype(BF)
    mixed_ref[...] = mixed
    odd = odd_ref[0] == 1

    @pl.when(odd)
    def after_is_far():
        far_ref[...] = mixed[1:4]
        near_ref[...] = mixed[0:3]

    @pl.when(jnp.logical_not(odd))
    def before_is_far():
        far_ref[...] = mixed[0:3]
        near_ref[...] = mixed[1:4]


def conv_part(rows, conv_ref, lanes, r):
    total = None
    for b in range(7):
        column = None
        for a in range(7):
            if r + a in rows:
                term = rows[r + a] * conv_ref[a * 7 + b, lanes][None, :]
                column = term if column is None else column + term
        moved = column[b + 1 : b + 1 + W]
        total = moved if total is None else total + moved
    return total


def own_conv_kernel(
    mixed_ref, conv_ref, w_in_hbm, w_back_hbm, out_ref, w_in_ref, w_back_ref, sems
):
    pairs = ((w_in_hbm, w_in_ref), (w_back_hbm, w_back_ref))
    loads = [pltpu.make_async_copy(a, b, sems.at[i]) for i, (a, b) in enumerate(pairs)]
    for load in loads:
        load.start()
    for lane in range(0, C, 128):
        lanes = slice(lane, lane + 128)
        rows = {3 + i: mixed_ref[i, :, lanes].astype(F32) for i in range(R)}
        for r in range(R):
            out_ref[r * W : (r + 1) * W, lanes] = conv_part(rows, conv_ref, lanes, r)
    for load in loads:
        load.wait()


def block_kernel(
    odd_ref, mixed_ref, own_ref, far_ref, near_ref, conv_ref, w_in_ref, w_back_ref, out_ref, conv_out
):
    odd = odd_ref[0] == 1
    for lane in range(0, C, 128):
        lanes = slice(lane, lane + 128)
        rows = {}
        for i in range(3):
            far, near = far_ref[i, :, lanes].astype(F32), near_ref[i, :, lanes].astype(F32)
            rows[i] = jnp.where(odd, near, far)
            rows[7 + i] = jnp.where(odd, far, near)
        for r in range(R):
            here = (slice(r * W, (r + 1) * W), lanes)
            conv_out[here] = own_ref[here] + conv_part(rows, conv_ref, lanes, r)
    normed = layer_norm(conv_out[...]).astype(BF)
    hidden = mm(normed, w_in_ref[...])
    hidden = 0.5 * hidden * (1.0 + lax.erf(hidden * math.sqrt(0.5)))
    back = mm(hidden.astype(BF), w_back_ref[...])
    own = mixed_ref[...].astype(F32)[:, E // 2 : E // 2 + W].reshape(CELLS, C)
    out_ref[...] = (own + back).astype(BF).reshape(R, W, C)


def per_device(field, w_qkv, w_out, conv_w, w_in, w_back):
    inner_pairs = [(i, i + 1) for i in range(0, LON, 2)]
    outer_pairs = [(i, (i + 1) % LON) for i in range(1, LON, 2)]
    inner_pairs, outer_pairs = (pairs + [(j, i) for i, j in pairs] for pairs in (inner_pairs, outer_pairs))
    near_pairs = [(i, i + 1) for i in range(0, LAT, 2)]
    far_pairs = [(i, i + 1) for i in range(1, LAT - 1, 2)]
    near_pairs, far_pairs = (pairs + [(j, i) for i, j in pairs] for pairs in (near_pairs, far_pairs))
    along_y = [[y * ZS + z for y in range(YS)] for z in range(ZS)]
    along_z = [[y * ZS + z for z in range(ZS)] for y in range(YS)]
    lon = lax.axis_index("lon").astype(jnp.int32)
    y, side = (lon >> 2).reshape(1), (lon & 1).reshape(1)
    odd = (lax.axis_index("lat").astype(jnp.int32) & 1).reshape(1)
    field, y, side, odd = lax.optimization_barrier((field, y, side, odd))
    row, outer, inner = call(
        zonal_project_kernel,
        (shape(R, W, 384), shape(R * E, C), shape(R * E, C)),
        200_000_000,
        in_specs=[SMEM, ANY, ANY],
        scratch_shapes=[
            pltpu.VMEM((R, W, C), BF),
            pltpu.VMEM((C, 256), BF),
            pltpu.VMEM((C, 128), BF),
            pltpu.SemaphoreType.DMA((3,)),
        ],
    )(side, in_hbm(field), in_hbm(w_qkv))
    row = lax.all_to_all(row, "lon", 0, 0, axis_index_groups=along_z)
    outer = lax.ppermute(outer, "lon", outer_pairs)
    row, outer = lax.optimization_barrier((row, outer))
    slots = call(
        spread_kernel,
        shape(YS, KEYS, 128),
        10_000_000,
        out_specs=ANY,
        scratch_shapes=[pltpu.VMEM((KEYS, 128), BF), pltpu.SemaphoreType.DMA((YS,))],
    )(row)
    slots = lax.all_to_all(slots, "lon", 0, 0, axis_index_groups=along_y)
    inner = lax.ppermute(inner, "lon", inner_pairs)
    merid, merid_edges = call(
        merid_own_kernel, (shape(LAT, MCELLS, MLANES), shape(2, MCELLS, MLANES)), 300_000_000
    )(field)
    merid, field_left, field_right = call(
        merid_edge_kernel,
        (shape(LAT, MCELLS, MLANES), shape(R * E, C), shape(R * E, C)),
        10_000_000,
        in_specs=[SMEM, ANY, VMEM, VMEM, VMEM],
        out_specs=[ANY, VMEM, VMEM],
        input_output_aliases={1: 0},
        scratch_shapes=[pltpu.VMEM((2, MCELLS, MLANES), BF), pltpu.SemaphoreType.DMA((2,))],
    )(side, merid, merid_edges, outer, inner)
    slots, merid = lax.optimization_barrier((slots, merid))
    merid = lax.all_to_all(merid, "lat", 0, 0)
    zonal = call(
        zonal_kernel, shape(ZS, WIDE, 256), 4_000_000_000, vmem=24, in_specs=[SMEM, VMEM, VMEM]
    )(y, row, slots)
    zonal = lax.all_to_all(zonal, "lon", 0, 0, axis_index_groups=along_z)
    merid = call(merid_kernel, shape(LAT, BROWS, 128), 1_000_000_000)(merid, w_qkv)
    merid = lax.all_to_all(merid, "lat", 0, 0)
    mixed, far, near = call(
        mix_kernel,
        (shape(R, WIDE, C), shape(3, WIDE, C), shape(3, WIDE, C)),
        800_000_000,
        in_specs=[SMEM] + [VMEM] * 6,
    )(odd, zonal, merid, field_left, field_right, field, w_out)
    near = lax.ppermute(near, "lat", near_pairs)
    far = lax.ppermute(far, "lat", far_pairs)
    conv_w = conv_w.reshape(49, C)
    own, w_in, w_back = call(
        own_conv_kernel,
        (jax.ShapeDtypeStruct((CELLS, C), F32), shape(*w_in.shape), shape(*w_back.shape)),
        1_000_000_000,
        in_specs=[VMEM, VMEM, ANY, ANY],
        scratch_shapes=[pltpu.SemaphoreType.DMA((2,))],
    )(mixed, conv_w, in_hbm(w_in), in_hbm(w_back))
    return call(
        block_kernel,
        shape(R, W, C),
        2_000_000_000,
        in_specs=[SMEM] + [VMEM] * 7,
        scratch_shapes=[pltpu.VMEM((CELLS, C), F32)],
    )(odd, mixed, own, far, near, conv_w, w_in, w_back)


def solution(mesh):
    return jax.shard_map(
        per_device,
        mesh=mesh,
        in_specs=(P("lat", "lon", None), P(), P(), P(), P(), P()),
        out_specs=P("lat", "lon", None),
        check_vma=False,
    )
```

```python
import math

import jax
import jax.numpy as jnp
from jax import lax
from jax.experimental import pallas as pl
from jax.experimental.pallas import tpu as pltpu
from jax.sharding import PartitionSpec as P

C = 512
HD = 64
LAT = 16
LON = 32
R = 4
W = 64
CELLS = R * W
E = 8
WIDE = W + E
MWIDE = W + 2 * E
MC = MWIDE // LAT
EDGES = (1, LAT - 2)
MCELLS = 16
MLANES = 640
BROWS = 40
YS = 8
ZS = 4
SPAN = ZS * W
KEYS = SPAN + 2 * E
F32 = jnp.float32
BF = jnp.bfloat16


def iota(shape, dim):
    return lax.broadcasted_iota(jnp.int32, shape, dim)


def one_hot(hit):
    return jnp.where(hit, 1.0, 0.0).astype(BF)


def mm(a, b):
    return jnp.dot(a, b, preferred_element_type=F32)


def mm_nt(a, b):
    return lax.dot_general(a, b, (((1,), (1,)), ((), ())), preferred_element_type=F32)


def layer_norm(values):
    center = values - jnp.mean(values, axis=-1, keepdims=True)
    spread = jnp.mean(center * center, axis=-1, keepdims=True)
    return center * lax.rsqrt(spread + 1e-06)


def shape(*dims):
    return jax.ShapeDtypeStruct(dims, BF)


VMEM = pl.BlockSpec(memory_space=pltpu.VMEM)
ANY = pl.BlockSpec(memory_space=pl.ANY)
SMEM = pl.BlockSpec(memory_space=pltpu.SMEM)


def call(kernel, out_shape, flops, vmem=16, **kw):
    return pl.pallas_call(
        kernel,
        out_shape=out_shape,
        compiler_params=pltpu.CompilerParams(vmem_limit_bytes=vmem * 1024 * 1024),
        cost_estimate=pl.CostEstimate(flops=flops, bytes_accessed=2_000_000, transcendentals=0),
        **kw,
    )


def in_hbm(array):
    return pltpu.with_memory_space_constraint(array, pltpu.HBM)


def zonal_project_kernel(
    side_ref, field_hbm, w_hbm, out_ref, outer_ref, inner_ref, field_ref, wq_ref, wkv_ref, sems
):
    loads = [
        pltpu.make_async_copy(field_hbm, field_ref, sems.at[0]),
        pltpu.make_async_copy(w_hbm.at[:, 512:640], wkv_ref, sems.at[1]),
        pltpu.make_async_copy(w_hbm.at[:, 0:256], wq_ref, sems.at[2]),
    ]
    for load in loads:
        load.start()
    loads[0].wait()
    field = field_ref[...].astype(F32)
    side = side_ref[0] == 1
    first = field[:, 0:E].reshape(R * E, C)
    last = field[:, W - E : W].reshape(R * E, C)
    outer_ref[...] = jnp.where(side, last, first).astype(BF)
    inner_ref[...] = jnp.where(side, first, last).astype(BF)
    normed = layer_norm(field.reshape(CELLS, C)).astype(BF)
    loads[1].wait()
    out_ref[:, :, 256:384] = mm(normed, wkv_ref[...]).astype(BF).reshape(R, W, 128)
    loads[2].wait()
    out_ref[:, :, 0:256] = mm(normed, wq_ref[...]).astype(BF).reshape(R, W, 256)


def spread_kernel(in_ref, out_hbm, slot_ref, sems):
    slot_ref[0:SPAN, :] = in_ref[:, :, 256:384].reshape(SPAN, 128)
    first = in_ref[0, :, 0:256].astype(F32)[0:E]
    last = in_ref[ZS - 1, :, 0:256].astype(F32)[W - E : W]
    edge = jnp.where(iota((E, 256), 0) < E // 2, first, last)
    slot_ref[SPAN:KEYS, :] = jnp.concatenate([edge[:, 0:128], edge[:, 128:256]], axis=0).astype(BF)
    copies = [pltpu.make_async_copy(slot_ref, out_hbm.at[y], sems.at[y]) for y in range(YS)]
    for copy in copies:
        copy.start()
    for copy in copies:
        copy.wait()


def zonal_kernel(y_ref, own_ref, all_ref, out_ref):
    y = y_ref[0]
    kv = all_ref[:, 0:SPAN, :].reshape(YS * SPAN, 128)
    ones = iota((YS * SPAN, 128), 1) < HD
    kv_one = jnp.where(ones, jnp.ones_like(kv), kv)
    behind = all_ref[lax.rem(y + YS - 1, YS), SPAN:KEYS, :].astype(F32)
    ahead = all_ref[lax.rem(y + 1, YS), SPAN:KEYS, :].astype(F32)
    count = SPAN + E
    low = iota((count, 128), 1) < HD
    for pair in range(2):
        lanes = slice(pair * 128, pair * 128 + 128)
        before, after = slice(pair * E + E // 2, pair * E + E), slice(pair * E, pair * E + E // 2)
        q = own_ref[:, :, lanes].astype(F32).reshape(SPAN, 128)
        q = jnp.concatenate([behind[before], q, ahead[after]], axis=0) * (1.0 / math.sqrt(HD))
        outs = []
        for head in range(2):
            placed = q if head == 0 else pltpu.roll(q, HD, 1)
            placed = jnp.where(low, placed, 0.0).astype(BF)
            score = mm_nt(placed, kv)
            weight = jnp.exp(score - jnp.max(score, axis=-1, keepdims=True)).astype(BF)
            outs.append(mm(weight, kv_one))
        even, odd = outs
        blended = jnp.where(low, pltpu.roll(even, HD, 1), odd)
        mass = jnp.where(low, even, pltpu.roll(odd, HD, 1))
        heads = blended / mass
        for z in range(ZS):
            out_ref[z, :, lanes] = heads[z * W : z * W + WIDE].astype(BF)


def widened(left, own, right):
    left, right = (a.astype(F32).reshape(R, E, a.shape[-1]) for a in (left, right))
    return jnp.concatenate([left[:, E // 2 :], own.astype(F32), right[:, 0 : E // 2]], axis=1)


def merid_slots(normed, first, row_step, width):
    dims = first.shape[:-2] + (MCELLS, normed.shape[0])
    i, u = iota(dims, len(dims) - 2), iota(dims, len(dims) - 1)
    c = first + (i >> 2)
    main = one_hot(((i & 3) * row_step + c == u) & (c >= 0) & (c < width))
    c = first + MC - 1
    last = one_hot(((i & 3) * row_step + c == u) & (c >= 0) & (c < width))
    shape_2d, shape_out = (-1, normed.shape[0]), dims[:-1] + (C,)
    main = mm(main.reshape(shape_2d), normed).reshape(shape_out)
    last = mm(last.reshape(shape_2d), normed).reshape(shape_out)
    block = iota(dims[:-1] + (128,), len(dims) - 2) >> 2
    tail = sum(jnp.where(block == b, last[..., b * 128 : b * 128 + 128], 0.0) for b in range(4))
    return jnp.concatenate([main, tail], axis=-1)


def merid_own_kernel(field_ref, out_ref, edge_ref):
    normed = layer_norm(field_ref[...].astype(F32).reshape(CELLS, C)).astype(BF)
    first = iota((LAT, MCELLS, CELLS), 0) * MC - E
    slots = merid_slots(normed, first, W, W).astype(BF)
    out_ref[...] = slots
    edge_ref[0] = slots[EDGES[0]]
    edge_ref[1] = slots[EDGES[1]]


def merid_edge_kernel(
    side_ref, slots_hbm, edge_ref, outer_ref, inner_ref, out_hbm, left_ref, right_ref, done_ref, sems
):
    side = side_ref[0] == 1
    outer, inner = outer_ref[...].astype(F32), inner_ref[...].astype(F32)
    halos = (jnp.where(side, inner, outer), jnp.where(side, outer, inner))
    copies = []
    for n, (m, ref, halo) in enumerate(zip(EDGES, (left_ref, right_ref), halos)):
        ref[...] = halo.astype(BF)
        normed = layer_norm(halo).astype(BF)
        first = jnp.full((MCELLS, R * E), m * MC - n * (W + E), jnp.int32)
        done_ref[n] = (edge_ref[n].astype(F32) + merid_slots(normed, first, E, E)).astype(BF)
        copies.append(pltpu.make_async_copy(done_ref.at[n], out_hbm.at[m], sems.at[n]))
        copies[n].start()
    for copy in copies:
        copy.wait()


def merid_kernel(in_ref, w_ref, out_ref):
    last = in_ref[:, :, C:MLANES].reshape(CELLS, 128)
    t, u = iota((LAT * R, CELLS), 0), iota((LAT * R, CELLS), 1)
    place = ((t >> 2) << 4) + (t & 3)
    last = [mm(one_hot(u == place + b * R), last) for b in range(4)]
    last = jnp.concatenate(last, axis=1).astype(BF)
    normed = jnp.concatenate([in_ref[:, :, 0:C].reshape(CELLS, C), last], axis=0)
    count = CELLS + LAT * R
    queries = mm(normed, w_ref[:, 256:512]).astype(BF)
    keys = mm(normed, w_ref[:, 640:896]).astype(BF)
    values = mm(normed, w_ref[:, 896:1152]).astype(BF)
    t, s = iota((count, count), 0), iota((count, count), 1)
    row = jnp.where(t < CELLS, (t >> 2) & 3, 4)
    key = jnp.where(s < CELLS, (s >> 2) & 3, 4)
    bias = jnp.where(row == key, 0.0, -1e30)
    low = iota((count, 128), 1) < HD
    scale = 1.0 / math.sqrt(HD)
    parts, tail = [], None
    t, u = iota((LAT * 2 * R, LAT * R), 0), iota((LAT * 2 * R, LAT * R), 1)
    same = u == ((t >> 3) << 2) + (t & 3)
    for pair in range(2):
        lanes = slice(pair * 128, pair * 128 + 128)
        q, k, v = queries[:, lanes], keys[:, lanes], values[:, lanes]
        outs = []
        for side in (low, jnp.logical_not(low)):
            score = mm_nt(jnp.where(side, q, jnp.zeros_like(q)), k) * scale + bias
            weight = jnp.exp(score - jnp.max(score, axis=-1, keepdims=True))
            mass = jnp.sum(weight, axis=-1, keepdims=True)
            outs.append(mm(weight.astype(BF), v) / mass)
        both = jnp.where(low, outs[0], outs[1])
        parts.append(both[0:CELLS].reshape(LAT, MCELLS, 128))
        placed = mm(one_hot(same & (((t >> 2) & 1) == pair)), both[CELLS:].astype(BF))
        tail = placed if tail is None else tail + placed
    parts.append(tail.reshape(LAT, 2 * R, 128))
    out_ref[...] = jnp.concatenate(parts, axis=1).astype(BF)


def mix_kernel(odd_ref, zonal_ref, merid_ref, left_ref, right_ref, field_ref, w_ref, mixed_ref, far_ref, near_ref):
    rows = R * WIDE
    x = merid_ref[...].astype(F32)
    pairs = [x[:, p * MCELLS : (p + 1) * MCELLS].reshape(CELLS, 128).astype(BF) for p in range(2)]
    last = x[:, 2 * MCELLS :].reshape(LAT * 2 * R, 128).astype(BF)
    dims = (R, WIDE, 1)
    r, w = iota(dims, 0), iota(dims, 1) + E // 2
    m = (w * 205) >> 10
    cc = w - m * MC
    place = jnp.where(cc < MC - 1, m * MCELLS + cc * R + r, -1)
    place = one_hot(place == iota((R, WIDE, CELLS), 2)).reshape(rows, CELLS)
    attended = mm(zonal_ref[...].reshape(rows, 256), w_ref[0:256])
    for p in range(2):
        place_last = jnp.where(cc == MC - 1, m * 2 * R + p * R + r, -1)
        place_last = one_hot(place_last == iota((R, WIDE, LAT * 2 * R), 2)).reshape(rows, LAT * 2 * R)
        merid = mm(place, pairs[p]) + mm(place_last, last)
        attended = attended + mm(merid.astype(BF), w_ref[256 + p * 128 : 384 + p * 128])
    wide = widened(left_ref[...], field_ref[...], right_ref[...])
    mixed = (wide + attended.reshape(R, WIDE, C)).astype(BF)
    mixed_ref[...] = mixed
    odd = odd_ref[0] == 1

    @pl.when(odd)
    def after_is_far():
        far_ref[...] = mixed[1:4]
        near_ref[...] = mixed[0:3]

    @pl.when(jnp.logical_not(odd))
    def before_is_far():
        far_ref[...] = mixed[0:3]
        near_ref[...] = mixed[1:4]


def conv_part(rows, conv_ref, lanes, r):
    total = None
    for b in range(7):
        column = None
        for a in range(7):
            if r + a in rows:
                term = rows[r + a] * conv_ref[a * 7 + b, lanes][None, :]
                column = term if column is None else column + term
        moved = column[b + 1 : b + 1 + W]
        total = moved if total is None else total + moved
    return total


def own_conv_kernel(
    mixed_ref, conv_ref, w_in_hbm, w_back_hbm, out_ref, w_in_ref, w_back_ref, sems
):
    pairs = ((w_in_hbm, w_in_ref), (w_back_hbm, w_back_ref))
    loads = [pltpu.make_async_copy(a, b, sems.at[i]) for i, (a, b) in enumerate(pairs)]
    for load in loads:
        load.start()
    for lane in range(0, C, 128):
        lanes = slice(lane, lane + 128)
        rows = {3 + i: mixed_ref[i, :, lanes].astype(F32) for i in range(R)}
        for r in range(R):
            out_ref[r * W : (r + 1) * W, lanes] = conv_part(rows, conv_ref, lanes, r)
    for load in loads:
        load.wait()


def block_kernel(
    odd_ref, mixed_ref, own_ref, far_ref, near_ref, conv_ref, w_in_ref, w_back_ref, out_ref, conv_out
):
    odd = odd_ref[0] == 1
    for half in range(0, R, 2):
        cells = slice(half * W, (half + 2) * W)
        for lane in range(0, C, 128):
            lanes = slice(lane, lane + 128)
            rows = {}
            for i in range(3):
                far, near = far_ref[i, :, lanes].astype(F32), near_ref[i, :, lanes].astype(F32)
                rows[i] = jnp.where(odd, near, far)
                rows[7 + i] = jnp.where(odd, far, near)
            for r in range(half, half + 2):
                here = (slice(r * W, (r + 1) * W), lanes)
                conv_out[here] = own_ref[here] + conv_part(rows, conv_ref, lanes, r)
        normed = layer_norm(conv_out[cells]).astype(BF)
        hidden = mm(normed, w_in_ref[...])
        hidden = 0.5 * hidden * (1.0 + lax.erf(hidden * math.sqrt(0.5)))
        back = mm(hidden.astype(BF), w_back_ref[...])
        own = mixed_ref[half : half + 2].astype(F32)[:, E // 2 : E // 2 + W].reshape(2 * W, C)
        out_ref[half : half + 2] = (own + back).astype(BF).reshape(2, W, C)


def per_device(field, w_qkv, w_out, conv_w, w_in, w_back):
    inner_pairs = [(i, i + 1) for i in range(0, LON, 2)]
    outer_pairs = [(i, (i + 1) % LON) for i in range(1, LON, 2)]
    inner_pairs, outer_pairs = (pairs + [(j, i) for i, j in pairs] for pairs in (inner_pairs, outer_pairs))
    near_pairs = [(i, i + 1) for i in range(0, LAT, 2)]
    far_pairs = [(i, i + 1) for i in range(1, LAT - 1, 2)]
    near_pairs, far_pairs = (pairs + [(j, i) for i, j in pairs] for pairs in (near_pairs, far_pairs))
    along_y = [[y * ZS + z for y in range(YS)] for z in range(ZS)]
    along_z = [[y * ZS + z for z in range(ZS)] for y in range(YS)]
    lon = lax.axis_index("lon").astype(jnp.int32)
    y, side = (lon >> 2).reshape(1), (lon & 1).reshape(1)
    odd = (lax.axis_index("lat").astype(jnp.int32) & 1).reshape(1)
    field, y, side, odd = lax.optimization_barrier((field, y, side, odd))
    row, outer, inner = call(
        zonal_project_kernel,
        (shape(R, W, 384), shape(R * E, C), shape(R * E, C)),
        200_000_000,
        in_specs=[SMEM, ANY, ANY],
        scratch_shapes=[
            pltpu.VMEM((R, W, C), BF),
            pltpu.VMEM((C, 256), BF),
            pltpu.VMEM((C, 128), BF),
            pltpu.SemaphoreType.DMA((3,)),
        ],
    )(side, in_hbm(field), in_hbm(w_qkv))
    row = lax.all_to_all(row, "lon", 0, 0, axis_index_groups=along_z)
    slots = call(
        spread_kernel,
        shape(YS, KEYS, 128),
        10_000_000,
        out_specs=ANY,
        scratch_shapes=[pltpu.VMEM((KEYS, 128), BF), pltpu.SemaphoreType.DMA((YS,))],
    )(row)
    slots = lax.all_to_all(slots, "lon", 0, 0, axis_index_groups=along_y)
    inner = lax.ppermute(inner, "lon", inner_pairs)
    outer = lax.ppermute(outer, "lon", outer_pairs)
    merid, merid_edges = call(
        merid_own_kernel, (shape(LAT, MCELLS, MLANES), shape(2, MCELLS, MLANES)), 300_000_000
    )(field)
    merid, field_left, field_right = call(
        merid_edge_kernel,
        (shape(LAT, MCELLS, MLANES), shape(R * E, C), shape(R * E, C)),
        10_000_000,
        in_specs=[SMEM, ANY, VMEM, VMEM, VMEM],
        out_specs=[ANY, VMEM, VMEM],
        input_output_aliases={1: 0},
        scratch_shapes=[pltpu.VMEM((2, MCELLS, MLANES), BF), pltpu.SemaphoreType.DMA((2,))],
    )(side, merid, merid_edges, outer, inner)
    slots, merid = lax.optimization_barrier((slots, merid))
    merid = lax.all_to_all(merid, "lat", 0, 0)
    zonal = call(
        zonal_kernel, shape(ZS, WIDE, 256), 4_000_000_000, vmem=24, in_specs=[SMEM, VMEM, VMEM]
    )(y, row, slots)
    zonal = lax.all_to_all(zonal, "lon", 0, 0, axis_index_groups=along_z)
    merid = call(merid_kernel, shape(LAT, BROWS, 128), 1_000_000_000)(merid, w_qkv)
    merid = lax.all_to_all(merid, "lat", 0, 0)
    mixed, far, near = call(
        mix_kernel,
        (shape(R, WIDE, C), shape(3, WIDE, C), shape(3, WIDE, C)),
        800_000_000,
        in_specs=[SMEM] + [VMEM] * 6,
    )(odd, zonal, merid, field_left, field_right, field, w_out)
    near = lax.ppermute(near, "lat", near_pairs)
    far = lax.ppermute(far, "lat", far_pairs)
    conv_w = conv_w.reshape(49, C)
    own, w_in, w_back = call(
        own_conv_kernel,
        (jax.ShapeDtypeStruct((CELLS, C), F32), shape(*w_in.shape), shape(*w_back.shape)),
        1_000_000_000,
        in_specs=[VMEM, VMEM, ANY, ANY],
        scratch_shapes=[pltpu.SemaphoreType.DMA((2,))],
    )(mixed, conv_w, in_hbm(w_in), in_hbm(w_back))
    return call(
        block_kernel,
        shape(R, W, C),
        2_000_000_000,
        in_specs=[SMEM] + [VMEM] * 7,
        scratch_shapes=[pltpu.VMEM((CELLS, C), F32)],
    )(odd, mixed, own, far, near, conv_w, w_in, w_back)


def solution(mesh):
    return jax.shard_map(
        per_device,
        mesh=mesh,
        in_specs=(P("lat", "lon", None), P(), P(), P(), P(), P()),
        out_specs=P("lat", "lon", None),
        check_vma=False,
    )
```

```python
import math

import jax
import jax.numpy as jnp
from jax import lax
from jax.experimental import pallas as pl
from jax.experimental.pallas import tpu as pltpu
from jax.sharding import PartitionSpec as P

C = 512
HD = 64
LAT = 16
LON = 32
R = 4
W = 64
CELLS = R * W
ECELLS = 16
E = 8
WIDE = W + E
MWIDE = W + 2 * E
MC = MWIDE // LAT
EDGES = (1, LAT - 2)
MCELLS = 16
MLANES = 640
BROWS = 40
YS = 8
ZS = 4
SPAN = ZS * W
KEYS = SPAN + 2 * E
F32 = jnp.float32
BF = jnp.bfloat16


def iota(shape, dim):
    return lax.broadcasted_iota(jnp.int32, shape, dim)


def one_hot(hit):
    return jnp.where(hit, 1.0, 0.0).astype(BF)


def mm(a, b):
    return jnp.dot(a, b, preferred_element_type=F32)


def mm_nt(a, b):
    return lax.dot_general(a, b, (((1,), (1,)), ((), ())), preferred_element_type=F32)


def layer_norm(values):
    center = values - jnp.mean(values, axis=-1, keepdims=True)
    spread = jnp.mean(center * center, axis=-1, keepdims=True)
    return center * lax.rsqrt(spread + 1e-06)


def shape(*dims):
    return jax.ShapeDtypeStruct(dims, BF)


VMEM = pl.BlockSpec(memory_space=pltpu.VMEM)
ANY = pl.BlockSpec(memory_space=pl.ANY)
SMEM = pl.BlockSpec(memory_space=pltpu.SMEM)


def call(kernel, out_shape, flops, vmem=16, **kw):
    return pl.pallas_call(
        kernel,
        out_shape=out_shape,
        compiler_params=pltpu.CompilerParams(vmem_limit_bytes=vmem * 1024 * 1024),
        cost_estimate=pl.CostEstimate(flops=flops, bytes_accessed=2_000_000, transcendentals=0),
        **kw,
    )


def in_hbm(array):
    return pltpu.with_memory_space_constraint(array, pltpu.HBM)


def zonal_project_kernel(
    side_ref, field_hbm, w_hbm, out_ref, outer_ref, inner_ref, field_ref, wq_ref, wkv_ref, sems
):
    loads = [
        pltpu.make_async_copy(field_hbm, field_ref, sems.at[0]),
        pltpu.make_async_copy(w_hbm.at[:, 512:640], wkv_ref, sems.at[1]),
        pltpu.make_async_copy(w_hbm.at[:, 0:256], wq_ref, sems.at[2]),
    ]
    for load in loads:
        load.start()
    loads[0].wait()
    field = field_ref[...].astype(F32)
    side = side_ref[0] == 1
    i, u = iota((2 * ECELLS, CELLS), 0), iota((2 * ECELLS, CELLS), 1)
    select = one_hot(u == ((i >> 2) & 3) * W + (i & 3) + jnp.where(i < ECELLS, 0, W - 4))
    edges = mm(select, field_ref[...].reshape(CELLS, C))
    first, last = edges[0:ECELLS], edges[ECELLS:]
    outer_ref[...] = jnp.where(side, last, first).astype(BF)
    inner_ref[...] = jnp.where(side, first, last).astype(BF)
    normed = layer_norm(field.reshape(CELLS, C)).astype(BF)
    loads[1].wait()
    out_ref[:, :, 256:384] = mm(normed, wkv_ref[...]).astype(BF).reshape(R, W, 128)
    loads[2].wait()
    out_ref[:, :, 0:256] = mm(normed, wq_ref[...]).astype(BF).reshape(R, W, 256)


def spread_kernel(in_ref, out_hbm, slot_ref, sems):
    slot_ref[0:SPAN, :] = in_ref[:, :, 256:384].reshape(SPAN, 128)
    first = in_ref[0, :, 0:256].astype(F32)[0:E]
    last = in_ref[ZS - 1, :, 0:256].astype(F32)[W - E : W]
    edge = jnp.where(iota((E, 256), 0) < E // 2, first, last)
    slot_ref[SPAN:KEYS, :] = jnp.concatenate([edge[:, 0:128], edge[:, 128:256]], axis=0).astype(BF)
    copies = [pltpu.make_async_copy(slot_ref, out_hbm.at[y], sems.at[y]) for y in range(YS)]
    for copy in copies:
        copy.start()
    for copy in copies:
        copy.wait()


def zonal_kernel(y_ref, own_ref, all_ref, out_ref):
    y = y_ref[0]
    kv = all_ref[:, 0:SPAN, :].reshape(YS * SPAN, 128)
    ones = iota((YS * SPAN, 128), 1) < HD
    kv_one = jnp.where(ones, jnp.ones_like(kv), kv)
    behind = all_ref[lax.rem(y + YS - 1, YS), SPAN:KEYS, :].astype(F32)
    ahead = all_ref[lax.rem(y + 1, YS), SPAN:KEYS, :].astype(F32)
    count = SPAN + E
    low = iota((count, 128), 1) < HD
    for pair in range(2):
        lanes = slice(pair * 128, pair * 128 + 128)
        before, after = slice(pair * E + E // 2, pair * E + E), slice(pair * E, pair * E + E // 2)
        q = own_ref[:, :, lanes].astype(F32).reshape(SPAN, 128)
        q = jnp.concatenate([behind[before], q, ahead[after]], axis=0) * (1.0 / math.sqrt(HD))
        outs = []
        for head in range(2):
            placed = q if head == 0 else pltpu.roll(q, HD, 1)
            placed = jnp.where(low, placed, 0.0).astype(BF)
            score = mm_nt(placed, kv)
            weight = jnp.exp(score - jnp.max(score, axis=-1, keepdims=True)).astype(BF)
            outs.append(mm(weight, kv_one))
        even, odd = outs
        blended = jnp.where(low, pltpu.roll(even, HD, 1), odd)
        mass = jnp.where(low, even, pltpu.roll(odd, HD, 1))
        heads = blended / mass
        for z in range(ZS):
            out_ref[z, :, lanes] = heads[z * W : z * W + WIDE].astype(BF)


def widened(left, own, right):
    left, right = (a.astype(F32).reshape(R, E, a.shape[-1]) for a in (left, right))
    return jnp.concatenate([left[:, E // 2 :], own.astype(F32), right[:, 0 : E // 2]], axis=1)


def merid_slots(normed, first, row_step, width):
    dims = first.shape[:-2] + (MCELLS, normed.shape[0])
    i, u = iota(dims, len(dims) - 2), iota(dims, len(dims) - 1)
    c = first + (i >> 2)
    main = one_hot(((i & 3) * row_step + c == u) & (c >= 0) & (c < width))
    c = first + MC - 1
    last = one_hot(((i & 3) * row_step + c == u) & (c >= 0) & (c < width))
    shape_2d, shape_out = (-1, normed.shape[0]), dims[:-1] + (C,)
    main = mm(main.reshape(shape_2d), normed).reshape(shape_out)
    last = mm(last.reshape(shape_2d), normed).reshape(shape_out)
    block = iota(dims[:-1] + (128,), len(dims) - 2) >> 2
    tail = sum(jnp.where(block == b, last[..., b * 128 : b * 128 + 128], 0.0) for b in range(4))
    return jnp.concatenate([main, tail], axis=-1)


def merid_own_kernel(field_ref, out_ref, edge_ref):
    normed = layer_norm(field_ref[...].astype(F32).reshape(CELLS, C)).astype(BF)
    first = iota((LAT, MCELLS, CELLS), 0) * MC - E
    slots = merid_slots(normed, first, W, W).astype(BF)
    out_ref[...] = slots
    edge_ref[0] = slots[EDGES[0]]
    edge_ref[1] = slots[EDGES[1]]


def merid_edge_kernel(
    side_ref, slots_hbm, edge_ref, outer_ref, inner_ref, out_hbm, left_ref, right_ref, done_ref, sems
):
    side = side_ref[0] == 1
    outer, inner = outer_ref[...].astype(F32), inner_ref[...].astype(F32)
    halos = (jnp.where(side, inner, outer), jnp.where(side, outer, inner))
    i, u = iota((R * E, ECELLS), 0), iota((R * E, ECELLS), 1)
    cell = ((i >> 3) << 2) + (i & 3)
    fits = [one_hot((u == cell) & (((i >> 2) & 1) == 1 - n)) for n in range(2)]
    halos = [mm(fit, halo.astype(BF)) for fit, halo in zip(fits, halos)]
    copies = []
    for n, (m, ref, halo) in enumerate(zip(EDGES, (left_ref, right_ref), halos)):
        ref[...] = halo.astype(BF)
        normed = layer_norm(halo).astype(BF)
        first = jnp.full((MCELLS, R * E), m * MC - n * (W + E), jnp.int32)
        done_ref[n] = (edge_ref[n].astype(F32) + merid_slots(normed, first, E, E)).astype(BF)
        copies.append(pltpu.make_async_copy(done_ref.at[n], out_hbm.at[m], sems.at[n]))
        copies[n].start()
    for copy in copies:
        copy.wait()


def merid_kernel(in_ref, w_ref, out_ref):
    last = in_ref[:, :, C:MLANES].reshape(CELLS, 128)
    t, u = iota((LAT * R, CELLS), 0), iota((LAT * R, CELLS), 1)
    place = ((t >> 2) << 4) + (t & 3)
    last = [mm(one_hot(u == place + b * R), last) for b in range(4)]
    last = jnp.concatenate(last, axis=1).astype(BF)
    normed = jnp.concatenate([in_ref[:, :, 0:C].reshape(CELLS, C), last], axis=0)
    count = CELLS + LAT * R
    queries = mm(normed, w_ref[:, 256:512]).astype(BF)
    keys = mm(normed, w_ref[:, 640:896]).astype(BF)
    values = mm(normed, w_ref[:, 896:1152]).astype(BF)
    t, s = iota((count, count), 0), iota((count, count), 1)
    row = jnp.where(t < CELLS, (t >> 2) & 3, 4)
    key = jnp.where(s < CELLS, (s >> 2) & 3, 4)
    bias = jnp.where(row == key, 0.0, -1e30)
    low = iota((count, 128), 1) < HD
    scale = 1.0 / math.sqrt(HD)
    parts, tail = [], None
    t, u = iota((LAT * 2 * R, LAT * R), 0), iota((LAT * 2 * R, LAT * R), 1)
    same = u == ((t >> 3) << 2) + (t & 3)
    for pair in range(2):
        lanes = slice(pair * 128, pair * 128 + 128)
        q, k, v = queries[:, lanes], keys[:, lanes], values[:, lanes]
        outs = []
        for side in (low, jnp.logical_not(low)):
            score = mm_nt(jnp.where(side, q, jnp.zeros_like(q)), k) * scale + bias
            weight = jnp.exp(score - jnp.max(score, axis=-1, keepdims=True))
            mass = jnp.sum(weight, axis=-1, keepdims=True)
            outs.append(mm(weight.astype(BF), v) / mass)
        both = jnp.where(low, outs[0], outs[1])
        parts.append(both[0:CELLS].reshape(LAT, MCELLS, 128))
        placed = mm(one_hot(same & (((t >> 2) & 1) == pair)), both[CELLS:].astype(BF))
        tail = placed if tail is None else tail + placed
    parts.append(tail.reshape(LAT, 2 * R, 128))
    out_ref[...] = jnp.concatenate(parts, axis=1).astype(BF)


def mix_kernel(odd_ref, zonal_ref, merid_ref, left_ref, right_ref, field_ref, w_ref, mixed_ref, far_ref, near_ref):
    rows = R * WIDE
    x = merid_ref[...].astype(F32)
    pairs = [x[:, p * MCELLS : (p + 1) * MCELLS].reshape(CELLS, 128).astype(BF) for p in range(2)]
    last = x[:, 2 * MCELLS :].reshape(LAT * 2 * R, 128).astype(BF)
    dims = (R, WIDE, 1)
    r, w = iota(dims, 0), iota(dims, 1) + E // 2
    m = (w * 205) >> 10
    cc = w - m * MC
    place = jnp.where(cc < MC - 1, m * MCELLS + cc * R + r, -1)
    place = one_hot(place == iota((R, WIDE, CELLS), 2)).reshape(rows, CELLS)
    attended = mm(zonal_ref[...].reshape(rows, 256), w_ref[0:256])
    for p in range(2):
        place_last = jnp.where(cc == MC - 1, m * 2 * R + p * R + r, -1)
        place_last = one_hot(place_last == iota((R, WIDE, LAT * 2 * R), 2)).reshape(rows, LAT * 2 * R)
        merid = mm(place, pairs[p]) + mm(place_last, last)
        attended = attended + mm(merid.astype(BF), w_ref[256 + p * 128 : 384 + p * 128])
    wide = widened(left_ref[...], field_ref[...], right_ref[...])
    mixed = (wide + attended.reshape(R, WIDE, C)).astype(BF)
    mixed_ref[...] = mixed
    odd = odd_ref[0] == 1

    @pl.when(odd)
    def after_is_far():
        far_ref[...] = mixed[1:4]
        near_ref[...] = mixed[0:3]

    @pl.when(jnp.logical_not(odd))
    def before_is_far():
        far_ref[...] = mixed[0:3]
        near_ref[...] = mixed[1:4]


def conv_part(rows, conv_ref, lanes, r):
    total = None
    for b in range(7):
        column = None
        for a in range(7):
            if r + a in rows:
                term = rows[r + a] * conv_ref[a * 7 + b, lanes][None, :]
                column = term if column is None else column + term
        moved = column[b + 1 : b + 1 + W]
        total = moved if total is None else total + moved
    return total


def own_conv_kernel(
    mixed_ref, conv_ref, w_in_hbm, w_back_hbm, out_ref, w_in_ref, w_back_ref, sems
):
    pairs = ((w_in_hbm, w_in_ref), (w_back_hbm, w_back_ref))
    loads = [pltpu.make_async_copy(a, b, sems.at[i]) for i, (a, b) in enumerate(pairs)]
    for load in loads:
        load.start()
    for lane in range(0, C, 128):
        lanes = slice(lane, lane + 128)
        rows = {3 + i: mixed_ref[i, :, lanes].astype(F32) for i in range(R)}
        for r in range(R):
            out_ref[r * W : (r + 1) * W, lanes] = conv_part(rows, conv_ref, lanes, r)
    for load in loads:
        load.wait()


def block_kernel(
    odd_ref, mixed_ref, own_ref, far_ref, near_ref, conv_ref, w_in_ref, w_back_ref, out_ref, conv_out
):
    odd = odd_ref[0] == 1
    for lane in range(0, C, 128):
        lanes = slice(lane, lane + 128)
        rows = {}
        for i in range(3):
            far, near = far_ref[i, :, lanes].astype(F32), near_ref[i, :, lanes].astype(F32)
            rows[i] = jnp.where(odd, near, far)
            rows[7 + i] = jnp.where(odd, far, near)
        for r in range(R):
            here = (slice(r * W, (r + 1) * W), lanes)
            conv_out[here] = own_ref[here] + conv_part(rows, conv_ref, lanes, r)
    normed = layer_norm(conv_out[...]).astype(BF)
    hidden = mm(normed, w_in_ref[...])
    hidden = 0.5 * hidden * (1.0 + lax.erf(hidden * math.sqrt(0.5)))
    back = mm(hidden.astype(BF), w_back_ref[...])
    own = mixed_ref[...].astype(F32)[:, E // 2 : E // 2 + W].reshape(CELLS, C)
    out_ref[...] = (own + back).astype(BF).reshape(R, W, C)


def per_device(field, w_qkv, w_out, conv_w, w_in, w_back):
    inner_pairs = [(i, i + 1) for i in range(0, LON, 2)]
    outer_pairs = [(i, (i + 1) % LON) for i in range(1, LON, 2)]
    inner_pairs, outer_pairs = (pairs + [(j, i) for i, j in pairs] for pairs in (inner_pairs, outer_pairs))
    near_pairs = [(i, i + 1) for i in range(0, LAT, 2)]
    far_pairs = [(i, i + 1) for i in range(1, LAT - 1, 2)]
    near_pairs, far_pairs = (pairs + [(j, i) for i, j in pairs] for pairs in (near_pairs, far_pairs))
    along_y = [[y * ZS + z for y in range(YS)] for z in range(ZS)]
    along_z = [[y * ZS + z for z in range(ZS)] for y in range(YS)]
    lon = lax.axis_index("lon").astype(jnp.int32)
    y, side = (lon >> 2).reshape(1), (lon & 1).reshape(1)
    odd = (lax.axis_index("lat").astype(jnp.int32) & 1).reshape(1)
    field, y, side, odd = lax.optimization_barrier((field, y, side, odd))
    row, outer, inner = call(
        zonal_project_kernel,
        (shape(R, W, 384), shape(ECELLS, C), shape(ECELLS, C)),
        200_000_000,
        in_specs=[SMEM, ANY, ANY],
        scratch_shapes=[
            pltpu.VMEM((R, W, C), BF),
            pltpu.VMEM((C, 256), BF),
            pltpu.VMEM((C, 128), BF),
            pltpu.SemaphoreType.DMA((3,)),
        ],
    )(side, in_hbm(field), in_hbm(w_qkv))
    row = lax.all_to_all(row, "lon", 0, 0, axis_index_groups=along_z)
    slots = call(
        spread_kernel,
        shape(YS, KEYS, 128),
        10_000_000,
        out_specs=ANY,
        scratch_shapes=[pltpu.VMEM((KEYS, 128), BF), pltpu.SemaphoreType.DMA((YS,))],
    )(row)
    slots = lax.all_to_all(slots, "lon", 0, 0, axis_index_groups=along_y)
    inner = lax.ppermute(inner, "lon", inner_pairs)
    outer = lax.ppermute(outer, "lon", outer_pairs)
    merid, merid_edges = call(
        merid_own_kernel, (shape(LAT, MCELLS, MLANES), shape(2, MCELLS, MLANES)), 300_000_000
    )(field)
    merid, field_left, field_right = call(
        merid_edge_kernel,
        (shape(LAT, MCELLS, MLANES), shape(R * E, C), shape(R * E, C)),
        10_000_000,
        in_specs=[SMEM, ANY, VMEM, VMEM, VMEM],
        out_specs=[ANY, VMEM, VMEM],
        input_output_aliases={1: 0},
        scratch_shapes=[pltpu.VMEM((2, MCELLS, MLANES), BF), pltpu.SemaphoreType.DMA((2,))],
    )(side, merid, merid_edges, outer, inner)
    slots, merid = lax.optimization_barrier((slots, merid))
    merid = lax.all_to_all(merid, "lat", 0, 0)
    zonal = call(
        zonal_kernel, shape(ZS, WIDE, 256), 4_000_000_000, vmem=24, in_specs=[SMEM, VMEM, VMEM]
    )(y, row, slots)
    zonal = lax.all_to_all(zonal, "lon", 0, 0, axis_index_groups=along_z)
    merid = call(merid_kernel, shape(LAT, BROWS, 128), 1_000_000_000)(merid, w_qkv)
    merid = lax.all_to_all(merid, "lat", 0, 0)
    mixed, far, near = call(
        mix_kernel,
        (shape(R, WIDE, C), shape(3, WIDE, C), shape(3, WIDE, C)),
        800_000_000,
        in_specs=[SMEM] + [VMEM] * 6,
    )(odd, zonal, merid, field_left, field_right, field, w_out)
    near = lax.ppermute(near, "lat", near_pairs)
    far = lax.ppermute(far, "lat", far_pairs)
    conv_w = conv_w.reshape(49, C)
    own, w_in, w_back = call(
        own_conv_kernel,
        (jax.ShapeDtypeStruct((CELLS, C), F32), shape(*w_in.shape), shape(*w_back.shape)),
        1_000_000_000,
        in_specs=[VMEM, VMEM, ANY, ANY],
        scratch_shapes=[pltpu.SemaphoreType.DMA((2,))],
    )(mixed, conv_w, in_hbm(w_in), in_hbm(w_back))
    return call(
        block_kernel,
        shape(R, W, C),
        2_000_000_000,
        in_specs=[SMEM] + [VMEM] * 7,
        scratch_shapes=[pltpu.VMEM((CELLS, C), F32)],
    )(odd, mixed, own, far, near, conv_w, w_in, w_back)


def solution(mesh):
    return jax.shard_map(
        per_device,
        mesh=mesh,
        in_specs=(P("lat", "lon", None), P(), P(), P(), P(), P()),
        out_specs=P("lat", "lon", None),
        check_vma=False,
    )
```

```python
import math

import jax
import jax.numpy as jnp
from jax import lax
from jax.experimental import pallas as pl
from jax.experimental.pallas import tpu as pltpu
from jax.sharding import PartitionSpec as P

C = 512
HD = 64
LAT = 16
LON = 32
R = 4
W = 64
CELLS = R * W
ECELLS = 16
E = 8
WIDE = W + E
MWIDE = W + 2 * E
MC = MWIDE // LAT
EDGES = (1, LAT - 2)
MCELLS = 16
MLANES = 640
BROWS = 40
YS = 8
ZS = 4
SPAN = ZS * W
KEYS = SPAN + 2 * E
F32 = jnp.float32
BF = jnp.bfloat16


def iota(shape, dim):
    return lax.broadcasted_iota(jnp.int32, shape, dim)


def one_hot(hit):
    return jnp.where(hit, 1.0, 0.0).astype(BF)


def mm(a, b):
    return jnp.dot(a, b, preferred_element_type=F32)


def mm_nt(a, b):
    return lax.dot_general(a, b, (((1,), (1,)), ((), ())), preferred_element_type=F32)


def layer_norm(values):
    center = values - jnp.mean(values, axis=-1, keepdims=True)
    spread = jnp.mean(center * center, axis=-1, keepdims=True)
    return center * lax.rsqrt(spread + 1e-06)


def shape(*dims):
    return jax.ShapeDtypeStruct(dims, BF)


VMEM = pl.BlockSpec(memory_space=pltpu.VMEM)
ANY = pl.BlockSpec(memory_space=pl.ANY)
SMEM = pl.BlockSpec(memory_space=pltpu.SMEM)


def call(kernel, out_shape, flops, vmem=16, **kw):
    return pl.pallas_call(
        kernel,
        out_shape=out_shape,
        compiler_params=pltpu.CompilerParams(vmem_limit_bytes=vmem * 1024 * 1024),
        cost_estimate=pl.CostEstimate(flops=flops, bytes_accessed=2_000_000, transcendentals=0),
        **kw,
    )


def in_hbm(array):
    return pltpu.with_memory_space_constraint(array, pltpu.HBM)


def zonal_project_kernel(
    side_ref, field_hbm, w_hbm, out_ref, outer_ref, inner_ref, field_ref, wq_ref, wkv_ref, sems
):
    loads = [
        pltpu.make_async_copy(field_hbm, field_ref, sems.at[0]),
        pltpu.make_async_copy(w_hbm.at[:, 512:640], wkv_ref, sems.at[1]),
        pltpu.make_async_copy(w_hbm.at[:, 0:256], wq_ref, sems.at[2]),
    ]
    for load in loads:
        load.start()
    loads[0].wait()
    field = field_ref[...].astype(F32)
    side = side_ref[0] == 1
    i, u = iota((2 * ECELLS, CELLS), 0), iota((2 * ECELLS, CELLS), 1)
    select = one_hot(u == ((i >> 2) & 3) * W + (i & 3) + jnp.where(i < ECELLS, 0, W - 4))
    edges = mm(select, field_ref[...].reshape(CELLS, C))
    first, last = edges[0:ECELLS], edges[ECELLS:]
    outer_ref[...] = jnp.where(side, last, first).astype(BF)
    inner_ref[...] = jnp.where(side, first, last).astype(BF)
    normed = layer_norm(field.reshape(CELLS, C)).astype(BF)
    loads[1].wait()
    out_ref[:, :, 256:384] = mm(normed, wkv_ref[...]).astype(BF).reshape(R, W, 128)
    loads[2].wait()
    out_ref[:, :, 0:256] = mm(normed, wq_ref[...]).astype(BF).reshape(R, W, 256)


def spread_kernel(in_ref, out_hbm, slot_ref, sems):
    slot_ref[0:SPAN, :] = in_ref[:, :, 256:384].reshape(SPAN, 128)
    first = in_ref[0, :, 0:256].astype(F32)[0:E]
    last = in_ref[ZS - 1, :, 0:256].astype(F32)[W - E : W]
    edge = jnp.where(iota((E, 256), 0) < E // 2, first, last)
    slot_ref[SPAN:KEYS, :] = jnp.concatenate([edge[:, 0:128], edge[:, 128:256]], axis=0).astype(BF)
    copies = [pltpu.make_async_copy(slot_ref, out_hbm.at[y], sems.at[y]) for y in range(YS)]
    for copy in copies:
        copy.start()
    for copy in copies:
        copy.wait()


def zonal_kernel(y_ref, own_ref, all_ref, out_ref):
    y = y_ref[0]
    kv = all_ref[:, 0:SPAN, :].reshape(YS * SPAN, 128)
    ones = iota((YS * SPAN, 128), 1) < HD
    kv_one = jnp.where(ones, jnp.ones_like(kv), kv)
    behind = all_ref[lax.rem(y + YS - 1, YS), SPAN:KEYS, :].astype(F32)
    ahead = all_ref[lax.rem(y + 1, YS), SPAN:KEYS, :].astype(F32)
    count = SPAN + E
    low = iota((count, 128), 1) < HD
    for pair in range(2):
        lanes = slice(pair * 128, pair * 128 + 128)
        before, after = slice(pair * E + E // 2, pair * E + E), slice(pair * E, pair * E + E // 2)
        q = own_ref[:, :, lanes].astype(F32).reshape(SPAN, 128)
        q = jnp.concatenate([behind[before], q, ahead[after]], axis=0) * (1.0 / math.sqrt(HD))
        outs = []
        for head in range(2):
            placed = q if head == 0 else pltpu.roll(q, HD, 1)
            placed = jnp.where(low, placed, 0.0).astype(BF)
            score = mm_nt(placed, kv)
            weight = jnp.exp(score - jnp.max(score, axis=-1, keepdims=True)).astype(BF)
            outs.append(mm(weight, kv_one))
        even, odd = outs
        blended = jnp.where(low, pltpu.roll(even, HD, 1), odd)
        mass = jnp.where(low, even, pltpu.roll(odd, HD, 1))
        heads = blended / mass
        for z in range(ZS):
            out_ref[z, :, lanes] = heads[z * W : z * W + WIDE].astype(BF)


def widened(left, own, right):
    left, right = (a.astype(F32).reshape(R, E, a.shape[-1]) for a in (left, right))
    return jnp.concatenate([left[:, E // 2 :], own.astype(F32), right[:, 0 : E // 2]], axis=1)


def merid_slots(normed, first, row_step, width):
    dims = first.shape[:-2] + (MCELLS, normed.shape[0])
    i, u = iota(dims, len(dims) - 2), iota(dims, len(dims) - 1)
    c = first + (i >> 2)
    main = one_hot(((i & 3) * row_step + c == u) & (c >= 0) & (c < width))
    c = first + MC - 1
    last = one_hot(((i & 3) * row_step + c == u) & (c >= 0) & (c < width))
    shape_2d, shape_out = (-1, normed.shape[0]), dims[:-1] + (C,)
    main = mm(main.reshape(shape_2d), normed).reshape(shape_out)
    last = mm(last.reshape(shape_2d), normed).reshape(shape_out)
    block = iota(dims[:-1] + (128,), len(dims) - 2) >> 2
    tail = sum(jnp.where(block == b, last[..., b * 128 : b * 128 + 128], 0.0) for b in range(4))
    return jnp.concatenate([main, tail], axis=-1)


def merid_own_kernel(field_ref, out_ref, edge_ref):
    normed = layer_norm(field_ref[...].astype(F32).reshape(CELLS, C)).astype(BF)
    first = iota((LAT, MCELLS, CELLS), 0) * MC - E
    slots = merid_slots(normed, first, W, W).astype(BF)
    out_ref[...] = slots
    edge_ref[0] = slots[EDGES[0]]
    edge_ref[1] = slots[EDGES[1]]


def merid_edge_kernel(
    side_ref, slots_hbm, edge_ref, outer_ref, inner_ref, out_hbm, left_ref, right_ref, done_ref, sems
):
    side = side_ref[0] == 1
    outer, inner = outer_ref[...].astype(F32), inner_ref[...].astype(F32)
    halos = (jnp.where(side, inner, outer), jnp.where(side, outer, inner))
    copies = []
    for n, (m, halo) in enumerate(zip(EDGES, halos)):
        normed = layer_norm(halo).astype(BF)
        first = jnp.full((MCELLS, ECELLS), m * MC - (E // 2 if n == 0 else W + E), jnp.int32)
        done_ref[n] = (edge_ref[n].astype(F32) + merid_slots(normed, first, 4, 4)).astype(BF)
        copies.append(pltpu.make_async_copy(done_ref.at[n], out_hbm.at[m], sems.at[n]))
        copies[n].start()
    i, u = iota((R * E, ECELLS), 0), iota((R * E, ECELLS), 1)
    cell = ((i >> 3) << 2) + (i & 3)
    for n, (ref, halo) in enumerate(zip((left_ref, right_ref), halos)):
        fit = one_hot((u == cell) & (((i >> 2) & 1) == 1 - n))
        ref[...] = mm(fit, halo.astype(BF)).astype(BF)
    for copy in copies:
        copy.wait()


def merid_kernel(in_ref, w_ref, out_ref):
    last = in_ref[:, :, C:MLANES].reshape(CELLS, 128)
    t, u = iota((LAT * R, CELLS), 0), iota((LAT * R, CELLS), 1)
    place = ((t >> 2) << 4) + (t & 3)
    last = [mm(one_hot(u == place + b * R), last) for b in range(4)]
    last = jnp.concatenate(last, axis=1).astype(BF)
    normed = jnp.concatenate([in_ref[:, :, 0:C].reshape(CELLS, C), last], axis=0)
    count = CELLS + LAT * R
    queries = mm(normed, w_ref[:, 256:512]).astype(BF)
    keys = mm(normed, w_ref[:, 640:896]).astype(BF)
    values = mm(normed, w_ref[:, 896:1152]).astype(BF)
    t, s = iota((count, count), 0), iota((count, count), 1)
    row = jnp.where(t < CELLS, (t >> 2) & 3, 4)
    key = jnp.where(s < CELLS, (s >> 2) & 3, 4)
    bias = jnp.where(row == key, 0.0, -1e30)
    low = iota((count, 128), 1) < HD
    scale = 1.0 / math.sqrt(HD)
    parts, tail = [], None
    t, u = iota((LAT * 2 * R, LAT * R), 0), iota((LAT * 2 * R, LAT * R), 1)
    same = u == ((t >> 3) << 2) + (t & 3)
    for pair in range(2):
        lanes = slice(pair * 128, pair * 128 + 128)
        q, k, v = queries[:, lanes], keys[:, lanes], values[:, lanes]
        outs = []
        for side in (low, jnp.logical_not(low)):
            score = mm_nt(jnp.where(side, q, jnp.zeros_like(q)), k) * scale + bias
            weight = jnp.exp(score - jnp.max(score, axis=-1, keepdims=True))
            mass = jnp.sum(weight, axis=-1, keepdims=True)
            outs.append(mm(weight.astype(BF), v) / mass)
        both = jnp.where(low, outs[0], outs[1])
        parts.append(both[0:CELLS].reshape(LAT, MCELLS, 128))
        placed = mm(one_hot(same & (((t >> 2) & 1) == pair)), both[CELLS:].astype(BF))
        tail = placed if tail is None else tail + placed
    parts.append(tail.reshape(LAT, 2 * R, 128))
    out_ref[...] = jnp.concatenate(parts, axis=1).astype(BF)


def mix_kernel(odd_ref, zonal_ref, merid_ref, left_ref, right_ref, field_ref, w_ref, mixed_ref, far_ref, near_ref):
    rows = R * WIDE
    x = merid_ref[...].astype(F32)
    pairs = [x[:, p * MCELLS : (p + 1) * MCELLS].reshape(CELLS, 128).astype(BF) for p in range(2)]
    last = x[:, 2 * MCELLS :].reshape(LAT * 2 * R, 128).astype(BF)
    dims = (R, WIDE, 1)
    r, w = iota(dims, 0), iota(dims, 1) + E // 2
    m = (w * 205) >> 10
    cc = w - m * MC
    place = jnp.where(cc < MC - 1, m * MCELLS + cc * R + r, -1)
    place = one_hot(place == iota((R, WIDE, CELLS), 2)).reshape(rows, CELLS)
    attended = mm(zonal_ref[...].reshape(rows, 256), w_ref[0:256])
    for p in range(2):
        place_last = jnp.where(cc == MC - 1, m * 2 * R + p * R + r, -1)
        place_last = one_hot(place_last == iota((R, WIDE, LAT * 2 * R), 2)).reshape(rows, LAT * 2 * R)
        merid = mm(place, pairs[p]) + mm(place_last, last)
        attended = attended + mm(merid.astype(BF), w_ref[256 + p * 128 : 384 + p * 128])
    wide = widened(left_ref[...], field_ref[...], right_ref[...])
    mixed = (wide + attended.reshape(R, WIDE, C)).astype(BF)
    mixed_ref[...] = mixed
    odd = odd_ref[0] == 1

    @pl.when(odd)
    def after_is_far():
        far_ref[...] = mixed[1:4]
        near_ref[...] = mixed[0:3]

    @pl.when(jnp.logical_not(odd))
    def before_is_far():
        far_ref[...] = mixed[0:3]
        near_ref[...] = mixed[1:4]


def conv_part(rows, conv_ref, lanes, r):
    total = None
    for b in range(7):
        column = None
        for a in range(7):
            if r + a in rows:
                term = rows[r + a] * conv_ref[a * 7 + b, lanes][None, :]
                column = term if column is None else column + term
        moved = column[b + 1 : b + 1 + W]
        total = moved if total is None else total + moved
    return total


def own_conv_kernel(
    mixed_ref, conv_ref, w_in_hbm, w_back_hbm, out_ref, w_in_ref, w_back_ref, sems
):
    pairs = ((w_in_hbm, w_in_ref), (w_back_hbm, w_back_ref))
    loads = [pltpu.make_async_copy(a, b, sems.at[i]) for i, (a, b) in enumerate(pairs)]
    for load in loads:
        load.start()
    for lane in range(0, C, 128):
        lanes = slice(lane, lane + 128)
        rows = {3 + i: mixed_ref[i, :, lanes].astype(F32) for i in range(R)}
        for r in range(R):
            out_ref[r * W : (r + 1) * W, lanes] = conv_part(rows, conv_ref, lanes, r)
    for load in loads:
        load.wait()


def block_kernel(
    odd_ref, mixed_ref, own_ref, far_ref, near_ref, conv_ref, w_in_ref, w_back_ref, out_ref, conv_out
):
    odd = odd_ref[0] == 1
    for lane in range(0, C, 128):
        lanes = slice(lane, lane + 128)
        rows = {}
        for i in range(3):
            far, near = far_ref[i, :, lanes].astype(F32), near_ref[i, :, lanes].astype(F32)
            rows[i] = jnp.where(odd, near, far)
            rows[7 + i] = jnp.where(odd, far, near)
        for r in range(R):
            here = (slice(r * W, (r + 1) * W), lanes)
            conv_out[here] = own_ref[here] + conv_part(rows, conv_ref, lanes, r)
    normed = layer_norm(conv_out[...]).astype(BF)
    hidden = mm(normed, w_in_ref[...])
    hidden = 0.5 * hidden * (1.0 + lax.erf(hidden * math.sqrt(0.5)))
    back = mm(hidden.astype(BF), w_back_ref[...])
    own = mixed_ref[...].astype(F32)[:, E // 2 : E // 2 + W].reshape(CELLS, C)
    out_ref[...] = (own + back).astype(BF).reshape(R, W, C)


def per_device(field, w_qkv, w_out, conv_w, w_in, w_back):
    inner_pairs = [(i, i + 1) for i in range(0, LON, 2)]
    outer_pairs = [(i, (i + 1) % LON) for i in range(1, LON, 2)]
    inner_pairs, outer_pairs = (pairs + [(j, i) for i, j in pairs] for pairs in (inner_pairs, outer_pairs))
    near_pairs = [(i, i + 1) for i in range(0, LAT, 2)]
    far_pairs = [(i, i + 1) for i in range(1, LAT - 1, 2)]
    near_pairs, far_pairs = (pairs + [(j, i) for i, j in pairs] for pairs in (near_pairs, far_pairs))
    along_y = [[y * ZS + z for y in range(YS)] for z in range(ZS)]
    along_z = [[y * ZS + z for z in range(ZS)] for y in range(YS)]
    lon = lax.axis_index("lon").astype(jnp.int32)
    y, side = (lon >> 2).reshape(1), (lon & 1).reshape(1)
    odd = (lax.axis_index("lat").astype(jnp.int32) & 1).reshape(1)
    field, y, side, odd = lax.optimization_barrier((field, y, side, odd))
    row, outer, inner = call(
        zonal_project_kernel,
        (shape(R, W, 384), shape(ECELLS, C), shape(ECELLS, C)),
        200_000_000,
        in_specs=[SMEM, ANY, ANY],
        scratch_shapes=[
            pltpu.VMEM((R, W, C), BF),
            pltpu.VMEM((C, 256), BF),
            pltpu.VMEM((C, 128), BF),
            pltpu.SemaphoreType.DMA((3,)),
        ],
    )(side, in_hbm(field), in_hbm(w_qkv))
    row = lax.all_to_all(row, "lon", 0, 0, axis_index_groups=along_z)
    slots = call(
        spread_kernel,
        shape(YS, KEYS, 128),
        10_000_000,
        out_specs=ANY,
        scratch_shapes=[pltpu.VMEM((KEYS, 128), BF), pltpu.SemaphoreType.DMA((YS,))],
    )(row)
    slots = lax.all_to_all(slots, "lon", 0, 0, axis_index_groups=along_y)
    inner = lax.ppermute(inner, "lon", inner_pairs)
    outer = lax.ppermute(outer, "lon", outer_pairs)
    merid, merid_edges = call(
        merid_own_kernel, (shape(LAT, MCELLS, MLANES), shape(2, MCELLS, MLANES)), 300_000_000
    )(field)
    merid, field_left, field_right = call(
        merid_edge_kernel,
        (shape(LAT, MCELLS, MLANES), shape(R * E, C), shape(R * E, C)),
        10_000_000,
        in_specs=[SMEM, ANY, VMEM, VMEM, VMEM],
        out_specs=[ANY, VMEM, VMEM],
        input_output_aliases={1: 0},
        scratch_shapes=[pltpu.VMEM((2, MCELLS, MLANES), BF), pltpu.SemaphoreType.DMA((2,))],
    )(side, merid, merid_edges, outer, inner)
    slots, merid = lax.optimization_barrier((slots, merid))
    merid = lax.all_to_all(merid, "lat", 0, 0)
    zonal = call(
        zonal_kernel, shape(ZS, WIDE, 256), 4_000_000_000, vmem=24, in_specs=[SMEM, VMEM, VMEM]
    )(y, row, slots)
    zonal = lax.all_to_all(zonal, "lon", 0, 0, axis_index_groups=along_z)
    merid = call(merid_kernel, shape(LAT, BROWS, 128), 1_000_000_000)(merid, w_qkv)
    merid = lax.all_to_all(merid, "lat", 0, 0)
    mixed, far, near = call(
        mix_kernel,
        (shape(R, WIDE, C), shape(3, WIDE, C), shape(3, WIDE, C)),
        800_000_000,
        in_specs=[SMEM] + [VMEM] * 6,
    )(odd, zonal, merid, field_left, field_right, field, w_out)
    near = lax.ppermute(near, "lat", near_pairs)
    far = lax.ppermute(far, "lat", far_pairs)
    conv_w = conv_w.reshape(49, C)
    own, w_in, w_back = call(
        own_conv_kernel,
        (jax.ShapeDtypeStruct((CELLS, C), F32), shape(*w_in.shape), shape(*w_back.shape)),
        1_000_000_000,
        in_specs=[VMEM, VMEM, ANY, ANY],
        scratch_shapes=[pltpu.SemaphoreType.DMA((2,))],
    )(mixed, conv_w, in_hbm(w_in), in_hbm(w_back))
    return call(
        block_kernel,
        shape(R, W, C),
        2_000_000_000,
        in_specs=[SMEM] + [VMEM] * 7,
        scratch_shapes=[pltpu.VMEM((CELLS, C), F32)],
    )(odd, mixed, own, far, near, conv_w, w_in, w_back)


def solution(mesh):
    return jax.shard_map(
        per_device,
        mesh=mesh,
        in_specs=(P("lat", "lon", None), P(), P(), P(), P(), P()),
        out_specs=P("lat", "lon", None),
        check_vma=False,
    )
```
